32 devices in a mesh: rep: 8 (over y, x, core), shard: 4 (over z).
Axes of the slice: x: 2, y: 2, z: 4, core: 2. Of those that a mesh axis runs over, the one named last changes fastest.
Arguments:
- tokens: bfloat16 [16384, 576], P(('rep', 'shard')), may hold values from -6 to 6
- lengths: int32 [32, 4], P(('rep', 'shard')), may hold values from 0 to 512, as said below
- gain_attn: bfloat16 [576], P('shard'), may hold values from 0.099609375 to 1.8984375
- w_query: bfloat16 [576, 576], P('shard'), may hold values from -0.25 to 0.25
- w_key: bfloat16 [576, 192], P('shard'), may hold values from -0.25 to 0.25
- w_value: bfloat16 [576, 192], P('shard'), may hold values from -0.25 to 0.25
- w_out: bfloat16 [576, 576], P('shard'), may hold values from -0.75 to 0.75
- gain_mlp: bfloat16 [576], P('shard'), may hold values from 0.099609375 to 1.8984375
- w_gate: bfloat16 [576, 1536], P('shard'), may hold values from -0.25 to 0.25
- w_up: bfloat16 [576, 1536], P('shard'), may hold values from -0.25 to 0.25
- w_down: bfloat16 [1536, 576], P('shard'), may hold values from -0.15625 to 0.15625
- cotangent: bfloat16 [16384, 576], P(('rep', 'shard')), may hold values from -6 to 6
Outputs:
- output: bfloat16 [16384, 576], P(('rep', 'shard'))
- grad_tokens: bfloat16 [16384, 576], P(('rep', 'shard'))
- grad_gain_attn: float32 [576], P('shard')
- grad_w_query: float32 [576, 576], P('shard')
- grad_w_key: float32 [576, 192], P('shard')
- grad_w_value: float32 [576, 192], P('shard')
- grad_w_out: float32 [576, 576], P('shard')
- grad_gain_mlp: float32 [576], P('shard')
- grad_w_gate: float32 [576, 1536], P('shard')
- grad_w_up: float32 [576, 1536], P('shard')
- grad_w_down: float32 [1536, 576], P('shard')
The draws below stay inside these ranges and needn't reach their ends.
Inputs may be any that keep to these rules, and one draw needn't show every extreme that they name: Each slab's lengths sum to between 128 and 512; lengths may be 0; in every draw some slab holds one sequence of 512 tokens and nothing else.
All inputs are finite; a program needn't handle non-finite values.
Results may differ from the reference program's by a relative error of at most 0.015.
Values may be sent and summed in bfloat16 or wider, within the bound.
No kernel may reach another device: no remote copies, remote signals or barrier semaphores. Data moves between devices by JAX's collectives and lax.ppermute only.
A program may use at most 128 MiB of HBM per device.

```python
import jax
import jax.numpy as jnp
from jax import lax

D = 576
HEADS = 9
KV = 3
HD = 64
FF = 1536
CAP = 512
NSEQ = 4
SLABS = 32
TOKENS = 16384


def draw_lengths(key, part):
    key = jax.random.fold_in(key, 11)
    key_total, key_cuts, key_full = jax.random.split(key, 3)
    totals = jax.random.randint(key_total, (SLABS,), CAP // 4, CAP + 1, dtype=jnp.int32)
    cut_points = jax.random.randint(key_cuts, (SLABS, NSEQ - 1), 0, CAP + 1, dtype=jnp.int32)
    cut_points = jnp.sort(cut_points, axis=1) * totals[:, None] // CAP
    bounds = jnp.concatenate([jnp.zeros((SLABS, 1), jnp.int32), cut_points, totals[:, None]], axis=1)
    pieces = bounds[:, 1:] - bounds[:, :-1]
    chosen = jax.random.randint(key_full, (), 0, SLABS, dtype=jnp.int32)
    single = jnp.zeros((NSEQ,), jnp.int32).at[0].set(CAP)
    row_ids = jnp.arange(SLABS, dtype=jnp.int32)
    return jnp.where((row_ids == chosen)[:, None], single[None, :], pieces)


def steps_of(own_key, extent, cuts, low, top_value):
    level = 1.0
    for dim, blocks in cuts:
        draws = jax.random.uniform(jax.random.fold_in(jax.random.fold_in(own_key, 6), dim), (blocks,), jnp.float32, low / len(cuts), top_value / len(cuts))
        level = level * jnp.repeat(jnp.exp(draws), extent[dim] // blocks).reshape((-1,) + (1,) * (len(extent) - 1 - dim))
    return level


def gaussian(key, shape, width, bound, shards=(), kind=jnp.bfloat16):
    drawn = jax.random.normal(key, shape, jnp.float32) * width
    if len(shards) > 0:
        drawn = steps_of(key, shape, shards, -0.22, 0.18) * drawn
    return jnp.clip(drawn, min=-bound, max=bound).astype(kind)


def setup_inputs(seed: int = 0) -> dict:
    splits = jax.random.split(jax.random.key(seed), 13)
    tokens = gaussian(splits[0], (TOKENS, D), 1.0, 6.0, ((0, 32),))
    lengths = draw_lengths(jax.random.fold_in(splits[12], 71), 0)
    gain_attn = jnp.clip(1.0 + 0.18 * jax.random.normal(splits[2], (D,), jnp.float32), 0.099609375, 1.8984375).astype(jnp.bfloat16)
    w_query = gaussian(splits[3], (D, D), D ** -0.5, 0.25, ((0, 4),))
    w_key = gaussian(splits[4], (D, KV * HD), D ** -0.5, 0.25, ((0, 4),))
    w_value = gaussian(splits[5], (D, KV * HD), D ** -0.5, 0.25, ((0, 4),))
    w_out = gaussian(splits[6], (D, D), (D // 8) ** -0.5, 0.75, ((0, 4),))
    gain_mlp = jnp.clip(1.0 + 0.18 * jax.random.normal(splits[7], (D,), jnp.float32), 0.099609375, 1.8984375).astype(jnp.bfloat16)
    w_gate = gaussian(splits[8], (D, FF), D ** -0.5, 0.25, ((0, 4),))
    w_up = gaussian(splits[9], (D, FF), D ** -0.5, 0.25, ((0, 4),))
    w_down = gaussian(splits[10], (FF, D), FF ** -0.5, 0.15625, ((0, 4),))
    cotangent = gaussian(splits[11], (TOKENS, D), 1.0, 6.0, ((0, 32),))
    return dict(tokens=tokens, lengths=lengths, gain_attn=gain_attn, w_query=w_query, w_key=w_key, w_value=w_value, w_out=w_out, gain_mlp=gain_mlp, w_gate=w_gate, w_up=w_up, w_down=w_down, cotangent=cotangent)


@jax.custom_vjp
def low(v):
    return lax.optimization_barrier(v.astype(jnp.bfloat16)).astype(jnp.float32)

@jax.custom_vjp
def low_back(v):
    return v

def low_keep(v):
    return (low(v), None)

def low_pass(kept, grad):
    return (grad,)

def back_keep(v):
    return (v, None)

def back_low(kept, grad):
    return (low(grad),)
low.defvjp(low_keep, low_pass)
low_back.defvjp(back_keep, back_low)
norm_eps = 1e-05
rope_base = 100000.0
neg_fill = -1e+30
group_slabs = 8

def token_layout(row_lengths):
    places = jnp.arange(CAP, dtype=jnp.int32)
    ends = jnp.cumsum(row_lengths, dtype=jnp.int32)
    passed = (places[:, None] >= ends[None, :]).astype(jnp.int32)
    segment = lax.optimization_barrier(jnp.sum(passed, axis=1)).astype(jnp.int32)
    offset = lax.optimization_barrier(jnp.sum(passed * row_lengths[None, :], axis=1)).astype(jnp.int32)
    return (segment, places - offset, places < ends[-1])

def rotate(values, cosine, sine):
    half = values.shape[-1] // 2
    first = values[..., :half]
    second = values[..., half:]
    return jnp.concatenate([first * cosine - second * sine, second * cosine + first * sine], axis=-1)

def rms_norm(values, gain):
    recip = lax.rsqrt(lax.optimization_barrier(jnp.mean(values * values, axis=-1, keepdims=True)) + norm_eps)
    return values * recip * gain

def project(values, weight):
    return jnp.einsum('gtd,de->gte', values, weight, precision=lax.Precision.HIGHEST)

def block_forward(inputs, segment, position, alive, params):
    gain_one, w_query, w_key, w_value, w_out, gain_two, w_gate, w_up, w_down = params
    groups = inputs.shape[0]
    ratio = HEADS // KV
    normed = low(rms_norm(inputs, gain_one))
    query = low_back(project(normed, w_query))
    keys = low_back(project(normed, w_key))
    values = low(low_back(project(normed, w_value)))
    half = HD // 2
    freq = rope_base ** (-(jnp.arange(half, dtype=jnp.float32) * 2.0 / HD))
    angle = position.astype(jnp.float32)[..., None] * freq
    cosine = jnp.cos(angle)[:, :, None, :]
    sine = jnp.sin(angle)[:, :, None, :]
    query_rot = low(rotate(query.reshape(groups, CAP, HEADS, HD), cosine, sine))
    key_rot = low(rotate(keys.reshape(groups, CAP, KV, HD), cosine, sine))
    query_rot = query_rot.reshape(groups, CAP, KV, ratio, HD)
    raw = jnp.einsum('gqkrd,gpkd->gkrqp', query_rot, key_rot, precision=lax.Precision.HIGHEST)
    scores = low_back(raw) * HD ** (-0.5)
    places = jnp.arange(CAP, dtype=jnp.int32)
    causal = places[:, None] >= places[None, :]
    same = segment[:, :, None] == segment[:, None, :]
    allowed = (same & causal[None])[:, None, None]
    logits = jnp.where(allowed, scores, neg_fill)
    weights = low(jax.nn.softmax(logits, axis=-1))
    mixed = jnp.einsum('gkrqp,gpkd->gqkrd', weights, values.reshape(groups, CAP, KV, HD), precision=lax.Precision.HIGHEST)
    mixed = low(low_back(mixed.reshape(groups, CAP, D)))
    attended = low_back(project(mixed, w_out))
    hidden_one = inputs + attended
    normed_two = low(rms_norm(hidden_one, gain_two))
    gate = low_back(project(normed_two, w_gate))
    upward = low_back(project(normed_two, w_up))
    hidden = low(jax.nn.silu(gate) * upward)
    down = low_back(project(hidden, w_down))
    return (hidden_one + down) * alive[..., None]

def layer_forward(segment, position, alive, inputs, *params):
    count = SLABS // group_slabs
    grouped = inputs.reshape(count, group_slabs, CAP, D)
    seg_groups = segment.reshape(count, group_slabs, CAP)
    pos_groups = position.reshape(count, group_slabs, CAP)
    live_groups = alive.reshape(count, group_slabs, CAP)

    def one_group(pieces):
        return block_forward(pieces[0], pieces[1], pieces[2], pieces[3], params)
    result = lax.map(jax.checkpoint(one_group), (grouped, seg_groups, pos_groups, live_groups))
    return result.reshape(TOKENS, D)

def reference(tokens, lengths, gain_attn, w_query, w_key, w_value, w_out, gain_mlp, w_gate, w_up, w_down, cotangent):
    segment, position, live = jax.vmap(token_layout)(lengths)
    alive = live.astype(jnp.float32)
    primals = [tokens, gain_attn, w_query, w_key, w_value, w_out, gain_mlp, w_gate, w_up, w_down]
    primals = [item.astype(jnp.float32) for item in primals]

    def forward(*items):
        return layer_forward(segment, position, alive, *items)
    result, pull = jax.vjp(forward, *primals)
    grads = pull(cotangent.astype(jnp.float32))
    return (result.astype(jnp.bfloat16), grads[0].astype(jnp.bfloat16), grads[1], grads[2], grads[3], grads[4], grads[5], grads[6], grads[7], grads[8], grads[9])
```

```python
import functools

import jax
import jax.numpy as jnp
from jax import lax
from jax.sharding import PartitionSpec as P

HEADS = 9
KV = 3
HD = 64


norm_eps = 1e-05
rope_base = 100000.0
neg_fill = -1e30


def token_layout(row_lengths, rows):
    places = jnp.arange(rows, dtype=jnp.int32)
    ends = jnp.cumsum(row_lengths, dtype=jnp.int32)
    passed = (places[:, None] >= ends[None, :]).astype(jnp.int32)
    segment = jnp.sum(passed, axis=1)
    offset = jnp.sum(passed * row_lengths[None, :], axis=1)
    return (places, segment, places - offset, places < ends[-1])


def rotation_tables(position, head_size):
    half = head_size // 2
    freq = rope_base ** (-(jnp.arange(half, dtype=jnp.float32) * 2.0 / head_size))
    angle = position.astype(jnp.float32)[:, None] * freq[None, :]
    return (jnp.cos(angle)[:, None, :], jnp.sin(angle)[:, None, :])


def rotate(values, cosine, sine):
    half = values.shape[-1] // 2
    first = values[..., :half]
    second = values[..., half:]
    return jnp.concatenate(
        [first * cosine - second * sine, second * cosine + first * sine], axis=-1
    )


def unrotate(grads, cosine, sine):
    half = grads.shape[-1] // 2
    first = grads[..., :half]
    second = grads[..., half:]
    return jnp.concatenate(
        [first * cosine + second * sine, second * cosine - first * sine], axis=-1
    )


def rms_norm(values, gain):
    recip = lax.rsqrt(jnp.mean(values * values, axis=-1, keepdims=True) + norm_eps)
    return (values * recip * gain, recip)


def norm_back(values, recip, gain, grad_normed):
    scaled = grad_normed * gain
    grad_values = recip * scaled - values * recip * recip * recip * jnp.mean(
        scaled * values, axis=-1, keepdims=True
    )
    grad_gain = jnp.sum(grad_normed * values * recip, axis=0)
    return (grad_values, grad_gain)


def matmul(left, right):
    return jnp.dot(left, right, preferred_element_type=jnp.float32)


def matmul_left_t(left, right):
    return lax.dot_general(
        left, right, (((0,), (0,)), ((), ())), preferred_element_type=jnp.float32
    )


def matmul_right_t(left, right):
    return lax.dot_general(
        left, right, (((1,), (1,)), ((), ())), preferred_element_type=jnp.float32
    )


def flip(value, bit, replicas):
    return lax.ppermute(value, "rep", [(i, i ^ (1 << bit)) for i in range(replicas)])


def shift(value, step, shards):
    return lax.ppermute(value, "shard", [((s + step) % shards, s) for s in range(shards)])


def pair_up(value, bit, rep_index, replicas, axis):
    other = flip(value, bit, replicas)
    low = (rep_index >> bit) & 1 == 0
    return jnp.stack([jnp.where(low, value, other), jnp.where(low, other, value)], axis=axis)


def pick(value, index, axis):
    return lax.dynamic_index_in_dim(value, index, axis, keepdims=False)


def gather(pieces, bits, order, shards, replicas):
    rep_index = lax.axis_index("rep")
    shard_index = lax.axis_index("shard")
    mine = pieces
    for bit in bits:
        mine = pick(mine, (rep_index >> bit) & 1, 0)
    got = jnp.stack([shift(mine, step, shards) for step in range(1, shards)])
    done = []
    for bit in order:
        at = sorted(done + [bits.index(bit)]).index(bits.index(bit))
        done.append(bits.index(bit))
        got = pair_up(got, bit, rep_index, replicas, 1 + at)
    whole = jnp.zeros((shards,) + pieces.shape, pieces.dtype)
    whole = lax.dynamic_update_index_in_dim(whole, pieces, shard_index, 0)
    for step in range(1, shards):
        at = (shard_index + step) % shards
        whole = lax.dynamic_update_index_in_dim(whole, got[step - 1], at, 0)
    return whole


def reduce_owned(grads, bits, order, shards, replicas):
    rep_index = lax.axis_index("rep")
    shard_index = lax.axis_index("shard")
    left = list(bits)
    value = grads
    for bit in order:
        axis = 1 + left.index(bit)
        left.remove(bit)
        side = (rep_index >> bit) & 1
        kept = pick(value, side, axis).astype(jnp.float32)
        other = flip(pick(value, 1 - side, axis), bit, replicas).astype(jnp.float32)
        value = (kept + other).astype(jnp.bfloat16)
    total = pick(value, shard_index, 0).astype(jnp.float32)
    for step in range(1, shards):
        sent = pick(value, (shard_index + shards - step) % shards, 0)
        total = total + shift(sent, step, shards).astype(jnp.float32)
    total = total.astype(jnp.bfloat16)
    bit = 3
    while (1 << bit) < replicas:
        total = (
            total.astype(jnp.float32) + flip(total, bit, replicas).astype(jnp.float32)
        ).astype(jnp.bfloat16)
        bit += 1
    done = []
    for bit in reversed(order):
        done.append(bits.index(bit))
        at = sorted(done).index(bits.index(bit))
        total = pair_up(total, bit, rep_index, replicas, at)
    return total.astype(jnp.float32)


ATTN_BITS = (2, 0, 1)
PAIR_BITS = (2, 0, 1)
DOWN_BITS = (0, 1, 2)


def attn_split(value):
    lead = value.shape[:-2]
    n = len(lead)
    value = value.reshape(lead + (2, value.shape[-2] // 2, 2, 2, value.shape[-1] // 4))
    return jnp.moveaxis(value, n + 1, n + 3)


def attn_join(value):
    n = value.ndim - 5
    value = jnp.moveaxis(value, n + 3, n + 1)
    lead = value.shape[:n]
    return value.reshape(lead + (2 * value.shape[n + 1], 4 * value.shape[n + 4]))


def cols_split(value):
    lead = value.shape[:-1]
    n = len(lead)
    value = value.reshape(lead + (2, 2, value.shape[-1] // 4))
    return jnp.moveaxis(value, n - 1, n + 1)


def cols_join(value):
    n = value.ndim - 4
    value = jnp.moveaxis(value, n + 2, n)
    return value.reshape(value.shape[: n + 1] + (4 * value.shape[-1],))


def rows_split(value):
    return value.reshape(value.shape[:-2] + (2, 2, 2, value.shape[-2] // 8, value.shape[-1]))


def rows_join(value):
    n = value.ndim - 5
    return value.reshape(value.shape[:n] + (8 * value.shape[-2], value.shape[-1]))


def pack_attn(query, key, value, out, gain_one, gain_two):
    lead = query.shape[:-2]
    width = query.shape[-1] + key.shape[-1] + value.shape[-1] + out.shape[-1]
    weights = jnp.concatenate([query, key, value, out], axis=-1)
    gains = jnp.concatenate([gain_one, gain_two], axis=-1)[..., None, :]
    pad = [(0, 0)] * len(lead) + [(0, 15), (0, width - gains.shape[-1])]
    return jnp.concatenate([weights, jnp.pad(gains, pad)], axis=-2)


def unpack_attn(packed, rows, widths):
    parts = []
    at = 0
    for width in widths:
        parts.append(packed[..., :rows, at : at + width])
        at += width
    gains = packed[..., rows, :]
    return parts + [gains[..., :rows], gains[..., rows : 2 * rows]]


def local(
    replicas,
    shards,
    tokens,
    lengths,
    gain_attn,
    w_query,
    w_key,
    w_value,
    w_out,
    gain_mlp,
    w_gate,
    w_up,
    w_down,
    cotangent,
):
    rows = tokens.shape[0]
    ratio = HEADS // KV
    scale = HD ** (-0.5)
    part = w_query.shape[0]
    widths = (w_query.shape[1], w_key.shape[1], w_value.shape[1], w_out.shape[1])
    attn = pack_attn(w_query, w_key, w_value, w_out, gain_attn, gain_mlp)
    attn = attn_join(gather(attn_split(attn), ATTN_BITS, (1, 2, 0), shards, replicas))
    query_full, key_full, value_full, out_full, gain_one, gain_two = unpack_attn(attn, part, widths)
    query_full, key_full, value_full, out_full = (
        item.reshape(shards * part, -1) for item in (query_full, key_full, value_full, out_full)
    )
    gain_one = gain_one.reshape(-1)
    gain_two = gain_two.reshape(-1)
    pair = cols_split(jnp.stack([w_gate, w_up]))
    pair = cols_join(gather(pair, PAIR_BITS, (2, 1, 0), shards, replicas))
    gate_full = pair[:, 0].reshape(shards * part, -1)
    up_full = pair[:, 1].reshape(shards * part, -1)
    down_full = rows_join(gather(rows_split(w_down), DOWN_BITS, (1, 2, 0), shards, replicas))
    down_full = down_full.reshape(-1, w_down.shape[1])
    places, segment, position, live = token_layout(lengths[0], rows)
    cosine, sine = rotation_tables(position, HD)
    alive = live.astype(jnp.float32)[:, None]
    allowed = ((segment[:, None] == segment[None, :]) & (places[:, None] >= places[None, :]))[
        None, None
    ]
    hidden_in = tokens.astype(jnp.float32)
    normed_f, recip_one = rms_norm(hidden_in, gain_one.astype(jnp.float32))
    normed = normed_f.astype(jnp.bfloat16)
    query = matmul(normed, query_full)
    keys = matmul(normed, key_full)
    values = matmul(normed, value_full).astype(jnp.bfloat16).reshape(rows, KV, HD)
    query_rot = (
        rotate(query.reshape(rows, HEADS, HD), cosine, sine)
        .astype(jnp.bfloat16)
        .reshape(rows, KV, ratio, HD)
    )
    key_rot = rotate(keys.reshape(rows, KV, HD), cosine, sine).astype(jnp.bfloat16)
    raw = jnp.einsum("qkrd,pkd->krqp", query_rot, key_rot, preferred_element_type=jnp.float32)
    logits = jnp.where(allowed, raw * scale, neg_fill)
    top = jnp.max(logits, axis=-1, keepdims=True)
    expo = jnp.exp(logits - top)
    total = jnp.sum(expo, axis=-1, keepdims=True)
    probs_low = (expo / total).astype(jnp.bfloat16)
    log_total = top + jnp.log(total)
    mixed = jnp.einsum("krqp,pkd->qkrd", probs_low, values, preferred_element_type=jnp.float32)
    mixed = mixed.reshape(rows, HEADS * HD).astype(jnp.bfloat16)
    hidden_one = hidden_in + matmul(mixed, out_full)
    normed_two_f, recip_two = rms_norm(hidden_one, gain_two.astype(jnp.float32))
    normed_two = normed_two_f.astype(jnp.bfloat16)
    gate = matmul(normed_two, gate_full)
    upward = matmul(normed_two, up_full)
    sigma = jax.nn.sigmoid(gate)
    active = gate * sigma
    hidden = (active * upward).astype(jnp.bfloat16)
    result = ((hidden_one + matmul(hidden, down_full)) * alive).astype(jnp.bfloat16)
    grad_out = cotangent.astype(jnp.float32) * alive
    grad_down_in = grad_out.astype(jnp.bfloat16)
    grad_w_down = matmul_left_t(hidden, grad_down_in)
    grad_hidden = matmul_right_t(grad_down_in, down_full)
    grad_gate = (grad_hidden * upward * sigma * (1.0 + gate * (1.0 - sigma))).astype(jnp.bfloat16)
    grad_upward = (grad_hidden * active).astype(jnp.bfloat16)
    grad_w_gate = matmul_left_t(normed_two, grad_gate)
    grad_w_up = matmul_left_t(normed_two, grad_upward)
    grad_normed_two = matmul_right_t(grad_gate, gate_full) + matmul_right_t(grad_upward, up_full)
    grad_from_two, grad_gain_mlp = norm_back(
        hidden_one, recip_two, gain_two.astype(jnp.float32), grad_normed_two
    )
    grad_hidden_one = grad_out + grad_from_two
    grad_attended = grad_hidden_one.astype(jnp.bfloat16)
    grad_w_out = matmul_left_t(mixed, grad_attended)
    grad_mixed = (
        matmul_right_t(grad_attended, out_full).astype(jnp.bfloat16).reshape(rows, KV, ratio, HD)
    )
    probs = jnp.exp(logits - log_total)
    probs_again = probs.astype(jnp.bfloat16)
    grad_values = jnp.einsum(
        "krqp,qkrd->pkd", probs_again, grad_mixed, preferred_element_type=jnp.float32
    )
    grad_values = grad_values.reshape(rows, KV * HD).astype(jnp.bfloat16)
    grad_probs = jnp.einsum(
        "qkrd,pkd->krqp", grad_mixed, values, preferred_element_type=jnp.float32
    )
    delta = jnp.sum(grad_probs * probs, axis=-1, keepdims=True)
    grad_raw = (scale * probs * (grad_probs - delta)).astype(jnp.bfloat16)
    grad_query_rot = jnp.einsum(
        "krqp,pkd->qkrd", grad_raw, key_rot, preferred_element_type=jnp.float32
    )
    grad_key_rot = jnp.einsum(
        "krqp,qkrd->pkd", grad_raw, query_rot, preferred_element_type=jnp.float32
    )
    grad_query = (
        unrotate(grad_query_rot.reshape(rows, HEADS, HD), cosine, sine)
        .reshape(rows, HEADS * HD)
        .astype(jnp.bfloat16)
    )
    grad_keys = unrotate(grad_key_rot, cosine, sine).reshape(rows, KV * HD).astype(jnp.bfloat16)
    grad_w_query = matmul_left_t(normed, grad_query)
    grad_w_key = matmul_left_t(normed, grad_keys)
    grad_w_value = matmul_left_t(normed, grad_values)
    grad_normed = (
        matmul_right_t(grad_query, query_full)
        + matmul_right_t(grad_keys, key_full)
        + matmul_right_t(grad_values, value_full)
    )
    grad_from_one, grad_gain_attn = norm_back(
        hidden_in, recip_one, gain_one.astype(jnp.float32), grad_normed
    )
    grad_tokens = (grad_hidden_one + grad_from_one).astype(jnp.bfloat16)
    low = jnp.bfloat16
    g_pair = jnp.stack(
        [item.astype(low).reshape(shards, part, -1) for item in (grad_w_gate, grad_w_up)], axis=1
    )
    g_pair = cols_join(reduce_owned(cols_split(g_pair), PAIR_BITS, (0, 1, 2), shards, replicas))
    g_down = rows_split(grad_w_down.astype(low).reshape((shards,) + w_down.shape))
    g_down = rows_join(reduce_owned(g_down, DOWN_BITS, (0, 2, 1), shards, replicas))
    g_attn = pack_attn(
        *(
            item.astype(low).reshape(shards, part, -1)
            for item in (grad_w_query, grad_w_key, grad_w_value, grad_w_out)
        ),
        grad_gain_attn.astype(low).reshape(shards, part),
        grad_gain_mlp.astype(low).reshape(shards, part),
    )
    g_attn = attn_join(reduce_owned(attn_split(g_attn), ATTN_BITS, (0, 2, 1), shards, replicas))
    g_query, g_key, g_value, g_out, g_gain_one, g_gain_two = unpack_attn(g_attn, part, widths)
    return (
        result,
        grad_tokens,
        g_gain_one,
        g_query,
        g_key,
        g_value,
        g_out,
        g_gain_two,
        g_pair[0],
        g_pair[1],
        g_down,
    )


def solution(mesh):
    in_specs = (
        P(("rep", "shard"), None),
        P(("rep", "shard"), None),
        P("shard"),
        P("shard", None),
        P("shard", None),
        P("shard", None),
        P("shard", None),
        P("shard"),
        P("shard", None),
        P("shard", None),
        P("shard", None),
        P(("rep", "shard"), None),
    )
    out_specs = (
        P(("rep", "shard"), None),
        P(("rep", "shard"), None),
        P("shard"),
        P("shard", None),
        P("shard", None),
        P("shard", None),
        P("shard", None),
        P("shard"),
        P("shard", None),
        P("shard", None),
        P("shard", None),
    )
    part = functools.partial(local, mesh.shape["rep"], mesh.shape["shard"])
    return jax.shard_map(part, mesh=mesh, in_specs=in_specs, out_specs=out_specs, check_vma=False)
```

```python
import functools

import jax
import jax.numpy as jnp
from jax import lax
from jax.experimental import pallas as pl
from jax.experimental.pallas import tpu as pltpu
from jax.sharding import PartitionSpec as P

HEADS = 9
KV = 3
HD = 64
RATIO = HEADS // KV


norm_eps = 1e-05
rope_base = 100000.0
neg_fill = -1e30

low = jnp.bfloat16
f32 = jnp.float32
VMEM_LIMIT = 60 * 1024 * 1024
QUERY_ROWS = 128


def token_layout(row_lengths, rows):
    places = jnp.arange(rows, dtype=jnp.int32)
    ends = jnp.cumsum(row_lengths, dtype=jnp.int32)
    passed = (places[:, None] >= ends[None, :]).astype(jnp.int32)
    segment = jnp.sum(passed, axis=1)
    offset = jnp.sum(passed * row_lengths[None, :], axis=1)
    return (segment, places - offset, places < ends[-1])


def rotation_tables(position, head_size):
    half = head_size // 2
    freq = rope_base ** (-(jnp.arange(half, dtype=f32) * 2.0 / head_size))
    angle = position.astype(f32)[:, None] * freq[None, :]
    cosine = jnp.cos(angle)
    sine = jnp.sin(angle)
    return (
        jnp.concatenate([cosine] * 4, axis=1),
        jnp.concatenate([-sine, sine, -sine, sine], axis=1),
    )


def matmul(left, right):
    return jnp.dot(left, right, preferred_element_type=f32)


def matmul_left_t(left, right):
    return lax.dot_general(left, right, (((0,), (0,)), ((), ())), preferred_element_type=f32)


def matmul_right_t(left, right):
    return lax.dot_general(left, right, (((1,), (1,)), ((), ())), preferred_element_type=f32)


def flip(value, bit, replicas):
    return lax.ppermute(value, "rep", [(i, i ^ (1 << bit)) for i in range(replicas)])


def shift_from(value, step, shards):
    return lax.ppermute(value, "shard", [((s + step) % shards, s) for s in range(shards)])


def shift_to(value, step, shards):
    return lax.ppermute(value, "shard", [(s, (s + step) % shards) for s in range(shards)])


def add_low(left, right):
    return (left.astype(f32) + right.astype(f32)).astype(low)


def gather(mine, order, shards, replicas):
    got = jnp.stack([shift_from(mine, step, shards) for step in range(1, shards)])
    for bit in order[:-1]:
        got = jnp.stack([got, flip(got, bit, replicas)])
    return got, flip(got, order[-1], replicas)


def scatter_in_plane(keep, send, order, replicas):
    other = flip(send, order[0], replicas)
    for bit in order[1:]:
        send = add_low(keep[1], other[1])
        moved = flip(send, bit, replicas)
        keep = add_low(keep[0], other[0])
        other = moved
    return keep, other


def scatter_over_shards(keep, other, shards, replicas):
    parts = [add_low(keep[step], other[step]) for step in range(1, shards)]
    moved = [shift_to(part, step + 1, shards) for step, part in enumerate(parts)]
    total = keep[0].astype(f32) + other[0].astype(f32)
    for part in moved:
        total = total + part.astype(f32)
    total = total.astype(low)
    bit = 3
    while (1 << bit) < replicas:
        total = add_low(total, flip(total, bit, replicas))
        bit += 1
    return total


def spread(total, order, replicas):
    for bit in order[:-1]:
        total = jnp.stack([total, flip(total, bit, replicas)])
    return total, flip(total, order[-1], replicas)


def start_all(copies):
    for copy in copies:
        copy.start()
    return copies


def wait_all(copies):
    for copy in copies:
        copy.wait()


class Copies:
    def __init__(self, sems):
        self.sems = sems
        self.made = []

    def start(self, source, target):
        copy = pltpu.make_async_copy(source, target, self.sems.at[len(self.made)])
        copy.start()
        self.made.append(copy)

    def wait(self):
        for copy in self.made:
            copy.wait()


def rows_at(start, count, unit=16):
    return pl.ds(pl.multiple_of(start, unit), count)


def relative(bit, rel):
    return 1 - bit if rel else bit


def shard_at(shard, step, shards):
    at = shard + step
    return jnp.where(at >= shards, at - shards, at)


def swap_halves(values):
    lane = lax.broadcasted_iota(jnp.int32, values.shape, 1)
    return jnp.where(
        lane % HD < HD // 2,
        pltpu.roll(values, 2 * HD - HD // 2, 1),
        pltpu.roll(values, HD // 2, 1),
    )


def norm_recip(values):
    return lax.rsqrt(jnp.mean(values * values, axis=-1, keepdims=True) + norm_eps)


def norm_back(values, recip, gain, grad_normed):
    scaled = grad_normed * gain
    inner = jnp.mean(scaled * values, axis=-1, keepdims=True)
    grad_values = recip * scaled - values * (recip * recip * recip * inner)
    grad_gain = jnp.sum(grad_normed * values * recip, axis=0, keepdims=True)
    return (grad_values, grad_gain)


def allowed_bias(seg_col, seg_row, bias):
    rows = bias.shape[0]
    query = lax.broadcasted_iota(jnp.int32, bias.shape, 0)
    key = lax.broadcasted_iota(jnp.int32, bias.shape, 1)
    same = seg_col[...] == seg_row[...]
    bias[...] = jnp.where(same & (query >= key), 0.0, neg_fill)


def project_kernel(
    shards,
    part,
    where_ref,
    tokens,
    cosine,
    sine,
    own,
    pieces,
    other,
    weights,
    gains,
    normed,
    query,
    keys,
    values,
    sems,
):
    core, x, y, shard = (where_ref[i] for i in range(4))
    width = tokens.shape[1]
    copies = Copies(sems)
    copies.start(own.at[pl.ds(0, part)], weights.at[rows_at(part * shard, part)])
    copies.start(own.at[pl.ds(part, 16)], weights.at[rows_at(width + 16 * shard, 16)])
    for rel_core, source in enumerate((pieces, other)):
        for rel_x in range(2):
            for rel_y in range(2):
                at_y = relative(y, rel_y)
                block = 2 * relative(core, rel_core) + relative(x, rel_x)
                columns = rows_at(384 * block, 384, 128)
                for step in range(1, shards):
                    at = shard_at(shard, step, shards)
                    piece = source.at[rel_x, rel_y, step - 1]
                    copies.start(
                        piece.at[pl.ds(0, 64)], weights.at[rows_at(part * at + 80 * at_y, 64), columns]
                    )
                    last = jnp.where(at_y == 0, part * at + 64, width + 16 * at)
                    copies.start(piece.at[pl.ds(64, 16)], weights.at[rows_at(last, 16), columns])
    hidden = tokens[...].astype(f32)
    scaled = hidden * norm_recip(hidden)
    copies.wait()
    total = sum(
        weights[width + 16 * s : width + 16 * s + 16, :width].astype(f32) for s in range(shards)
    )
    gains[...] = total[:8]
    n1 = (scaled * total[0:1]).astype(low)
    normed[...] = n1
    for block in range(8):
        start = 512 + 128 * block
        result = matmul(n1, weights[0:width, start : start + 128])
        heads = [2 * block - 1, 2 * block]
        if heads[0] < HEADS + KV:
            turned = result * cosine[...] + swap_halves(result) * sine[...]
        for side, head in enumerate(heads):
            lanes = slice(HD * side, HD * side + HD)
            if head < 0:
                continue
            if head < HEADS:
                query[head] = (turned[:, lanes] * HD**-0.5).astype(low)
            elif head < HEADS + KV:
                keys[head - HEADS] = turned[:, lanes].astype(low)
            else:
                values[head - HEADS - KV] = result[:, lanes].astype(low)


def attend_kernel(
    tokens, seg_col, seg_row, gains, weights, query, keys, values, mixed, log_total, hidden_one, normed_two, bias
):
    rows, width = tokens.shape
    allowed_bias(seg_col, seg_row, bias)
    for kv in range(KV):
        for block in range(rows // QUERY_ROWS):
            at = slice(QUERY_ROWS * block, QUERY_ROWS * (block + 1))
            reach = QUERY_ROWS * (block + 1)
            stacked = jnp.concatenate([query[RATIO * kv + i, at] for i in range(RATIO)], axis=0)
            scores = matmul_right_t(stacked, keys[kv, :reach])
            logits = scores.reshape(RATIO, QUERY_ROWS, reach) + bias[at, :reach][None]
            top = jnp.max(logits, axis=-1, keepdims=True)
            expo = jnp.exp(logits - top)
            total = jnp.sum(expo, axis=-1, keepdims=True)
            probs = (expo * (1.0 / total)).astype(low).reshape(RATIO * QUERY_ROWS, reach)
            log_total[RATIO * kv : RATIO * kv + RATIO, at] = top + jnp.log(total)
            result = matmul(probs, values[kv, :reach]).astype(low)
            for i in range(RATIO):
                head = RATIO * kv + i
                mixed[at, HD * head : HD * head + HD] = result[QUERY_ROWS * i : QUERY_ROWS * (i + 1)]
    hidden = tokens[...].astype(f32) + matmul(mixed[...], weights[0:width, 0:width])
    hidden_one[...] = hidden
    normed_two[...] = (hidden * norm_recip(hidden) * gains[1:2]).astype(low)


def feed_kernel(
    shards,
    part,
    where_ref,
    hidden_one,
    normed_two,
    gains,
    live,
    cotangent,
    own_gate,
    own_up,
    own_down,
    pair_pieces,
    pair_other,
    down_pieces,
    down_other,
    result,
    grad_one,
    grad_gain,
    pair_keep,
    pair_send,
    down_keep,
    down_send,
    pair,
    down,
    hidden,
    grad_gate,
    grad_up,
    grad_pair,
    grad_down,
    sems,
):
    core, x, y, shard = (where_ref[i] for i in range(4))
    width = hidden_one.shape[1]
    down_part = own_down.shape[0]
    eighth = down_part // 8
    copies = Copies(sems)
    copies.start(own_gate, pair.at[0, rows_at(part * shard, part)])
    copies.start(own_up, pair.at[1, rows_at(part * shard, part)])
    copies.start(own_down, down.at[rows_at(down_part * shard, down_part)])
    for rel_core, (source, down_source) in enumerate(
        ((pair_pieces, down_pieces), (pair_other, down_other))
    ):
        at_core = relative(core, rel_core)
        for rel_x in range(2):
            at_x = relative(x, rel_x)
            block = 2 * at_core + at_x
            columns = rows_at(384 * block, 384, 128)
            for rel_y in range(2):
                at_y = relative(y, rel_y)
                for step in range(1, shards):
                    at = shard_at(shard, step, shards)
                    copies.start(
                        source.at[rel_x, rel_y, step - 1],
                        pair.at[at_y, rows_at(part * at, part), columns],
                    )
                    copies.start(
                        down_source.at[rel_y, rel_x, step - 1],
                        down.at[rows_at(down_part * at + eighth * (2 * block + at_y), eighth)],
                    )
    alive = live[...]
    grad_out = cotangent[...].astype(f32) * alive
    grad_low = grad_out.astype(low)
    n2 = normed_two[...]
    copies.wait()
    hidden_width = pair.shape[2]
    for start in range(0, hidden_width, 384):
        at = slice(start, start + 384)
        gate = matmul(n2, pair[0, :, at])
        upward = matmul(n2, pair[1, :, at])
        grad_hidden = matmul_right_t(grad_low, down[at, :])
        sigma = jax.nn.sigmoid(gate)
        active = gate * sigma
        hidden[:, at] = (active * upward).astype(low)
        grad_up[:, at] = (grad_hidden * active).astype(low)
        grad_gate[:, at] = (grad_hidden * upward * (sigma + active * (1.0 - sigma))).astype(low)
    turned = n2.T
    sent = Copies(sems)
    for unit, grads in enumerate((grad_gate, grad_up)):
        for block in range(4):
            at = slice(384 * block, 384 * block + 384)
            grad_pair[unit, :, at] = matmul(turned, grads[:, at]).astype(low)
    for start in range(0, hidden_width, 384):
        at = slice(start, start + 384)
        grad_down[at, :] = matmul_left_t(hidden[:, at], grad_low).astype(low)
    for rel_core, (target, down_target) in enumerate(((pair_keep, down_keep), (pair_send, down_send))):
        at_core = relative(core, rel_core)
        for rel_x in range(2):
            at_x = relative(x, rel_x)
            block = 2 * at_core + at_x
            columns = rows_at(384 * block, 384, 128)
            for rel_y in range(2):
                at_y = relative(y, rel_y)
                for step in range(shards):
                    at = shard_at(shard, step, shards)
                    sent.start(
                        grad_pair.at[at_y, rows_at(part * at, part), columns],
                        target.at[rel_x, rel_y, step],
                    )
                    sent.start(
                        grad_down.at[rows_at(down_part * at + eighth * (2 * block + at_y), eighth)],
                        down_target.at[rel_y, rel_x, step],
                    )
    h1 = hidden_one[...]
    result[...] = ((h1 + matmul(hidden[...], down[...])) * alive).astype(low)
    grad_normed = matmul_right_t(grad_gate[...], pair[0]) + matmul_right_t(grad_up[...], pair[1])
    grad_from, gain_row = norm_back(h1, norm_recip(h1), gains[1:2], grad_normed)
    grad_one[...] = grad_out + grad_from
    grad_gain[...] = jnp.broadcast_to(gain_row, grad_gain.shape)
    sent.wait()


def back_kernel(
    shards,
    part,
    where_ref,
    tokens,
    seg_col,
    seg_row,
    cosine,
    sine,
    gains,
    weights,
    normed,
    query,
    keys,
    values,
    mixed,
    log_total,
    grad_one,
    grad_gain_two,
    grad_tokens,
    keep,
    send,
    bias,
    grad_mixed,
    grad_heads,
    grad_low,
    grad_weights,
    sems,
):
    core, x, y, shard = (where_ref[i] for i in range(4))
    rows, width = tokens.shape
    allowed_bias(seg_col, seg_row, bias)
    dh1 = grad_one[...]
    da = dh1.astype(low)
    grad_mixed[...] = matmul_right_t(da, weights[0:width, 0:width]).astype(low)
    for kv in range(KV):
        grad_keys = [None] * (rows // QUERY_ROWS)
        grad_values = [None] * (rows // QUERY_ROWS)
        for block in range(rows // QUERY_ROWS):
            at = slice(QUERY_ROWS * block, QUERY_ROWS * (block + 1))
            reach = QUERY_ROWS * (block + 1)
            heads = [RATIO * kv + i for i in range(RATIO)]
            stacked = jnp.concatenate([query[head, at] for head in heads], axis=0)
            grads = [grad_mixed[at, HD * head : HD * head + HD] for head in heads]
            out = [mixed[at, HD * head : HD * head + HD] for head in heads]
            grads = jnp.concatenate(grads, axis=0)
            out = jnp.concatenate(out, axis=0)
            delta = jnp.sum(grads.astype(f32) * out.astype(f32), axis=-1, keepdims=True)
            scores = matmul_right_t(stacked, keys[kv, :reach]).reshape(RATIO, QUERY_ROWS, reach)
            lse = log_total[heads[0] : heads[0] + RATIO, at]
            probs = jnp.exp(scores + bias[at, :reach][None] - lse).reshape(-1, reach)
            grad_probs = matmul_right_t(grads, values[kv, :reach])
            grad_scores = (probs * (grad_probs - delta)).astype(low)
            grad_query = matmul(grad_scores, keys[kv, :reach])
            for i, head in enumerate(heads):
                grad_heads[at, HD + HD * head : 2 * HD + HD * head] = (
                    grad_query[QUERY_ROWS * i : QUERY_ROWS * (i + 1)] * HD**-0.5
                )
            key_part = matmul_left_t(grad_scores, stacked)
            value_part = matmul_left_t(probs.astype(low), grads)
            for j in range(block + 1):
                at_j = slice(QUERY_ROWS * j, QUERY_ROWS * (j + 1))
                if grad_keys[j] is None:
                    grad_keys[j], grad_values[j] = key_part[at_j], value_part[at_j]
                else:
                    grad_keys[j] = grad_keys[j] + key_part[at_j]
                    grad_values[j] = grad_values[j] + value_part[at_j]
        at_key = HD * (1 + HEADS + kv)
        at_value = HD * (1 + HEADS + KV + kv)
        grad_heads[:, at_key : at_key + HD] = jnp.concatenate(grad_keys, axis=0)
        grad_heads[:, at_value : at_value + HD] = jnp.concatenate(grad_values, axis=0)
    grad_heads[:, 0:HD] = jnp.zeros((rows, HD), f32)
    for block in range(8):
        at = slice(128 * block, 128 * block + 128)
        value = grad_heads[:, at]
        first, second = 2 * block - 1, 2 * block
        if first < HEADS + KV:
            turned = value * cosine[...] - swap_halves(value) * sine[...]
            if second < HEADS + KV:
                value = turned
            else:
                lane = lax.broadcasted_iota(jnp.int32, value.shape, 1)
                value = jnp.where(lane < HD, turned, value)
        grad_low[:, at] = value.astype(low)
    turned = normed[...].T
    for start in range(0, 1024, 512):
        at = slice(start, start + 512)
        grad_weights[0:width, 512 + start : 1024 + start] = matmul(turned, grad_low[:, at]).astype(low)
    grad_weights[0:width, 0:width] = matmul_left_t(mixed[...], da).astype(low)
    grad_normed = matmul_right_t(grad_low[...], weights[0:width, 512:1536])
    hidden = tokens[...].astype(f32)
    grad_from, gain_row = norm_back(hidden, norm_recip(hidden), gains[0:1], grad_normed)
    grad_tokens[...] = (dh1 + grad_from).astype(low)
    row = lax.broadcasted_iota(jnp.int32, (16, width), 0)
    both = jnp.where(
        row == 0,
        jnp.broadcast_to(gain_row, (16, width)),
        jnp.where(row == 1, jnp.broadcast_to(grad_gain_two[0:1], (16, width)), 0.0),
    )
    grad_weights[width : width + 16, :] = jnp.zeros((16, grad_weights.shape[1]), low)
    grad_weights[width : width + 16, 0:width] = both.astype(low)
    copies = Copies(sems)
    for rel_core, target in enumerate((keep, send)):
        for rel_x in range(2):
            for rel_y in range(2):
                at_y = relative(y, rel_y)
                block = 2 * relative(core, rel_core) + relative(x, rel_x)
                columns = rows_at(384 * block, 384, 128)
                for step in range(shards):
                    at = shard_at(shard, step, shards)
                    piece = target.at[rel_x, rel_y, step]
                    copies.start(
                        grad_weights.at[rows_at(part * at + 80 * at_y, 64), columns],
                        piece.at[pl.ds(0, 64)],
                    )
                    last = jnp.where(at_y == 0, part * at + 64, width)
                    copies.start(grad_weights.at[rows_at(last, 16), columns], piece.at[pl.ds(64, 16)])
    copies.wait()


def finish_kernel(
    where_ref,
    attn_pieces,
    attn_other,
    pair_pieces,
    pair_other,
    down_pieces,
    down_other,
    out_query,
    out_key,
    out_value,
    out_out,
    out_gains,
    out_gate,
    out_up,
    out_down,
    attn,
    pair,
    down,
    sems,
):
    core, x, y = (where_ref[i] for i in range(3))
    part = out_gate.shape[0]
    eighth = down.shape[0] // 8
    copies = Copies(sems)
    for rel_core, (a_from, p_from, d_from) in enumerate(
        ((attn_pieces, pair_pieces, down_pieces), (attn_other, pair_other, down_other))
    ):
        for rel_x in range(2):
            for rel_y in range(2):
                at_y = relative(y, rel_y)
                block = 2 * relative(core, rel_core) + relative(x, rel_x)
                columns = rows_at(384 * block, 384, 128)
                copies.start(a_from.at[rel_x, rel_y], attn.at[rows_at(80 * at_y, 80), columns])
                copies.start(p_from.at[rel_x, rel_y], pair.at[at_y, :, columns])
                copies.start(
                    d_from.at[rel_y, rel_x], down.at[rows_at(eighth * (2 * block + at_y), eighth)]
                )
    copies.wait()
    width = out_out.shape[1]
    kv_width = out_key.shape[1]
    out_out[...] = attn[0:part, 0:width].astype(f32)
    rest = attn[0:part, 512:].astype(f32)
    at = width - 512
    out_query[...] = rest[:, at : at + width]
    out_key[...] = rest[:, at + width : at + width + kv_width]
    out_value[...] = rest[:, at + width + kv_width :]
    out_gains[...] = attn[part : part + 16, 0:width].astype(f32)[:8]
    out_gate[...] = pair[0].astype(f32)
    out_up[...] = pair[1].astype(f32)
    out_down[...] = down[...].astype(f32)


VM = pl.BlockSpec(memory_space=pltpu.VMEM)
SM = pl.BlockSpec(memory_space=pltpu.SMEM)
HB = pl.BlockSpec(memory_space=pl.ANY)


def shape(sizes, kind):
    return jax.ShapeDtypeStruct(tuple(sizes), kind)


def call(kernel, name, operands, in_specs, out_shape, out_specs, scratch, flops):
    moved = sum(item.size * item.dtype.itemsize for item in operands)
    moved += sum(item.size * item.dtype.itemsize for item in out_shape)
    return pl.pallas_call(
        kernel,
        name=name,
        in_specs=in_specs,
        out_shape=out_shape,
        out_specs=out_specs,
        scratch_shapes=scratch,
        cost_estimate=pl.CostEstimate(flops=flops, bytes_accessed=moved, transcendentals=0),
        compiler_params=pltpu.CompilerParams(vmem_limit_bytes=VMEM_LIMIT),
    )(*operands)


def local(
    replicas,
    shards,
    tokens,
    lengths,
    gain_attn,
    w_query,
    w_key,
    w_value,
    w_out,
    gain_mlp,
    w_gate,
    w_up,
    w_down,
    cotangent,
):
    rows, width = tokens.shape
    part = w_gate.shape[0]
    hidden_width = w_gate.shape[1]
    packed = 2 * width + 2 * w_key.shape[1]
    rep_index = lax.axis_index("rep")
    shard = lax.axis_index("shard")
    core, x, y = ((rep_index >> bit) & 1 for bit in range(3))
    where = jnp.stack([core, x, y, shard]).astype(jnp.int32)
    block = 2 * core + x

    gain_rows = jnp.zeros((2, packed), low)
    gain_rows = lax.dynamic_update_slice(
        gain_rows, jnp.stack([gain_attn, gain_mlp]), (0, part * shard)
    )
    own = jnp.concatenate(
        [
            jnp.concatenate([w_out, w_query, w_key, w_value], axis=1),
            gain_rows,
            jnp.zeros((14, packed), low),
        ],
        axis=0,
    )
    attn_mine = lax.dynamic_slice(own, (80 * y, 384 * block), (80, 384))
    attn_got, attn_other = gather(attn_mine, (2, 1, 0), shards, replicas)
    pair_mine = jnp.where(
        y == 0,
        lax.dynamic_slice(w_gate, (0, 384 * block), (part, 384)),
        lax.dynamic_slice(w_up, (0, 384 * block), (part, 384)),
    )
    eighth = w_down.shape[0] // 8
    down_mine = lax.dynamic_slice(w_down, (eighth * (2 * block + y), 0), (eighth, width))
    pair_got, pair_other = gather(pair_mine, (2, 1, 0), shards, replicas)
    down_got, down_other = gather(down_mine, (1, 2, 0), shards, replicas)

    segment, position, live = token_layout(lengths[0], rows)
    cosine, sine = rotation_tables(position, HD)
    alive = live.astype(f32)[:, None]
    seg_col = segment[:, None]
    seg_row = segment[None, :]

    weights, gains, normed, query, keys, values = call(
        functools.partial(project_kernel, shards, part),
        "project",
        (where, tokens, cosine, sine, own, attn_got, attn_other),
        [SM, VM, VM, VM, HB, HB, HB],
        (
            shape((width + 16 * shards, packed), low),
            shape((8, width), f32),
            shape((rows, width), low),
            shape((HEADS, rows, HD), low),
            shape((KV, rows, HD), low),
            shape((KV, rows, HD), low),
        ),
        [VM] * 6,
        [pltpu.SemaphoreType.DMA((2 + 16 * (shards - 1),))],
        2 * rows * width * 1024,
    )
    mixed, log_total, hidden_one, normed_two = call(
        attend_kernel,
        "attend",
        (tokens, seg_col, seg_row, gains, weights, query, keys, values),
        [VM] * 8,
        (
            shape((rows, width), low),
            shape((HEADS, rows, 1), f32),
            shape((rows, width), f32),
            shape((rows, width), low),
        ),
        [VM] * 4,
        [pltpu.VMEM((rows, rows), f32)],
        8 * HEADS * rows * rows * HD,
    )
    pair_shape = shape((2, 2, shards, part, 384), low)
    down_shape = shape((2, 2, shards, eighth, width), low)
    result, grad_one, grad_gain_two, pair_keep, pair_send, down_keep, down_send = call(
        functools.partial(feed_kernel, shards, part),
        "feed",
        (
            where,
            hidden_one,
            normed_two,
            gains,
            alive,
            cotangent,
            w_gate,
            w_up,
            w_down,
            pair_got,
            pair_other,
            down_got,
            down_other,
        ),
        [SM] + [VM] * 5 + [HB] * 7,
        (
            shape((rows, width), low),
            shape((rows, width), f32),
            shape((8, width), f32),
            pair_shape,
            pair_shape,
            down_shape,
            down_shape,
        ),
        [VM] * 3 + [HB] * 4,
        [
            pltpu.VMEM((2, shards * part, hidden_width), low),
            pltpu.VMEM((hidden_width, width), low),
            pltpu.VMEM((rows, hidden_width), low),
            pltpu.VMEM((rows, hidden_width), low),
            pltpu.VMEM((rows, hidden_width), low),
            pltpu.VMEM((2, shards * part, hidden_width), low),
            pltpu.VMEM((hidden_width, width), low),
            pltpu.SemaphoreType.DMA((16 * shards + 3,)),
        ],
        18 * rows * width * hidden_width,
    )
    attn_shape = shape((2, 2, shards, 80, 384), low)
    grad_tokens, attn_keep, attn_send = call(
        functools.partial(back_kernel, shards, part),
        "back",
        (
            where,
            tokens,
            seg_col,
            seg_row,
            cosine,
            sine,
            gains,
            weights,
            normed,
            query,
            keys,
            values,
            mixed,
            log_total,
            grad_one,
            grad_gain_two,
        ),
        [SM] + [VM] * 15,
        (shape((rows, width), low), attn_shape, attn_shape),
        [VM, HB, HB],
        [
            pltpu.VMEM((rows, rows), f32),
            pltpu.VMEM((rows, width), low),
            pltpu.VMEM((rows, 1024), f32),
            pltpu.VMEM((rows, 1024), low),
            pltpu.VMEM((width + 16, packed), low),
            pltpu.SemaphoreType.DMA((16 * shards,)),
        ],
        20 * HEADS * rows * rows * HD + 4 * rows * width * 2048,
    )
    pair_total = scatter_over_shards(
        *scatter_in_plane(pair_keep, pair_send, (0, 1, 2), replicas), shards, replicas
    )
    down_total = scatter_over_shards(
        *scatter_in_plane(down_keep, down_send, (0, 2, 1), replicas), shards, replicas
    )
    attn_total = scatter_over_shards(
        *scatter_in_plane(attn_keep, attn_send, (0, 1, 2), replicas), shards, replicas
    )
    g_query, g_key, g_value, g_out, g_gains, g_gate, g_up, g_down = call(
        finish_kernel,
        "finish",
        (
            where,
            *spread(attn_total, (2, 1, 0), replicas),
            *spread(pair_total, (2, 1, 0), replicas),
            *spread(down_total, (1, 2, 0), replicas),
        ),
        [SM] + [HB] * 6,
        (
            shape(w_query.shape, f32),
            shape(w_key.shape, f32),
            shape(w_value.shape, f32),
            shape(w_out.shape, f32),
            shape((8, width), f32),
            shape(w_gate.shape, f32),
            shape(w_up.shape, f32),
            shape(w_down.shape, f32),
        ),
        [VM] * 8,
        [
            pltpu.VMEM((160, packed), low),
            pltpu.VMEM((2, part, hidden_width), low),
            pltpu.VMEM(w_down.shape, low),
            pltpu.SemaphoreType.DMA((24,)),
        ],
        0,
    )
    g_gains = lax.dynamic_slice(g_gains, (0, part * shard), (2, part))
    return (
        result,
        grad_tokens,
        g_gains[0],
        g_query,
        g_key,
        g_value,
        g_out,
        g_gains[1],
        g_gate,
        g_up,
        g_down,
    )


def solution(mesh):
    in_specs = (
        P(("rep", "shard"), None),
        P(("rep", "shard"), None),
        P("shard"),
        P("shard", None),
        P("shard", None),
        P("shard", None),
        P("shard", None),
        P("shard"),
        P("shard", None),
        P("shard", None),
        P("shard", None),
        P(("rep", "shard"), None),
    )
    out_specs = (
        P(("rep", "shard"), None),
        P(("rep", "shard"), None),
        P("shard"),
        P("shard", None),
        P("shard", None),
        P("shard", None),
        P("shard", None),
        P("shard"),
        P("shard", None),
        P("shard", None),
        P("shard", None),
    )
    part = functools.partial(local, mesh.shape["rep"], mesh.shape["shard"])
    return jax.shard_map(part, mesh=mesh, in_specs=in_specs, out_specs=out_specs, check_vma=False)
```

```python
import functools

import jax
import jax.numpy as jnp
from jax import lax
from jax.experimental import pallas as pl
from jax.experimental.pallas import tpu as pltpu
from jax.sharding import PartitionSpec as P
import numpy as np

HEADS = 9
KV = 3
HD = 64
RATIO = HEADS // KV


norm_eps = 1e-05
rope_base = 100000.0
neg_fill = -1e30

low = jnp.bfloat16
f32 = jnp.float32
QUERY_ROWS = 128


def rotation_tables(places, head_size):
    half = head_size // 2
    freq = np.float32(rope_base) ** (-(np.arange(half, dtype=np.float32) * np.float32(2.0) / head_size))
    angle = np.arange(places, dtype=np.float32)[:, None] * freq.astype(np.float32)[None, :]
    return np.concatenate([np.cos(angle)] * 4, axis=1), np.concatenate([np.sin(angle)] * 4, axis=1)


def matmul(left, right):
    return jnp.dot(left, right, preferred_element_type=f32)


def matmul_left_t(left, right):
    return lax.dot_general(left, right, (((0,), (0,)), ((), ())), preferred_element_type=f32)


def matmul_right_t(left, right):
    return lax.dot_general(left, right, (((1,), (1,)), ((), ())), preferred_element_type=f32)


def flip(value, bit, replicas):
    return lax.ppermute(value, "rep", [(i, i ^ (1 << bit)) for i in range(replicas)])


def shift_from(value, step, shards):
    return lax.ppermute(value, "shard", [((s + step) % shards, s) for s in range(shards)])


def shift_to(value, step, shards):
    return lax.ppermute(value, "shard", [(s, (s + step) % shards) for s in range(shards)])


def add_low(left, right):
    return (left.astype(f32) + right.astype(f32)).astype(low)


def gather(mine, order, shards, replicas):
    got = jnp.stack([shift_from(mine, step, shards) for step in range(1, shards)])
    for bit in order[:-1]:
        got = jnp.stack([got, flip(got, bit, replicas)])
    return got, flip(got, order[-1], replicas)


def scatter_in_plane(keep, send, order, replicas):
    other = flip(send, order[0], replicas)
    for bit in order[1:]:
        send = add_low(keep[1], other[1])
        moved = flip(send, bit, replicas)
        keep = add_low(keep[0], other[0])
        other = moved
    return keep, other


def scatter_over_shards(keep, other, shards, replicas):
    parts = [add_low(keep[step], other[step]) for step in range(1, shards)]
    moved = [shift_to(part, step + 1, shards) for step, part in enumerate(parts)]
    total = keep[0].astype(f32) + other[0].astype(f32)
    for part in moved:
        total = total + part.astype(f32)
    total = total.astype(low)
    bit = 3
    while (1 << bit) < replicas:
        total = add_low(total, flip(total, bit, replicas))
        bit += 1
    return total


def spread(total, order, replicas):
    for bit in order[:-1]:
        total = jnp.stack([total, flip(total, bit, replicas)])
    return total, flip(total, order[-1], replicas)


class Copies:
    def __init__(self, sems):
        self.sems = sems
        self.made = []

    def start(self, source, target):
        copy = pltpu.make_async_copy(source, target, self.sems.at[len(self.made)])
        copy.start()
        self.made.append(copy)

    def wait(self):
        for copy in self.made:
            copy.wait()


def rows_at(start, count, unit=16):
    return pl.ds(pl.multiple_of(start, unit), count)


def relative(bit, rel):
    return 1 - bit if rel else bit


def shard_at(shard, step, shards):
    at = shard + step
    return jnp.where(at >= shards, at - shards, at)


def swap_halves(values):
    lane = lax.broadcasted_iota(jnp.int32, values.shape, 1)
    return jnp.where(
        lane % HD < HD // 2,
        pltpu.roll(values, 2 * HD - HD // 2, 1),
        pltpu.roll(values, HD // 2, 1),
    )


def norm_recip(values):
    return lax.rsqrt(jnp.mean(values * values, axis=-1, keepdims=True) + norm_eps)


def norm_back(values, recip, gain, grad_normed):
    scaled = grad_normed * gain
    inner = jnp.mean(scaled * values, axis=-1, keepdims=True)
    grad_values = recip * scaled - values * (recip * recip * recip * inner)
    grad_gain = jnp.sum(grad_normed * values * recip, axis=0, keepdims=True)
    return (grad_values, grad_gain)


def prepare_kernel(
    where_ref,
    lengths,
    tokens_t,
    cotangent_t,
    table_cos,
    table_sin,
    gate,
    up,
    down_t,
    cosine,
    sine,
    bias,
    hidden,
    scaled,
    grad_low,
    pair_mine,
    down_mine,
    down,
):
    core, x, y = (where_ref[i] for i in range(3))
    block = 2 * core + x
    columns = rows_at(384 * block, 384, 128)
    pair_mine[...] = jnp.where(y == 0, gate[:, columns], up[:, columns])
    down[...] = down_t[...].T
    eighth = down_mine.shape[0]
    down_mine[...] = down[rows_at(eighth * (2 * block + y), eighth), :]
    rows = hidden.shape[0]
    count = lengths.shape[1]
    ends = []
    for i in range(count):
        ends.append(lengths[0, i] + (ends[-1] if ends else 0))
    place = lax.broadcasted_iota(jnp.int32, cosine.shape, 0)
    start_cos = jnp.broadcast_to(table_cos[0:1], cosine.shape)
    start_sin = jnp.broadcast_to(table_sin[0:1], cosine.shape)
    for end in ends:
        start_cos = jnp.where(place >= end, table_cos[pl.ds(end, 1)], start_cos)
        start_sin = jnp.where(place >= end, table_sin[pl.ds(end, 1)], start_sin)
    cos, sin = table_cos[0:rows], table_sin[0:rows]
    cosine[...] = cos * start_cos + sin * start_sin
    signed = sin * start_cos - cos * start_sin
    lane = lax.broadcasted_iota(jnp.int32, cosine.shape, 1)
    sine[...] = jnp.where(lane % HD < HD // 2, -signed, signed)
    query = lax.broadcasted_iota(jnp.int32, bias.shape, 0)
    key = lax.broadcasted_iota(jnp.int32, bias.shape, 1)
    allowed = query >= key
    for end in ends:
        allowed = allowed & ((query < end) | (key >= end))
    bias[...] = jnp.where(allowed, 0.0, neg_fill)
    values = tokens_t[...].T.astype(f32)
    hidden[...] = values
    scaled[...] = values * norm_recip(values)
    wide = lax.broadcasted_iota(jnp.int32, grad_low.shape, 0)
    grad_low[...] = jnp.where(wide < ends[-1], cotangent_t[...].T, jnp.zeros((), low))


def project_kernel(
    shards,
    part,
    where_ref,
    scaled,
    cosine,
    sine,
    own,
    pieces,
    other,
    weights,
    gains,
    normed,
    query,
    keys,
    values,
    sems,
):
    core, x, y, shard = (where_ref[i] for i in range(4))
    width = scaled.shape[1]
    copies = Copies(sems)
    copies.start(own.at[pl.ds(0, part)], weights.at[rows_at(part * shard, part)])
    copies.start(own.at[pl.ds(part, 16)], weights.at[rows_at(width + 16 * shard, 16)])
    for rel_core, source in enumerate((pieces, other)):
        for rel_x in range(2):
            for rel_y in range(2):
                at_y = relative(y, rel_y)
                block = 2 * relative(core, rel_core) + relative(x, rel_x)
                columns = rows_at(384 * block, 384, 128)
                for step in range(1, shards):
                    at = shard_at(shard, step, shards)
                    piece = source.at[rel_x, rel_y, step - 1]
                    copies.start(
                        piece.at[pl.ds(0, 64)], weights.at[rows_at(part * at + 80 * at_y, 64), columns]
                    )
                    last = jnp.where(at_y == 0, part * at + 64, width + 16 * at)
                    copies.start(piece.at[pl.ds(64, 16)], weights.at[rows_at(last, 16), columns])
    copies.wait()
    total = sum(
        weights[width + 16 * s : width + 16 * s + 16, :width].astype(f32) for s in range(shards)
    )
    gains[...] = total[:8]
    n1 = (scaled[...] * total[0:1]).astype(low)
    normed[...] = n1
    for block in range(8):
        start = 512 + 128 * block
        result = matmul(n1, weights[0:width, start : start + 128])
        heads = [2 * block - 1, 2 * block]
        if heads[0] < HEADS + KV:
            turned = result * cosine[...] + swap_halves(result) * sine[...]
        for side, head in enumerate(heads):
            lanes = slice(HD * side, HD * side + HD)
            if head < 0:
                continue
            if head < HEADS:
                query[head] = (turned[:, lanes] * HD**-0.5).astype(low)
            elif head < HEADS + KV:
                keys[head - HEADS] = turned[:, lanes].astype(low)
            else:
                values[head - HEADS - KV] = result[:, lanes].astype(low)


def attend_kernel(kv, bias, query, keys, values, mixed, log_total):
    rows = bias.shape[0]
    for block in range(rows // QUERY_ROWS):
        at = slice(QUERY_ROWS * block, QUERY_ROWS * (block + 1))
        reach = QUERY_ROWS * (block + 1)
        stacked = jnp.concatenate([query[RATIO * kv + i, at] for i in range(RATIO)], axis=0)
        scores = matmul_right_t(stacked, keys[kv, :reach])
        logits = scores.reshape(RATIO, QUERY_ROWS, reach) + bias[at, :reach][None]
        top = jnp.max(logits, axis=-1, keepdims=True)
        expo = jnp.exp(logits - top)
        total = jnp.sum(expo, axis=-1, keepdims=True)
        probs = (expo * (1.0 / total)).astype(low).reshape(RATIO * QUERY_ROWS, reach)
        log_total[:, at] = top + jnp.log(total)
        result = matmul(probs, values[kv, :reach]).astype(low)
        for i in range(RATIO):
            mixed[at, HD * i : HD * i + HD] = result[QUERY_ROWS * i : QUERY_ROWS * (i + 1)]


def attend_last_kernel(
    kv,
    bias,
    query,
    keys,
    values,
    hidden_in,
    gains,
    weights,
    *rest,
):
    before, (mixed, log_total, hidden_one, normed_two) = rest[:kv], rest[kv:]
    attend_kernel(kv, bias, query, keys, values, mixed, log_total)
    width = hidden_in.shape[1]
    every = jnp.concatenate([item[...] for item in before] + [mixed[...]], axis=1)
    hidden = hidden_in[...] + matmul(every, weights[0:width, 0:width])
    hidden_one[...] = hidden
    normed_two[...] = (hidden * norm_recip(hidden) * gains[1:2]).astype(low)


def feed_kernel(
    shards,
    part,
    where_ref,
    hidden_one,
    normed_two,
    gains,
    lengths,
    cotangent,
    own_gate,
    own_up,
    own_down,
    pair_pieces,
    pair_other,
    down_pieces,
    down_other,
    result,
    grad_one,
    grad_gain,
    pair_keep,
    pair_send,
    down_keep,
    down_send,
    pair,
    down,
    hidden,
    grad_gate,
    grad_up,
    grad_pair,
    grad_down,
    sems,
):
    core, x, y, shard = (where_ref[i] for i in range(4))
    width = hidden_one.shape[1]
    down_part = own_down.shape[0]
    eighth = down_part // 8
    copies = Copies(sems)
    copies.start(own_gate, pair.at[0, rows_at(part * shard, part)])
    copies.start(own_up, pair.at[1, rows_at(part * shard, part)])
    copies.start(own_down, down.at[rows_at(down_part * shard, down_part)])
    for rel_core, (source, down_source) in enumerate(
        ((pair_pieces, down_pieces), (pair_other, down_other))
    ):
        at_core = relative(core, rel_core)
        for rel_x in range(2):
            at_x = relative(x, rel_x)
            block = 2 * at_core + at_x
            columns = rows_at(384 * block, 384, 128)
            for rel_y in range(2):
                at_y = relative(y, rel_y)
                for step in range(1, shards):
                    at = shard_at(shard, step, shards)
                    copies.start(
                        source.at[rel_x, rel_y, step - 1],
                        pair.at[at_y, rows_at(part * at, part), columns],
                    )
                    copies.start(
                        down_source.at[rel_y, rel_x, step - 1],
                        down.at[rows_at(down_part * at + eighth * (2 * block + at_y), eighth)],
                    )
    grad_low = cotangent[...]
    n2 = normed_two[...]
    copies.wait()
    hidden_width = pair.shape[2]
    for start in range(0, hidden_width, 384):
        at = slice(start, start + 384)
        gate = matmul(n2, pair[0, :, at])
        upward = matmul(n2, pair[1, :, at])
        grad_hidden = matmul_right_t(grad_low, down[at, :])
        sigma = jax.nn.sigmoid(gate)
        active = gate * sigma
        hidden[:, at] = (active * upward).astype(low)
        grad_up[:, at] = (grad_hidden * active).astype(low)
        grad_gate[:, at] = (grad_hidden * upward * (sigma + active * (1.0 - sigma))).astype(low)
    turned = n2.T
    sent = Copies(sems)
    for unit, grads in enumerate((grad_gate, grad_up)):
        for block in range(4):
            at = slice(384 * block, 384 * block + 384)
            grad_pair[unit, :, at] = matmul(turned, grads[:, at]).astype(low)
    for start in range(0, hidden_width, 384):
        at = slice(start, start + 384)
        grad_down[at, :] = matmul_left_t(hidden[:, at], grad_low).astype(low)
    for rel_core, (target, down_target) in enumerate(((pair_keep, down_keep), (pair_send, down_send))):
        at_core = relative(core, rel_core)
        for rel_x in range(2):
            at_x = relative(x, rel_x)
            block = 2 * at_core + at_x
            columns = rows_at(384 * block, 384, 128)
            for rel_y in range(2):
                at_y = relative(y, rel_y)
                for step in range(shards):
                    at = shard_at(shard, step, shards)
                    sent.start(
                        grad_pair.at[at_y, rows_at(part * at, part), columns],
                        target.at[rel_x, rel_y, step],
                    )
                    sent.start(
                        grad_down.at[rows_at(down_part * at + eighth * (2 * block + at_y), eighth)],
                        down_target.at[rel_y, rel_x, step],
                    )
    h1 = hidden_one[...]
    total = lengths[0, 0]
    for i in range(1, lengths.shape[1]):
        total = total + lengths[0, i]
    row = lax.broadcasted_iota(jnp.int32, h1.shape, 0)
    summed = h1 + matmul(hidden[...], down[...])
    result[...] = jnp.where(row < total, summed, 0.0).astype(low).T
    grad_normed = matmul_right_t(grad_gate[...], pair[0]) + matmul_right_t(grad_up[...], pair[1])
    grad_from, gain_row = norm_back(h1, norm_recip(h1), gains[1:2], grad_normed)
    grad_one[...] = grad_low.astype(f32) + grad_from
    grad_gain[...] = jnp.broadcast_to(gain_row, grad_gain.shape)
    sent.wait()


def back_heads_kernel(
    kv,
    bias,
    cosine,
    sine,
    weights,
    query,
    keys,
    values,
    mixed,
    log_total,
    grad_one,
    grad_turned,
    grad_values_out,
    grad_out,
    grad_mixed,
    grad_heads,
):
    rows, width = grad_one.shape
    span = RATIO * HD
    da = grad_one[...].astype(low)
    grad_mixed[...] = matmul_right_t(da, weights[span * kv : span * kv + span, 0:width]).astype(low)
    grad_out[...] = matmul_left_t(mixed[...], da).astype(low)
    grad_keys = [None] * (rows // QUERY_ROWS)
    grad_values = [None] * (rows // QUERY_ROWS)
    for block in range(rows // QUERY_ROWS):
        at = slice(QUERY_ROWS * block, QUERY_ROWS * (block + 1))
        reach = QUERY_ROWS * (block + 1)
        stacked = jnp.concatenate([query[RATIO * kv + i, at] for i in range(RATIO)], axis=0)
        grads = jnp.concatenate([grad_mixed[at, HD * i : HD * i + HD] for i in range(RATIO)], axis=0)
        out = jnp.concatenate([mixed[at, HD * i : HD * i + HD] for i in range(RATIO)], axis=0)
        delta = jnp.sum(grads.astype(f32) * out.astype(f32), axis=-1, keepdims=True)
        scores = matmul_right_t(stacked, keys[kv, :reach]).reshape(RATIO, QUERY_ROWS, reach)
        probs = jnp.exp(scores + bias[at, :reach][None] - log_total[:, at]).reshape(-1, reach)
        grad_probs = matmul_right_t(grads, values[kv, :reach])
        grad_scores = (probs * (grad_probs - delta)).astype(low)
        grad_query = matmul(grad_scores, keys[kv, :reach])
        for i in range(RATIO):
            grad_heads[at, HD * i : HD * i + HD] = (
                grad_query[QUERY_ROWS * i : QUERY_ROWS * (i + 1)] * HD**-0.5
            )
        key_part = matmul_left_t(grad_scores, stacked)
        value_part = matmul_left_t(probs.astype(low), grads)
        for j in range(block + 1):
            at_j = slice(QUERY_ROWS * j, QUERY_ROWS * (j + 1))
            if grad_keys[j] is None:
                grad_keys[j], grad_values[j] = key_part[at_j], value_part[at_j]
            else:
                grad_keys[j] = grad_keys[j] + key_part[at_j]
                grad_values[j] = grad_values[j] + value_part[at_j]
    grad_heads[:, span : span + HD] = jnp.concatenate(grad_keys, axis=0)
    grad_values_out[...] = jnp.concatenate(grad_values, axis=0).astype(low)
    for start in range(0, span + HD, 2 * HD):
        value = grad_heads[:, start : start + 2 * HD]
        turned = value * cosine[...] - swap_halves(value) * sine[...]
        grad_turned[:, start : start + 2 * HD] = turned.astype(low)


def back_last_kernel(
    shards,
    part,
    where_ref,
    hidden_in,
    gains,
    weights,
    normed,
    grad_one,
    grad_gain_two,
    *rest,
):
    core, x, y, shard = (where_ref[i] for i in range(4))
    rows, width = hidden_in.shape
    turned, values, outs = rest[0:KV], rest[KV : 2 * KV], rest[2 * KV : 3 * KV]
    grad_tokens, keep, send, grad_low, grad_weights, sems = rest[3 * KV :]
    span = RATIO * HD
    grad_low[...] = jnp.concatenate(
        [jnp.zeros((rows, HD), low)]
        + [item[:, 0:span] for item in turned]
        + [item[:, span : span + HD] for item in turned]
        + [item[...] for item in values],
        axis=1,
    )
    normed_t = normed[...].T
    for start in range(0, 1024, 512):
        at = slice(start, start + 512)
        grad_weights[0:width, 512 + start : 1024 + start] = matmul(normed_t, grad_low[:, at]).astype(low)
    for kv in range(KV):
        grad_weights[span * kv : span * kv + span, 0:width] = outs[kv][...]
    grad_normed = matmul_right_t(grad_low[...], weights[0:width, 512:1536])
    hidden = hidden_in[...]
    grad_from, gain_row = norm_back(hidden, norm_recip(hidden), gains[0:1], grad_normed)
    grad_tokens[...] = (grad_one[...] + grad_from).astype(low).T
    row = lax.broadcasted_iota(jnp.int32, (16, width), 0)
    both = jnp.where(
        row == 0,
        jnp.broadcast_to(gain_row, (16, width)),
        jnp.where(row == 1, jnp.broadcast_to(grad_gain_two[0:1], (16, width)), 0.0),
    )
    grad_weights[width : width + 16, :] = jnp.zeros((16, grad_weights.shape[1]), low)
    grad_weights[width : width + 16, 0:width] = both.astype(low)
    copies = Copies(sems)
    for rel_core, target in enumerate((keep, send)):
        for rel_x in range(2):
            for rel_y in range(2):
                at_y = relative(y, rel_y)
                block = 2 * relative(core, rel_core) + relative(x, rel_x)
                columns = rows_at(384 * block, 384, 128)
                for step in range(shards):
                    at = shard_at(shard, step, shards)
                    piece = target.at[rel_y, rel_x, step]
                    copies.start(
                        grad_weights.at[rows_at(part * at + 80 * at_y, 64), columns],
                        piece.at[pl.ds(0, 64)],
                    )
                    last = jnp.where(at_y == 0, part * at + 64, width)
                    copies.start(grad_weights.at[rows_at(last, 16), columns], piece.at[pl.ds(64, 16)])
    copies.wait()


def finish_feed_kernel(
    where_ref,
    pair_pieces,
    pair_other,
    down_pieces,
    down_other,
    out_gate,
    out_up,
    out_down,
    pair,
    down,
    sems,
):
    core, x, y = (where_ref[i] for i in range(3))
    eighth = down.shape[0] // 8
    copies = Copies(sems)
    for rel_core, (p_from, d_from) in enumerate(
        ((pair_pieces, down_pieces), (pair_other, down_other))
    ):
        for rel_x in range(2):
            for rel_y in range(2):
                at_y = relative(y, rel_y)
                block = 2 * relative(core, rel_core) + relative(x, rel_x)
                columns = rows_at(384 * block, 384, 128)
                copies.start(p_from.at[rel_x, rel_y], pair.at[at_y, :, columns])
                copies.start(
                    d_from.at[rel_y, rel_x], down.at[rows_at(eighth * (2 * block + at_y), eighth)]
                )
    copies.wait()
    out_gate[...] = pair[0].astype(f32)
    out_up[...] = pair[1].astype(f32)
    out_down[...] = down[...].T.astype(f32)


def finish_attn_kernel(
    where_ref,
    pieces,
    other,
    out_query,
    out_key,
    out_value,
    out_out,
    out_gains,
    attn,
    sems,
):
    core, x, y = (where_ref[i] for i in range(3))
    part = out_out.shape[0]
    copies = Copies(sems)
    for rel_core, source in enumerate((pieces, other)):
        for rel_x in range(2):
            for rel_y in range(2):
                block = 2 * relative(core, rel_core) + relative(x, rel_x)
                columns = rows_at(384 * block, 384, 128)
                copies.start(
                    source.at[rel_y, rel_x], attn.at[rows_at(80 * relative(y, rel_y), 80), columns]
                )
    copies.wait()
    width = out_out.shape[1]
    kv_width = out_key.shape[1]
    out_out[...] = attn[0:part, 0:width].astype(f32)
    rest = attn[0:part, 512:].astype(f32)
    at = width - 512
    out_query[...] = rest[:, at : at + width]
    out_key[...] = rest[:, at + width : at + width + kv_width]
    out_value[...] = rest[:, at + width + kv_width :]
    out_gains[...] = attn[part : part + 16, 0:width].astype(f32)[:8]


VM = pl.BlockSpec(memory_space=pltpu.VMEM)
SM = pl.BlockSpec(memory_space=pltpu.SMEM)
HB = pl.BlockSpec(memory_space=pl.ANY)


def shape(sizes, kind):
    return jax.ShapeDtypeStruct(tuple(sizes), kind)


def call(kernel, name, operands, in_specs, out_shape, out_specs, scratch, micros, room):
    moved = sum(item.size * item.dtype.itemsize for item in out_shape)
    return pl.pallas_call(
        kernel,
        name=name,
        in_specs=in_specs,
        out_shape=out_shape,
        out_specs=out_specs,
        scratch_shapes=scratch,
        cost_estimate=pl.CostEstimate(
            flops=int(micros * 1.1e9), bytes_accessed=moved, transcendentals=0
        ),
        compiler_params=pltpu.CompilerParams(vmem_limit_bytes=room << 20),
    )(*operands)


def local(
    replicas,
    shards,
    tokens,
    lengths,
    gain_attn,
    w_query,
    w_key,
    w_value,
    w_out,
    gain_mlp,
    w_gate,
    w_up,
    w_down,
    cotangent,
):
    rows, width = tokens.shape
    part = w_gate.shape[0]
    hidden_width = w_gate.shape[1]
    down_part = w_down.shape[0]
    eighth = down_part // 8
    packed = 2 * width + 2 * w_key.shape[1]
    rep_index = lax.axis_index("rep")
    shard = lax.axis_index("shard")
    core, x, y = ((rep_index >> bit) & 1 for bit in range(3))
    where = jnp.stack([core, x, y, shard]).astype(jnp.int32)
    block = 2 * core + x

    gain_rows = jnp.zeros((2, packed), low)
    gain_rows = lax.dynamic_update_slice(
        gain_rows, jnp.stack([gain_attn, gain_mlp]), (0, part * shard)
    )
    own = jnp.concatenate(
        [
            jnp.concatenate([w_out, w_query, w_key, w_value], axis=1),
            gain_rows,
            jnp.zeros((14, packed), low),
        ],
        axis=0,
    )
    attn_mine = lax.dynamic_slice(own, (80 * y, 384 * block), (80, 384))
    attn_got, attn_other = gather(attn_mine, (2, 1, 0), shards, replicas)
    table_cos, table_sin = rotation_tables(rows + 8, HD)
    cosine, sine, bias, hidden_in, scaled, grad_low, pair_mine, down_mine, own_down = call(
        prepare_kernel,
        "prepare",
        (where, lengths, tokens.T, cotangent.T, table_cos, table_sin, w_gate, w_up, w_down.T),
        [SM, SM] + [VM] * 7,
        (
            shape((rows, 2 * HD), f32),
            shape((rows, 2 * HD), f32),
            shape((rows, rows), f32),
            shape((rows, width), f32),
            shape((rows, width), f32),
            shape((rows, width), low),
            shape((part, 384), low),
            shape((eighth, width), low),
            shape((down_part, width), low),
        ),
        [VM] * 9,
        [],
        5,
        24,
    )
    pair_got, pair_other = gather(pair_mine, (2, 1, 0), shards, replicas)
    down_got, down_other = gather(down_mine, (1, 2, 0), shards, replicas)

    weights, gains, normed, query, keys, values = call(
        functools.partial(project_kernel, shards, part),
        "project",
        (where, scaled, cosine, sine, own, attn_got, attn_other),
        [SM, VM, VM, VM, HB, HB, HB],
        (
            shape((width + 16 * shards, packed), low),
            shape((8, width), f32),
            shape((rows, width), low),
            shape((HEADS, rows, HD), low),
            shape((KV, rows, HD), low),
            shape((KV, rows, HD), low),
        ),
        [VM] * 6,
        [pltpu.SemaphoreType.DMA((2 + 16 * (shards - 1),))],
        5,
        24,
    )
    mixed, log_total = [], []
    for kv in range(KV):
        outs = [shape((rows, RATIO * HD), low), shape((RATIO, rows, 1), f32)]
        operands = (bias, query, keys, values)
        if kv < KV - 1:
            one, two = call(
                functools.partial(attend_kernel, kv),
                f"attend_{kv}",
                operands,
                [VM] * 4,
                outs,
                [VM] * 2,
                [],
                3,
                24,
            )
        else:
            operands += (hidden_in, gains, weights, *mixed)
            one, two, hidden_one, normed_two = call(
                functools.partial(attend_last_kernel, kv),
                f"attend_{kv}",
                operands,
                [VM] * len(operands),
                outs + [shape((rows, width), f32), shape((rows, width), low)],
                [VM] * 4,
                [],
                4,
                24,
            )
        mixed.append(one)
        log_total.append(two)
    pair_shape = shape((2, 2, shards, part, 384), low)
    down_shape = shape((2, 2, shards, eighth, width), low)
    result, grad_one, grad_gain_two, pair_keep, pair_send, down_keep, down_send = call(
        functools.partial(feed_kernel, shards, part),
        "feed",
        (
            where,
            hidden_one,
            normed_two,
            gains,
            lengths,
            grad_low,
            w_gate,
            w_up,
            own_down,
            pair_got,
            pair_other,
            down_got,
            down_other,
        ),
        [SM] + [VM] * 3 + [SM, VM] + [HB] * 7,
        (
            shape((width, rows), low),
            shape((rows, width), f32),
            shape((8, width), f32),
            pair_shape,
            pair_shape,
            down_shape,
            down_shape,
        ),
        [VM] * 3 + [HB] * 4,
        [
            pltpu.VMEM((2, shards * part, hidden_width), low),
            pltpu.VMEM((hidden_width, width), low),
            pltpu.VMEM((rows, hidden_width), low),
            pltpu.VMEM((rows, hidden_width), low),
            pltpu.VMEM((rows, hidden_width), low),
            pltpu.VMEM((2, shards * part, hidden_width), low),
            pltpu.VMEM((hidden_width, width), low),
            pltpu.SemaphoreType.DMA((16 * shards + 3,)),
        ],
        19,
        48,
    )
    grad_turned, grad_values, grad_out = [], [], []
    for kv in range(KV):
        one, two, three = call(
            functools.partial(back_heads_kernel, kv),
            f"back_{kv}",
            (bias, cosine, sine, weights, query, keys, values, mixed[kv], log_total[kv], grad_one),
            [VM] * 10,
            (
                shape((rows, RATIO * HD + HD), low),
                shape((rows, HD), low),
                shape((RATIO * HD, width), low),
            ),
            [VM] * 3,
            [pltpu.VMEM((rows, RATIO * HD), low), pltpu.VMEM((rows, RATIO * HD + HD), f32)],
            5,
            24,
        )
        grad_turned.append(one)
        grad_values.append(two)
        grad_out.append(three)
    attn_shape = shape((2, 2, shards, 80, 384), low)
    grad_tokens, attn_keep, attn_send = call(
        functools.partial(back_last_kernel, shards, part),
        "back_last",
        (
            where,
            hidden_in,
            gains,
            weights,
            normed,
            grad_one,
            grad_gain_two,
            *grad_turned,
            *grad_values,
            *grad_out,
        ),
        [SM] + [VM] * (6 + 3 * KV),
        (shape((width, rows), low), attn_shape, attn_shape),
        [VM, HB, HB],
        [
            pltpu.VMEM((rows, 1024), low),
            pltpu.VMEM((width + 16, packed), low),
            pltpu.SemaphoreType.DMA((16 * shards,)),
        ],
        6,
        24,
    )
    pair_total = scatter_over_shards(
        *scatter_in_plane(pair_keep, pair_send, (0, 1, 2), replicas), shards, replicas
    )
    down_total = scatter_over_shards(
        *scatter_in_plane(down_keep, down_send, (0, 2, 1), replicas), shards, replicas
    )
    attn_total = scatter_over_shards(
        *scatter_in_plane(attn_keep, attn_send, (0, 2, 1), replicas), shards, replicas
    )
    g_gate, g_up, g_down = call(
        finish_feed_kernel,
        "finish_feed",
        (
            where,
            *spread(pair_total, (2, 1, 0), replicas),
            *spread(down_total, (1, 2, 0), replicas),
        ),
        [SM] + [HB] * 4,
        (
            shape(w_gate.shape, f32),
            shape(w_up.shape, f32),
            shape((width, down_part), f32),
        ),
        [VM] * 3,
        [
            pltpu.VMEM((2, part, hidden_width), low),
            pltpu.VMEM(w_down.shape, low),
            pltpu.SemaphoreType.DMA((16,)),
        ],
        3,
        16,
    )
    g_query, g_key, g_value, g_out, g_gains = call(
        finish_attn_kernel,
        "finish_attn",
        (where, *spread(attn_total, (1, 2, 0), replicas)),
        [SM] + [HB] * 2,
        (
            shape(w_query.shape, f32),
            shape(w_key.shape, f32),
            shape(w_value.shape, f32),
            shape(w_out.shape, f32),
            shape((8, width), f32),
        ),
        [VM] * 5,
        [pltpu.VMEM((160, packed), low), pltpu.SemaphoreType.DMA((8,))],
        2,
        16,
    )
    g_gains = lax.dynamic_slice(g_gains, (0, part * shard), (2, part))
    return (
        result.T,
        grad_tokens.T,
        g_gains[0],
        g_query,
        g_key,
        g_value,
        g_out,
        g_gains[1],
        g_gate,
        g_up,
        g_down.T,
    )


def solution(mesh):
    in_specs = (
        P(("rep", "shard"), None),
        P(("rep", "shard"), None),
        P("shard"),
        P("shard", None),
        P("shard", None),
        P("shard", None),
        P("shard", None),
        P("shard"),
        P("shard", None),
        P("shard", None),
        P("shard", None),
        P(("rep", "shard"), None),
    )
    out_specs = (
        P(("rep", "shard"), None),
        P(("rep", "shard"), None),
        P("shard"),
        P("shard", None),
        P("shard", None),
        P("shard", None),
        P("shard", None),
        P("shard"),
        P("shard", None),
        P("shard", None),
        P("shard", None),
    )
    part = functools.partial(local, mesh.shape["rep"], mesh.shape["shard"])
    return jax.shard_map(part, mesh=mesh, in_specs=in_specs, out_specs=out_specs, check_vma=False)
```

```python
import functools

import jax
import jax.numpy as jnp
from jax import lax
from jax.experimental import pallas as pl
from jax.experimental.pallas import tpu as pltpu
from jax.sharding import PartitionSpec as P
import numpy as np

HEADS = 9
KV = 3
HD = 64
RATIO = HEADS // KV


norm_eps = 1e-05
rope_base = 100000.0
neg_fill = -1e30

low = jnp.bfloat16
f32 = jnp.float32
QUERY_ROWS = 128


def rotation_tables(places, head_size):
    half = head_size // 2
    freq = np.float32(rope_base) ** (-(np.arange(half, dtype=np.float32) * np.float32(2.0) / head_size))
    angle = np.arange(places, dtype=np.float32)[:, None] * freq.astype(np.float32)[None, :]
    return np.concatenate([np.cos(angle)] * 4, axis=1), np.concatenate([np.sin(angle)] * 4, axis=1)


def matmul(left, right):
    return jnp.dot(left, right, preferred_element_type=f32)


def matmul_left_t(left, right):
    return lax.dot_general(left, right, (((0,), (0,)), ((), ())), preferred_element_type=f32)


def matmul_right_t(left, right):
    return lax.dot_general(left, right, (((1,), (1,)), ((), ())), preferred_element_type=f32)


def flip(value, bit, replicas):
    return lax.ppermute(value, "rep", [(i, i ^ (1 << bit)) for i in range(replicas)])


def shift_from(value, step, shards):
    return lax.ppermute(value, "shard", [((s + step) % shards, s) for s in range(shards)])


def shift_to(value, step, shards):
    return lax.ppermute(value, "shard", [(s, (s + step) % shards) for s in range(shards)])


def add_low(left, right):
    return (left.astype(f32) + right.astype(f32)).astype(low)


def after(value, *others):
    return lax.optimization_barrier((value, *others))[0]


def gather_shards(mine, shards):
    return jnp.stack([shift_from(mine, step, shards) for step in range(1, shards)])


def gather_bit(got, bit, replicas):
    return jnp.stack([got, flip(got, bit, replicas)])


def halve(keep, other, bit, replicas):
    sent = flip(add_low(keep[1], other[1]), bit, replicas)
    return add_low(keep[0], other[0]), sent


def scatter_over_shards(keep, other, shards, replicas):
    parts = [add_low(keep[step], other[step]) for step in range(1, shards)]
    moved = [shift_to(part, step + 1, shards) for step, part in enumerate(parts)]
    total = keep[0].astype(f32) + other[0].astype(f32)
    for part in moved:
        total = total + part.astype(f32)
    total = total.astype(low)
    bit = 3
    while (1 << bit) < replicas:
        total = add_low(total, flip(total, bit, replicas))
        bit += 1
    return total


def spread(total, order, replicas):
    for bit in order[:-1]:
        total = jnp.stack([total, flip(total, bit, replicas)])
    return total, flip(total, order[-1], replicas)


class Copies:
    def __init__(self, sems):
        self.sems = sems
        self.made = []

    def start(self, source, target):
        copy = pltpu.make_async_copy(source, target, self.sems.at[len(self.made)])
        copy.start()
        self.made.append(copy)

    def wait(self):
        for copy in self.made:
            copy.wait()


def rows_at(start, count, unit=16):
    return pl.ds(pl.multiple_of(start, unit), count)


def relative(bit, rel):
    return 1 - bit if rel else bit


def shard_at(shard, step, shards):
    at = shard + step
    return jnp.where(at >= shards, at - shards, at)


def swap_halves(values):
    lane = lax.broadcasted_iota(jnp.int32, values.shape, 1)
    return jnp.where(
        lane % HD < HD // 2,
        pltpu.roll(values, 2 * HD - HD // 2, 1),
        pltpu.roll(values, HD // 2, 1),
    )


def norm_recip(values):
    return lax.rsqrt(jnp.mean(values * values, axis=-1, keepdims=True) + norm_eps)


def norm_back(values, recip, gain, grad_normed):
    scaled = grad_normed * gain
    inner = jnp.mean(scaled * values, axis=-1, keepdims=True)
    grad_values = recip * scaled - values * (recip * recip * recip * inner)
    grad_gain = jnp.sum(grad_normed * values * recip, axis=0, keepdims=True)
    return (grad_values, grad_gain)


def prepare_kernel(
    lengths,
    tokens_t,
    cotangent_t,
    table_cos,
    table_sin,
    down_t,
    cosine,
    sine,
    bias,
    hidden,
    scaled,
    grad_low,
    down,
):
    down[...] = down_t[...].T
    rows = hidden.shape[0]
    count = lengths.shape[1]
    ends = []
    for i in range(count):
        ends.append(lengths[0, i] + (ends[-1] if ends else 0))
    place = lax.broadcasted_iota(jnp.int32, cosine.shape, 0)
    start_cos = jnp.broadcast_to(table_cos[0:1], cosine.shape)
    start_sin = jnp.broadcast_to(table_sin[0:1], cosine.shape)
    for end in ends:
        start_cos = jnp.where(place >= end, table_cos[pl.ds(end, 1)], start_cos)
        start_sin = jnp.where(place >= end, table_sin[pl.ds(end, 1)], start_sin)
    cos, sin = table_cos[0:rows], table_sin[0:rows]
    cosine[...] = cos * start_cos + sin * start_sin
    signed = sin * start_cos - cos * start_sin
    lane = lax.broadcasted_iota(jnp.int32, cosine.shape, 1)
    sine[...] = jnp.where(lane % HD < HD // 2, -signed, signed)
    query = lax.broadcasted_iota(jnp.int32, bias.shape, 0)
    key = lax.broadcasted_iota(jnp.int32, bias.shape, 1)
    allowed = query >= key
    for end in ends:
        allowed = allowed & ((query < end) | (key >= end))
    bias[...] = jnp.where(allowed, 0.0, neg_fill)
    values = tokens_t[...].T.astype(f32)
    hidden[...] = values
    scaled[...] = values * norm_recip(values)
    wide = lax.broadcasted_iota(jnp.int32, grad_low.shape, 0)
    grad_low[...] = jnp.where(wide < ends[-1], cotangent_t[...].T, jnp.zeros((), low))


def project_kernel(
    shards,
    part,
    where_ref,
    scaled,
    cosine,
    sine,
    own,
    pieces,
    other,
    weights,
    gains,
    normed,
    query,
    keys,
    values,
    sems,
):
    core, x, y, shard = (where_ref[i] for i in range(4))
    width = scaled.shape[1]
    copies = Copies(sems)
    copies.start(own.at[pl.ds(0, part)], weights.at[rows_at(part * shard, part)])
    copies.start(own.at[pl.ds(part, 16)], weights.at[rows_at(width + 16 * shard, 16)])
    for rel_core, source in enumerate((pieces, other)):
        for rel_x in range(2):
            for rel_y in range(2):
                at_y = relative(y, rel_y)
                block = 2 * relative(core, rel_core) + relative(x, rel_x)
                columns = rows_at(384 * block, 384, 128)
                for step in range(1, shards):
                    at = shard_at(shard, step, shards)
                    piece = source.at[rel_x, rel_y, step - 1]
                    copies.start(
                        piece.at[pl.ds(0, 64)], weights.at[rows_at(part * at + 80 * at_y, 64), columns]
                    )
                    last = jnp.where(at_y == 0, part * at + 64, width + 16 * at)
                    copies.start(piece.at[pl.ds(64, 16)], weights.at[rows_at(last, 16), columns])
    copies.wait()
    total = sum(
        weights[width + 16 * s : width + 16 * s + 16, :width].astype(f32) for s in range(shards)
    )
    gains[...] = total[:8]
    n1 = (scaled[...] * total[0:1]).astype(low)
    normed[...] = n1
    for block in range(8):
        start = 512 + 128 * block
        result = matmul(n1, weights[0:width, start : start + 128])
        heads = [2 * block - 1, 2 * block]
        if heads[0] < HEADS + KV:
            turned = result * cosine[...] + swap_halves(result) * sine[...]
        for side, head in enumerate(heads):
            lanes = slice(HD * side, HD * side + HD)
            if head < 0:
                continue
            if head < HEADS:
                query[head] = (turned[:, lanes] * HD**-0.5).astype(low)
            elif head < HEADS + KV:
                keys[head - HEADS] = turned[:, lanes].astype(low)
            else:
                values[head - HEADS - KV] = result[:, lanes].astype(low)


def attend_kernel(kv, bias, query, keys, values, mixed, log_total):
    rows = bias.shape[0]
    for block in range(rows // QUERY_ROWS):
        at = slice(QUERY_ROWS * block, QUERY_ROWS * (block + 1))
        reach = QUERY_ROWS * (block + 1)
        stacked = jnp.concatenate([query[RATIO * kv + i, at] for i in range(RATIO)], axis=0)
        scores = matmul_right_t(stacked, keys[kv, :reach])
        logits = scores.reshape(RATIO, QUERY_ROWS, reach) + bias[at, :reach][None]
        top = jnp.max(logits, axis=-1, keepdims=True)
        expo = jnp.exp(logits - top)
        total = jnp.sum(expo, axis=-1, keepdims=True)
        probs = (expo * (1.0 / total)).astype(low).reshape(RATIO * QUERY_ROWS, reach)
        log_total[:, at] = top + jnp.log(total)
        result = matmul(probs, values[kv, :reach]).astype(low)
        for i in range(RATIO):
            mixed[at, HD * i : HD * i + HD] = result[QUERY_ROWS * i : QUERY_ROWS * (i + 1)]


def attend_last_kernel(
    kv,
    bias,
    query,
    keys,
    values,
    hidden_in,
    gains,
    weights,
    *rest,
):
    before, (mixed, log_total, hidden_one, normed_two) = rest[:kv], rest[kv:]
    attend_kernel(kv, bias, query, keys, values, mixed, log_total)
    width = hidden_in.shape[1]
    every = jnp.concatenate([item[...] for item in before] + [mixed[...]], axis=1)
    hidden = hidden_in[...] + matmul(every, weights[0:width, 0:width])
    hidden_one[...] = hidden
    normed_two[...] = (hidden * norm_recip(hidden) * gains[1:2]).astype(low)


def feed_kernel(
    shards,
    part,
    where_ref,
    hidden_one,
    normed_two,
    gains,
    lengths,
    cotangent,
    own_gate,
    own_up,
    own_down,
    pair_pieces,
    pair_other,
    down_pieces,
    down_other,
    result,
    grad_one,
    grad_gain,
    pair_keep,
    pair_send,
    down_keep,
    down_send,
    pair,
    down,
    hidden,
    grad_gate,
    grad_up,
    grad_pair,
    grad_down,
    sems,
):
    core, x, y, shard = (where_ref[i] for i in range(4))
    width = hidden_one.shape[1]
    down_part = own_down.shape[0]
    eighth = down_part // 8
    copies = Copies(sems)
    copies.start(own_gate, pair.at[0, rows_at(part * shard, part)])
    copies.start(own_up, pair.at[1, rows_at(part * shard, part)])
    copies.start(own_down, down.at[rows_at(down_part * shard, down_part)])
    for rel_core, (source, down_source) in enumerate(
        ((pair_pieces, down_pieces), (pair_other, down_other))
    ):
        at_core = relative(core, rel_core)
        for rel_x in range(2):
            at_x = relative(x, rel_x)
            block = 2 * at_core + at_x
            columns = rows_at(384 * block, 384, 128)
            for rel_y in range(2):
                at_y = relative(y, rel_y)
                for step in range(1, shards):
                    at = shard_at(shard, step, shards)
                    copies.start(
                        source.at[rel_x, rel_y, step - 1],
                        pair.at[at_y, rows_at(part * at, part), columns],
                    )
                    copies.start(
                        down_source.at[rel_y, rel_x, step - 1],
                        down.at[rows_at(down_part * at + eighth * (2 * block + at_y), eighth)],
                    )
    grad_low = cotangent[...]
    n2 = normed_two[...]
    copies.wait()
    hidden_width = pair.shape[2]
    for start in range(0, hidden_width, 384):
        at = slice(start, start + 384)
        gate = matmul(n2, pair[0, :, at])
        upward = matmul(n2, pair[1, :, at])
        grad_hidden = matmul_right_t(grad_low, down[at, :])
        sigma = jax.nn.sigmoid(gate)
        active = gate * sigma
        hidden[:, at] = (active * upward).astype(low)
        grad_up[:, at] = (grad_hidden * active).astype(low)
        grad_gate[:, at] = (grad_hidden * upward * (sigma + active * (1.0 - sigma))).astype(low)
    turned = n2.T
    sent = Copies(sems)
    for unit, grads in enumerate((grad_gate, grad_up)):
        for block in range(4):
            at = slice(384 * block, 384 * block + 384)
            grad_pair[unit, :, at] = matmul(turned, grads[:, at]).astype(low)
    for start in range(0, hidden_width, 384):
        at = slice(start, start + 384)
        grad_down[at, :] = matmul_left_t(hidden[:, at], grad_low).astype(low)
    for rel_core, (target, down_target) in enumerate(((pair_keep, down_keep), (pair_send, down_send))):
        at_core = relative(core, rel_core)
        for rel_x in range(2):
            at_x = relative(x, rel_x)
            block = 2 * at_core + at_x
            columns = rows_at(384 * block, 384, 128)
            for rel_y in range(2):
                at_y = relative(y, rel_y)
                for step in range(shards):
                    at = shard_at(shard, step, shards)
                    sent.start(
                        grad_pair.at[at_y, rows_at(part * at, part), columns],
                        target.at[rel_x, rel_y, step],
                    )
                    sent.start(
                        grad_down.at[rows_at(down_part * at + eighth * (2 * block + at_y), eighth)],
                        down_target.at[rel_y, rel_x, step],
                    )
    h1 = hidden_one[...]
    total = lengths[0, 0]
    for i in range(1, lengths.shape[1]):
        total = total + lengths[0, i]
    row = lax.broadcasted_iota(jnp.int32, h1.shape, 0)
    summed = h1 + matmul(hidden[...], down[...])
    result[...] = jnp.where(row < total, summed, 0.0).astype(low).T
    grad_normed = matmul_right_t(grad_gate[...], pair[0]) + matmul_right_t(grad_up[...], pair[1])
    grad_from, gain_row = norm_back(h1, norm_recip(h1), gains[1:2], grad_normed)
    grad_one[...] = grad_low.astype(f32) + grad_from
    grad_gain[...] = jnp.broadcast_to(gain_row, grad_gain.shape)
    sent.wait()


def back_heads_kernel(
    kv,
    bias,
    cosine,
    sine,
    weights,
    query,
    keys,
    values,
    mixed,
    log_total,
    grad_one,
    grad_turned,
    grad_values_out,
    grad_out,
    grad_mixed,
    grad_heads,
):
    rows, width = grad_one.shape
    span = RATIO * HD
    da = grad_one[...].astype(low)
    grad_mixed[...] = matmul_right_t(da, weights[span * kv : span * kv + span, 0:width]).astype(low)
    grad_out[...] = matmul_left_t(mixed[...], da).astype(low)
    grad_keys = [None] * (rows // QUERY_ROWS)
    grad_values = [None] * (rows // QUERY_ROWS)
    for block in range(rows // QUERY_ROWS):
        at = slice(QUERY_ROWS * block, QUERY_ROWS * (block + 1))
        reach = QUERY_ROWS * (block + 1)
        stacked = jnp.concatenate([query[RATIO * kv + i, at] for i in range(RATIO)], axis=0)
        grads = jnp.concatenate([grad_mixed[at, HD * i : HD * i + HD] for i in range(RATIO)], axis=0)
        out = jnp.concatenate([mixed[at, HD * i : HD * i + HD] for i in range(RATIO)], axis=0)
        delta = jnp.sum(grads.astype(f32) * out.astype(f32), axis=-1, keepdims=True)
        scores = matmul_right_t(stacked, keys[kv, :reach]).reshape(RATIO, QUERY_ROWS, reach)
        probs = jnp.exp(scores + bias[at, :reach][None] - log_total[:, at]).reshape(-1, reach)
        grad_probs = matmul_right_t(grads, values[kv, :reach])
        grad_scores = (probs * (grad_probs - delta)).astype(low)
        grad_query = matmul(grad_scores, keys[kv, :reach])
        for i in range(RATIO):
            grad_heads[at, HD * i : HD * i + HD] = (
                grad_query[QUERY_ROWS * i : QUERY_ROWS * (i + 1)] * HD**-0.5
            )
        key_part = matmul_left_t(grad_scores, stacked)
        value_part = matmul_left_t(probs.astype(low), grads)
        for j in range(block + 1):
            at_j = slice(QUERY_ROWS * j, QUERY_ROWS * (j + 1))
            if grad_keys[j] is None:
                grad_keys[j], grad_values[j] = key_part[at_j], value_part[at_j]
            else:
                grad_keys[j] = grad_keys[j] + key_part[at_j]
                grad_values[j] = grad_values[j] + value_part[at_j]
    grad_heads[:, span : span + HD] = jnp.concatenate(grad_keys, axis=0)
    grad_values_out[...] = jnp.concatenate(grad_values, axis=0).astype(low)
    for start in range(0, span + HD, 2 * HD):
        value = grad_heads[:, start : start + 2 * HD]
        turned = value * cosine[...] - swap_halves(value) * sine[...]
        grad_turned[:, start : start + 2 * HD] = turned.astype(low)


def back_last_kernel(
    shards,
    part,
    where_ref,
    hidden_in,
    gains,
    weights,
    normed,
    grad_one,
    grad_gain_two,
    *rest,
):
    core, x, y, shard = (where_ref[i] for i in range(4))
    rows, width = hidden_in.shape
    turned, values, outs = rest[0:KV], rest[KV : 2 * KV], rest[2 * KV : 3 * KV]
    grad_tokens, keep, send, grad_low, grad_weights, sems = rest[3 * KV :]
    span = RATIO * HD
    grad_low[...] = jnp.concatenate(
        [jnp.zeros((rows, HD), low)]
        + [item[:, 0:span] for item in turned]
        + [item[:, span : span + HD] for item in turned]
        + [item[...] for item in values],
        axis=1,
    )
    normed_t = normed[...].T
    for start in range(0, 1024, 512):
        at = slice(start, start + 512)
        grad_weights[0:width, 512 + start : 1024 + start] = matmul(normed_t, grad_low[:, at]).astype(low)
    for kv in range(KV):
        grad_weights[span * kv : span * kv + span, 0:width] = outs[kv][...]
    grad_normed = matmul_right_t(grad_low[...], weights[0:width, 512:1536])
    hidden = hidden_in[...]
    grad_from, gain_row = norm_back(hidden, norm_recip(hidden), gains[0:1], grad_normed)
    grad_tokens[...] = (grad_one[...] + grad_from).astype(low).T
    row = lax.broadcasted_iota(jnp.int32, (16, width), 0)
    both = jnp.where(
        row == 0,
        jnp.broadcast_to(gain_row, (16, width)),
        jnp.where(row == 1, jnp.broadcast_to(grad_gain_two[0:1], (16, width)), 0.0),
    )
    grad_weights[width : width + 16, :] = jnp.zeros((16, grad_weights.shape[1]), low)
    grad_weights[width : width + 16, 0:width] = both.astype(low)
    copies = Copies(sems)
    for rel_core, target in enumerate((keep, send)):
        for rel_x in range(2):
            for rel_y in range(2):
                at_y = relative(y, rel_y)
                block = 2 * relative(core, rel_core) + relative(x, rel_x)
                columns = rows_at(384 * block, 384, 128)
                for step in range(shards):
                    at = shard_at(shard, step, shards)
                    piece = target.at[rel_y, rel_x, step]
                    copies.start(
                        grad_weights.at[rows_at(part * at + 80 * at_y, 64), columns],
                        piece.at[pl.ds(0, 64)],
                    )
                    last = jnp.where(at_y == 0, part * at + 64, width)
                    copies.start(grad_weights.at[rows_at(last, 16), columns], piece.at[pl.ds(64, 16)])
    copies.wait()


def finish_feed_kernel(
    where_ref,
    pair_pieces,
    pair_other,
    down_pieces,
    down_other,
    out_gate,
    out_up,
    out_down,
    pair,
    down,
    sems,
):
    core, x, y = (where_ref[i] for i in range(3))
    eighth = down.shape[0] // 8
    copies = Copies(sems)
    for rel_core, (p_from, d_from) in enumerate(
        ((pair_pieces, down_pieces), (pair_other, down_other))
    ):
        for rel_x in range(2):
            for rel_y in range(2):
                at_y = relative(y, rel_y)
                block = 2 * relative(core, rel_core) + relative(x, rel_x)
                columns = rows_at(384 * block, 384, 128)
                copies.start(p_from.at[rel_x, rel_y], pair.at[at_y, :, columns])
                copies.start(
                    d_from.at[rel_y, rel_x], down.at[rows_at(eighth * (2 * block + at_y), eighth)]
                )
    copies.wait()
    out_gate[...] = pair[0].astype(f32)
    out_up[...] = pair[1].astype(f32)
    out_down[...] = down[...].T.astype(f32)


def finish_attn_kernel(
    where_ref,
    pieces,
    other,
    out_query,
    out_key,
    out_value,
    out_out,
    out_gains,
    attn,
    sems,
):
    core, x, y = (where_ref[i] for i in range(3))
    part = out_out.shape[0]
    copies = Copies(sems)
    for rel_core, source in enumerate((pieces, other)):
        for rel_x in range(2):
            for rel_y in range(2):
                block = 2 * relative(core, rel_core) + relative(x, rel_x)
                columns = rows_at(384 * block, 384, 128)
                copies.start(
                    source.at[rel_y, rel_x], attn.at[rows_at(80 * relative(y, rel_y), 80), columns]
                )
    copies.wait()
    width = out_out.shape[1]
    kv_width = out_key.shape[1]
    out_out[...] = attn[0:part, 0:width].astype(f32)
    rest = attn[0:part, 512:].astype(f32)
    at = width - 512
    out_query[...] = rest[:, at : at + width]
    out_key[...] = rest[:, at + width : at + width + kv_width]
    out_value[...] = rest[:, at + width + kv_width :]
    out_gains[...] = attn[part : part + 16, 0:width].astype(f32)[:8]


VM = pl.BlockSpec(memory_space=pltpu.VMEM)
SM = pl.BlockSpec(memory_space=pltpu.SMEM)
HB = pl.BlockSpec(memory_space=pl.ANY)


def shape(sizes, kind):
    return jax.ShapeDtypeStruct(tuple(sizes), kind)


def call(kernel, name, operands, in_specs, out_shape, out_specs, scratch, micros, room):
    moved = sum(item.size * item.dtype.itemsize for item in out_shape)
    return pl.pallas_call(
        kernel,
        name=name,
        in_specs=in_specs,
        out_shape=out_shape,
        out_specs=out_specs,
        scratch_shapes=scratch,
        cost_estimate=pl.CostEstimate(
            flops=int(micros * 1e7), bytes_accessed=moved, transcendentals=0
        ),
        compiler_params=pltpu.CompilerParams(vmem_limit_bytes=room << 20),
    )(*operands)


def local(
    replicas,
    shards,
    tokens,
    lengths,
    gain_attn,
    w_query,
    w_key,
    w_value,
    w_out,
    gain_mlp,
    w_gate,
    w_up,
    w_down,
    cotangent,
):
    rows, width = tokens.shape
    part = w_gate.shape[0]
    hidden_width = w_gate.shape[1]
    down_part = w_down.shape[0]
    eighth = down_part // 8
    packed = 2 * width + 2 * w_key.shape[1]
    rep_index = lax.axis_index("rep")
    shard = lax.axis_index("shard")
    core, x, y = ((rep_index >> bit) & 1 for bit in range(3))
    where = jnp.stack([core, x, y, shard]).astype(jnp.int32)
    block = 2 * core + x

    gain_rows = jnp.zeros((2, packed), low)
    gain_rows = lax.dynamic_update_slice(
        gain_rows, jnp.stack([gain_attn, gain_mlp]), (0, part * shard)
    )
    own = jnp.concatenate(
        [
            jnp.concatenate([w_out, w_query, w_key, w_value], axis=1),
            gain_rows,
            jnp.zeros((14, packed), low),
        ],
        axis=0,
    )
    attn_mine = lax.dynamic_slice(own, (80 * y, 384 * block), (80, 384))
    pair_mine = jnp.where(
        y == 0,
        lax.dynamic_slice(w_gate, (0, 384 * block), (part, 384)),
        lax.dynamic_slice(w_up, (0, 384 * block), (part, 384)),
    )
    down_mine = lax.dynamic_slice(w_down, (eighth * (2 * block + y), 0), (eighth, width))
    pair_got = gather_shards(pair_mine, shards)
    down_got = gather_shards(down_mine, shards)
    attn_got = gather_shards(attn_mine, shards)
    table_cos, table_sin = rotation_tables(rows + 8, HD)
    cosine, sine, bias, hidden_in, scaled, grad_low, own_down = call(
        prepare_kernel,
        "prepare",
        (lengths, tokens.T, cotangent.T, table_cos, table_sin, w_down.T),
        [SM] + [VM] * 5,
        (
            shape((rows, 2 * HD), f32),
            shape((rows, 2 * HD), f32),
            shape((rows, rows), f32),
            shape((rows, width), f32),
            shape((rows, width), f32),
            shape((rows, width), low),
            shape((down_part, width), low),
        ),
        [VM] * 7,
        [],
        5,
        24,
    )
    attn_got = after(attn_got, pair_got, down_got, scaled)
    pair_got = gather_bit(pair_got, 2, replicas)
    down_got = gather_bit(down_got, 1, replicas)
    attn_got = gather_bit(gather_bit(attn_got, 2, replicas), 1, replicas)
    attn_got = after(attn_got, pair_got, down_got)
    attn_other = flip(attn_got, 0, replicas)
    pair_got = gather_bit(after(pair_got, attn_other), 1, replicas)
    down_got = gather_bit(after(down_got, attn_other), 2, replicas)

    weights, gains, normed, query, keys, values = call(
        functools.partial(project_kernel, shards, part),
        "project",
        (where, scaled, cosine, sine, own, attn_got, attn_other),
        [SM, VM, VM, VM, HB, HB, HB],
        (
            shape((width + 16 * shards, packed), low),
            shape((8, width), f32),
            shape((rows, width), low),
            shape((HEADS, rows, HD), low),
            shape((KV, rows, HD), low),
            shape((KV, rows, HD), low),
        ),
        [VM] * 6,
        [pltpu.SemaphoreType.DMA((2 + 16 * (shards - 1),))],
        5,
        24,
    )
    mixed, log_total = [], []
    for kv in range(KV):
        outs = [shape((rows, RATIO * HD), low), shape((RATIO, rows, 1), f32)]
        operands = (bias, query, keys, values)
        if kv < KV - 1:
            one, two = call(
                functools.partial(attend_kernel, kv),
                f"attend_{kv}",
                operands,
                [VM] * 4,
                outs,
                [VM] * 2,
                [],
                3,
                24,
            )
        else:
            operands += (after(hidden_in, down_got), gains, weights, *mixed)
            one, two, hidden_one, normed_two = call(
                functools.partial(attend_last_kernel, kv),
                f"attend_{kv}",
                operands,
                [VM] * len(operands),
                outs + [shape((rows, width), f32), shape((rows, width), low)],
                [VM] * 4,
                [],
                4,
                24,
            )
        mixed.append(one)
        log_total.append(two)
    pair_other = flip(after(pair_got, normed_two), 0, replicas)
    down_other = flip(after(down_got, normed_two), 0, replicas)
    pair_shape = shape((2, 2, shards, part, 384), low)
    down_shape = shape((2, 2, shards, eighth, width), low)
    result, grad_one, grad_gain_two, pair_keep, pair_send, down_keep, down_send = call(
        functools.partial(feed_kernel, shards, part),
        "feed",
        (
            where,
            hidden_one,
            normed_two,
            gains,
            lengths,
            grad_low,
            w_gate,
            w_up,
            own_down,
            pair_got,
            pair_other,
            down_got,
            down_other,
        ),
        [SM] + [VM] * 3 + [SM, VM] + [HB] * 7,
        (
            shape((width, rows), low),
            shape((rows, width), f32),
            shape((8, width), f32),
            pair_shape,
            pair_shape,
            down_shape,
            down_shape,
        ),
        [VM] * 3 + [HB] * 4,
        [
            pltpu.VMEM((2, shards * part, hidden_width), low),
            pltpu.VMEM((hidden_width, width), low),
            pltpu.VMEM((rows, hidden_width), low),
            pltpu.VMEM((rows, hidden_width), low),
            pltpu.VMEM((rows, hidden_width), low),
            pltpu.VMEM((2, shards * part, hidden_width), low),
            pltpu.VMEM((hidden_width, width), low),
            pltpu.SemaphoreType.DMA((16 * shards + 3,)),
        ],
        19,
        48,
    )
    pair_sent = flip(pair_send, 0, replicas)
    down_sent = flip(down_send, 0, replicas)
    grad_turned, grad_values, grad_out = [], [], []
    for kv in range(KV):
        if kv == 1:
            pair_left = halve(pair_keep, after(pair_sent, grad_turned[0]), 1, replicas)
            down_left = halve(down_keep, down_sent, 2, replicas)
            grad_one = after(grad_one, pair_sent, down_sent)
        one, two, three = call(
            functools.partial(back_heads_kernel, kv),
            f"back_{kv}",
            (bias, cosine, sine, weights, query, keys, values, mixed[kv], log_total[kv], grad_one),
            [VM] * 10,
            (
                shape((rows, RATIO * HD + HD), low),
                shape((rows, HD), low),
                shape((RATIO * HD, width), low),
            ),
            [VM] * 3,
            [pltpu.VMEM((rows, RATIO * HD), low), pltpu.VMEM((rows, RATIO * HD + HD), f32)],
            5,
            24,
        )
        grad_turned.append(one)
        grad_values.append(two)
        grad_out.append(three)
    grad_one = after(grad_one, down_left[1])
    attn_shape = shape((2, 2, shards, 80, 384), low)
    grad_tokens, attn_keep, attn_send = call(
        functools.partial(back_last_kernel, shards, part),
        "back_last",
        (
            where,
            hidden_in,
            gains,
            weights,
            normed,
            grad_one,
            grad_gain_two,
            *grad_turned,
            *grad_values,
            *grad_out,
        ),
        [SM] + [VM] * (6 + 3 * KV),
        (shape((width, rows), low), attn_shape, attn_shape),
        [VM, HB, HB],
        [
            pltpu.VMEM((rows, 1024), low),
            pltpu.VMEM((width + 16, packed), low),
            pltpu.SemaphoreType.DMA((16 * shards,)),
        ],
        6,
        24,
    )
    pair_left = halve(*pair_left, 2, replicas)
    pair_total = scatter_over_shards(*pair_left, shards, replicas)
    down_left = halve(*down_left, 1, replicas)
    down_total = scatter_over_shards(*down_left, shards, replicas)
    attn_left = halve(attn_keep, flip(attn_send, 0, replicas), 2, replicas)
    attn_left = halve(*attn_left, 1, replicas)
    attn_total = scatter_over_shards(*attn_left, shards, replicas)
    g_gate, g_up, g_down = call(
        finish_feed_kernel,
        "finish_feed",
        (
            where,
            *spread(pair_total, (2, 1, 0), replicas),
            *spread(down_total, (1, 2, 0), replicas),
        ),
        [SM] + [HB] * 4,
        (
            shape(w_gate.shape, f32),
            shape(w_up.shape, f32),
            shape((width, down_part), f32),
        ),
        [VM] * 3,
        [
            pltpu.VMEM((2, part, hidden_width), low),
            pltpu.VMEM(w_down.shape, low),
            pltpu.SemaphoreType.DMA((16,)),
        ],
        3,
        16,
    )
    g_query, g_key, g_value, g_out, g_gains = call(
        finish_attn_kernel,
        "finish_attn",
        (where, *spread(attn_total, (1, 2, 0), replicas)),
        [SM] + [HB] * 2,
        (
            shape(w_query.shape, f32),
            shape(w_key.shape, f32),
            shape(w_value.shape, f32),
            shape(w_out.shape, f32),
            shape((8, width), f32),
        ),
        [VM] * 5,
        [pltpu.VMEM((160, packed), low), pltpu.SemaphoreType.DMA((8,))],
        2,
        16,
    )
    g_gains = lax.dynamic_slice(g_gains, (0, part * shard), (2, part))
    return (
        result.T,
        grad_tokens.T,
        g_gains[0],
        g_query,
        g_key,
        g_value,
        g_out,
        g_gains[1],
        g_gate,
        g_up,
        g_down.T,
    )


def solution(mesh):
    in_specs = (
        P(("rep", "shard"), None),
        P(("rep", "shard"), None),
        P("shard"),
        P("shard", None),
        P("shard", None),
        P("shard", None),
        P("shard", None),
        P("shard"),
        P("shard", None),
        P("shard", None),
        P("shard", None),
        P(("rep", "shard"), None),
    )
    out_specs = (
        P(("rep", "shard"), None),
        P(("rep", "shard"), None),
        P("shard"),
        P("shard", None),
        P("shard", None),
        P("shard", None),
        P("shard", None),
        P("shard"),
        P("shard", None),
        P("shard", None),
        P("shard", None),
    )
    part = functools.partial(local, mesh.shape["rep"], mesh.shape["shard"])
    return jax.shard_map(part, mesh=mesh, in_specs=in_specs, out_specs=out_specs, check_vma=False)
```

```python
import functools

import jax
import jax.numpy as jnp
from jax import lax
from jax.experimental import pallas as pl
from jax.experimental.pallas import tpu as pltpu
from jax.sharding import PartitionSpec as P
import numpy as np

HEADS = 9
KV = 3
HD = 64
RATIO = HEADS // KV


norm_eps = 1e-05
rope_base = 100000.0
neg_fill = -1e30

low = jnp.bfloat16
f32 = jnp.float32
QUERY_ROWS = 128


def rotation_tables(places, head_size):
    half = head_size // 2
    freq = np.float32(rope_base) ** (-(np.arange(half, dtype=np.float32) * np.float32(2.0) / head_size))
    angle = np.arange(places, dtype=np.float32)[:, None] * freq.astype(np.float32)[None, :]
    return np.concatenate([np.cos(angle)] * 4, axis=1), np.concatenate([np.sin(angle)] * 4, axis=1)


def matmul(left, right):
    return jnp.dot(left, right, preferred_element_type=f32)


def matmul_left_t(left, right):
    return lax.dot_general(left, right, (((0,), (0,)), ((), ())), preferred_element_type=f32)


def matmul_right_t(left, right):
    return lax.dot_general(left, right, (((1,), (1,)), ((), ())), preferred_element_type=f32)


def flip(value, bit, replicas):
    return lax.ppermute(value, "rep", [(i, i ^ (1 << bit)) for i in range(replicas)])


def shift_from(value, step, shards):
    return lax.ppermute(value, "shard", [((s + step) % shards, s) for s in range(shards)])


def shift_to(value, step, shards):
    return lax.ppermute(value, "shard", [(s, (s + step) % shards) for s in range(shards)])


def add_low(left, right):
    return (left.astype(f32) + right.astype(f32)).astype(low)


def after(value, *others):
    return lax.optimization_barrier((value, *others))[0]


def gather_shards(mine, shards):
    return jnp.stack([shift_from(mine, step, shards) for step in range(1, shards)])


def gather_bit(got, bit, replicas):
    return jnp.stack([got, flip(got, bit, replicas)])


def halve(keep, other, bit, replicas):
    sent = flip(add_low(keep[1], other[1]), bit, replicas)
    return add_low(keep[0], other[0]), sent


def scatter_over_shards(keep, other, shards, replicas):
    parts = [add_low(keep[step], other[step]) for step in range(1, shards)]
    moved = [shift_to(part, step + 1, shards) for step, part in enumerate(parts)]
    total = keep[0].astype(f32) + other[0].astype(f32)
    for part in moved:
        total = total + part.astype(f32)
    total = total.astype(low)
    bit = 3
    while (1 << bit) < replicas:
        total = add_low(total, flip(total, bit, replicas))
        bit += 1
    return total


def spread(total, order, replicas):
    for bit in order[:-1]:
        total = jnp.stack([total, flip(total, bit, replicas)])
    return total, flip(total, order[-1], replicas)


class Copies:
    def __init__(self, sems):
        self.sems = sems
        self.made = []

    def start(self, source, target):
        copy = pltpu.make_async_copy(source, target, self.sems.at[len(self.made)])
        copy.start()
        self.made.append(copy)

    def wait(self, first=0, last=None):
        for copy in self.made[first:last]:
            copy.wait()


def rows_at(start, count, unit=16):
    return pl.ds(pl.multiple_of(start, unit), count)


def relative(bit, rel):
    return 1 - bit if rel else bit


def shard_at(shard, step, shards):
    at = shard + step
    return jnp.where(at >= shards, at - shards, at)


def swap_halves(values):
    lane = lax.broadcasted_iota(jnp.int32, values.shape, 1)
    return jnp.where(
        lane % HD < HD // 2,
        pltpu.roll(values, 2 * HD - HD // 2, 1),
        pltpu.roll(values, HD // 2, 1),
    )


def norm_recip(values):
    return lax.rsqrt(jnp.mean(values * values, axis=-1, keepdims=True) + norm_eps)


def norm_back(values, recip, gain, grad_normed):
    scaled = grad_normed * gain
    inner = jnp.mean(scaled * values, axis=-1, keepdims=True)
    grad_values = recip * scaled - values * (recip * recip * recip * inner)
    grad_gain = jnp.sum(grad_normed * values * recip, axis=0, keepdims=True)
    return (grad_values, grad_gain)


def pack_kernel(
    where_ref, w_out, w_query, w_key, w_value, gain_one, gain_two, gate, up, down_t, own, mine, down
):
    core, x, y, shard = (where_ref[i] for i in range(4))
    block = 2 * core + x
    part = gate.shape[0]
    packed = own.shape[1]
    columns = rows_at(384 * block, 384, 128)
    mine[0:part] = jnp.where(y == 0, gate[:, columns], up[:, columns])
    own[0:part] = jnp.concatenate([w_out[...], w_query[...], w_key[...], w_value[...]], axis=1)
    row = lax.broadcasted_iota(jnp.int32, (16, part), 0)
    gains = jnp.where(
        row == 0,
        jnp.broadcast_to(gain_one[...].astype(f32), row.shape),
        jnp.where(row == 1, jnp.broadcast_to(gain_two[...].astype(f32), row.shape), 0.0),
    )
    gains = jnp.concatenate([gains, jnp.zeros((16, packed - part), f32)], axis=1)
    own[part : part + 16] = pltpu.roll(gains, part * shard, 1).astype(low)
    mine[part : part + 80] = own[rows_at(80 * y, 80), columns]
    down[...] = down_t[...].T
    eighth = down.shape[0] // 8
    piece = down[rows_at(eighth * (2 * block + y), eighth), :]
    mine[part + 80 : part + 80 + eighth] = piece[:, :384]
    mine[part + 80 + eighth :] = jnp.concatenate(
        [piece[:, 384:], jnp.zeros((eighth, 768 - piece.shape[1]), low)], axis=1
    )


def fold(value):
    rest = value[..., 384:]
    pad = [(0, 0)] * (value.ndim - 1) + [(0, 384 - rest.shape[-1])]
    return jnp.concatenate([value[..., :384], jnp.pad(rest, pad)], axis=-2)


def unfold(value, width):
    half = value.shape[-2] // 2
    return jnp.concatenate([value[..., :half, :], value[..., half:, : width - 384]], axis=-1)


def prepare_kernel(
    lengths,
    tokens_t,
    cotangent_t,
    table_cos,
    table_sin,
    cosine,
    sine,
    bias,
    hidden,
    scaled,
    grad_low,
):
    rows = hidden.shape[0]
    count = lengths.shape[1]
    ends = []
    for i in range(count):
        ends.append(lengths[0, i] + (ends[-1] if ends else 0))
    place = lax.broadcasted_iota(jnp.int32, cosine.shape, 0)
    start_cos = jnp.broadcast_to(table_cos[0:1], cosine.shape)
    start_sin = jnp.broadcast_to(table_sin[0:1], cosine.shape)
    for end in ends:
        start_cos = jnp.where(place >= end, table_cos[pl.ds(end, 1)], start_cos)
        start_sin = jnp.where(place >= end, table_sin[pl.ds(end, 1)], start_sin)
    cos, sin = table_cos[0:rows], table_sin[0:rows]
    cosine[...] = cos * start_cos + sin * start_sin
    signed = sin * start_cos - cos * start_sin
    lane = lax.broadcasted_iota(jnp.int32, cosine.shape, 1)
    sine[...] = jnp.where(lane % HD < HD // 2, -signed, signed)
    query = lax.broadcasted_iota(jnp.int32, bias.shape, 0)
    key = lax.broadcasted_iota(jnp.int32, bias.shape, 1)
    allowed = query >= key
    for end in ends:
        allowed = allowed & ((query < end) | (key >= end))
    bias[...] = jnp.where(allowed, 0.0, neg_fill)
    values = tokens_t[...].T.astype(f32)
    hidden[...] = values
    scaled[...] = values * norm_recip(values)
    wide = lax.broadcasted_iota(jnp.int32, grad_low.shape, 0)
    grad_low[...] = jnp.where(wide < ends[-1], cotangent_t[...].T, jnp.zeros((), low))


def project_kernel(
    shards,
    part,
    where_ref,
    scaled,
    cosine,
    sine,
    own,
    pieces,
    other,
    weights,
    gains,
    normed,
    query,
    keys,
    values,
    sems,
):
    core, x, y, shard = (where_ref[i] for i in range(4))
    width = scaled.shape[1]
    copies = Copies(sems)
    copies.start(own.at[pl.ds(0, part)], weights.at[rows_at(part * shard, part)])
    copies.start(own.at[pl.ds(part, 16)], weights.at[rows_at(width + 16 * shard, 16)])
    for rel_core, source in enumerate((pieces, other)):
        for rel_x in range(2):
            for rel_y in range(2):
                at_y = relative(y, rel_y)
                block = 2 * relative(core, rel_core) + relative(x, rel_x)
                columns = rows_at(384 * block, 384, 128)
                for step in range(1, shards):
                    at = shard_at(shard, step, shards)
                    piece = source.at[rel_y, rel_x, step - 1]
                    copies.start(
                        piece.at[pl.ds(0, 64)], weights.at[rows_at(part * at + 80 * at_y, 64), columns]
                    )
                    last = jnp.where(at_y == 0, part * at + 64, width + 16 * at)
                    copies.start(piece.at[pl.ds(64, 16)], weights.at[rows_at(last, 16), columns])
    copies.wait()
    total = sum(
        weights[width + 16 * s : width + 16 * s + 16, :width].astype(f32) for s in range(shards)
    )
    gains[...] = total[:8]
    n1 = (scaled[...] * total[0:1]).astype(low)
    normed[...] = n1
    for block in range(8):
        start = 512 + 128 * block
        result = matmul(n1, weights[0:width, start : start + 128])
        heads = [2 * block - 1, 2 * block]
        if heads[0] < HEADS + KV:
            turned = result * cosine[...] + swap_halves(result) * sine[...]
        for side, head in enumerate(heads):
            lanes = slice(HD * side, HD * side + HD)
            if head < 0:
                continue
            if head < HEADS:
                query[head] = (turned[:, lanes] * HD**-0.5).astype(low)
            elif head < HEADS + KV:
                keys[head - HEADS] = turned[:, lanes].astype(low)
            else:
                values[head - HEADS - KV] = result[:, lanes].astype(low)


def attend_kernel(kv, bias, query, keys, values, mixed, log_total):
    rows = bias.shape[0]
    for block in range(rows // QUERY_ROWS):
        at = slice(QUERY_ROWS * block, QUERY_ROWS * (block + 1))
        reach = QUERY_ROWS * (block + 1)
        stacked = jnp.concatenate([query[RATIO * kv + i, at] for i in range(RATIO)], axis=0)
        scores = matmul_right_t(stacked, keys[kv, :reach])
        logits = scores.reshape(RATIO, QUERY_ROWS, reach) + bias[at, :reach][None]
        top = jnp.max(logits, axis=-1, keepdims=True)
        expo = jnp.exp(logits - top)
        total = jnp.sum(expo, axis=-1, keepdims=True)
        probs = (expo * (1.0 / total)).astype(low).reshape(RATIO * QUERY_ROWS, reach)
        log_total[:, at] = top + jnp.log(total)
        result = matmul(probs, values[kv, :reach]).astype(low)
        for i in range(RATIO):
            mixed[at, HD * i : HD * i + HD] = result[QUERY_ROWS * i : QUERY_ROWS * (i + 1)]


def attend_last_kernel(
    kv,
    bias,
    query,
    keys,
    values,
    hidden_in,
    gains,
    weights,
    *rest,
):
    before, (mixed, log_total, hidden_one, normed_two) = rest[:kv], rest[kv:]
    attend_kernel(kv, bias, query, keys, values, mixed, log_total)
    width = hidden_in.shape[1]
    every = jnp.concatenate([item[...] for item in before] + [mixed[...]], axis=1)
    hidden = hidden_in[...] + matmul(every, weights[0:width, 0:width])
    hidden_one[...] = hidden
    normed_two[...] = (hidden * norm_recip(hidden) * gains[1:2]).astype(low)


def feed_kernel(
    shards,
    part,
    where_ref,
    hidden_one,
    normed_two,
    gains,
    lengths,
    cotangent,
    own_gate,
    own_up,
    own_down,
    pair_pieces,
    pair_other,
    down_pieces,
    down_other,
    result,
    grad_one,
    grad_gain,
    pair_keep,
    pair_send,
    down_keep,
    down_send,
    pair,
    down,
    hidden,
    grad_gate,
    grad_up,
    grad_pair,
    grad_down,
    sems,
):
    core, x, y, shard = (where_ref[i] for i in range(4))
    width = hidden_one.shape[1]
    down_part = own_down.shape[0]
    eighth = down_part // 8
    copies = Copies(sems)
    copies.start(own_gate, pair.at[0, rows_at(part * shard, part)])
    copies.start(own_up, pair.at[1, rows_at(part * shard, part)])
    for rel_core, source in enumerate((pair_pieces, pair_other)):
        for rel_x in range(2):
            block = 2 * relative(core, rel_core) + relative(x, rel_x)
            columns = rows_at(384 * block, 384, 128)
            for rel_y in range(2):
                at_y = relative(y, rel_y)
                for step in range(1, shards):
                    at = shard_at(shard, step, shards)
                    copies.start(
                        source.at[rel_x, rel_y, step - 1],
                        pair.at[at_y, rows_at(part * at, part), columns],
                    )
    first = len(copies.made)
    copies.start(own_down, down.at[rows_at(down_part * shard, down_part)])
    for rel_core, source in enumerate((down_pieces, down_other)):
        for rel_x in range(2):
            block = 2 * relative(core, rel_core) + relative(x, rel_x)
            for rel_y in range(2):
                place = eighth * (2 * block + relative(y, rel_y))
                for step in range(1, shards):
                    at = shard_at(shard, step, shards)
                    copies.start(
                        source.at[rel_y, rel_x, step - 1],
                        down.at[rows_at(down_part * at + place, eighth)],
                    )
    grad_low = cotangent[...]
    n2 = normed_two[...]
    copies.wait(0, first)
    hidden_width = pair.shape[2]
    for start in range(0, hidden_width, 512):
        at = slice(start, start + 512)
        gate = matmul(n2, pair[0, :, at])
        upward = matmul(n2, pair[1, :, at])
        if start == 0:
            copies.wait(first)
        grad_hidden = matmul_right_t(grad_low, down[at, :])
        sigma = jax.nn.sigmoid(gate)
        active = gate * sigma
        hidden[:, at] = (active * upward).astype(low)
        grad_up[:, at] = (grad_hidden * active).astype(low)
        grad_gate[:, at] = (grad_hidden * upward * (sigma + active * (1.0 - sigma))).astype(low)
    turned = n2.T
    sent = Copies(sems)
    for unit, grads in enumerate((grad_gate, grad_up)):
        for start in range(0, hidden_width, 512):
            at = slice(start, start + 512)
            grad_pair[unit, :, at] = matmul(turned, grads[:, at]).astype(low)
    for start in range(0, hidden_width, 512):
        at = slice(start, start + 512)
        grad_down[at, :] = matmul_left_t(hidden[:, at], grad_low).astype(low)
    for rel_core, (target, down_target) in enumerate(((pair_keep, down_keep), (pair_send, down_send))):
        at_core = relative(core, rel_core)
        for rel_x in range(2):
            at_x = relative(x, rel_x)
            block = 2 * at_core + at_x
            columns = rows_at(384 * block, 384, 128)
            for rel_y in range(2):
                at_y = relative(y, rel_y)
                for step in range(shards):
                    at = shard_at(shard, step, shards)
                    sent.start(
                        grad_pair.at[at_y, rows_at(part * at, part), columns],
                        target.at[rel_x, rel_y, step],
                    )
                    sent.start(
                        grad_down.at[rows_at(down_part * at + eighth * (2 * block + at_y), eighth)],
                        down_target.at[rel_y, rel_x, step],
                    )
    h1 = hidden_one[...]
    total = lengths[0, 0]
    for i in range(1, lengths.shape[1]):
        total = total + lengths[0, i]
    row = lax.broadcasted_iota(jnp.int32, h1.shape, 0)
    summed = h1 + matmul(hidden[...], down[...])
    result[...] = jnp.where(row < total, summed, 0.0).astype(low).T
    grad_normed = matmul_right_t(grad_gate[...], pair[0]) + matmul_right_t(grad_up[...], pair[1])
    grad_from, gain_row = norm_back(h1, norm_recip(h1), gains[1:2], grad_normed)
    grad_one[...] = grad_low.astype(f32) + grad_from
    grad_gain[...] = jnp.broadcast_to(gain_row, grad_gain.shape)
    sent.wait()


def back_heads_kernel(
    kv,
    bias,
    cosine,
    sine,
    weights,
    query,
    keys,
    values,
    mixed,
    log_total,
    grad_one,
    grad_turned,
    grad_values_out,
    grad_out,
    grad_mixed,
    grad_heads,
):
    rows, width = grad_one.shape
    span = RATIO * HD
    da = grad_one[...].astype(low)
    grad_mixed[...] = matmul_right_t(da, weights[span * kv : span * kv + span, 0:width]).astype(low)
    grad_out[...] = matmul_left_t(mixed[...], da).astype(low)
    grad_keys = [None] * (rows // QUERY_ROWS)
    grad_values = [None] * (rows // QUERY_ROWS)
    for block in range(rows // QUERY_ROWS):
        at = slice(QUERY_ROWS * block, QUERY_ROWS * (block + 1))
        reach = QUERY_ROWS * (block + 1)
        stacked = jnp.concatenate([query[RATIO * kv + i, at] for i in range(RATIO)], axis=0)
        grads = jnp.concatenate([grad_mixed[at, HD * i : HD * i + HD] for i in range(RATIO)], axis=0)
        out = jnp.concatenate([mixed[at, HD * i : HD * i + HD] for i in range(RATIO)], axis=0)
        delta = jnp.sum(grads.astype(f32) * out.astype(f32), axis=-1, keepdims=True)
        scores = matmul_right_t(stacked, keys[kv, :reach]).reshape(RATIO, QUERY_ROWS, reach)
        probs = jnp.exp(scores + bias[at, :reach][None] - log_total[:, at]).reshape(-1, reach)
        grad_probs = matmul_right_t(grads, values[kv, :reach])
        grad_scores = (probs * (grad_probs - delta)).astype(low)
        grad_query = matmul(grad_scores, keys[kv, :reach])
        for i in range(RATIO):
            grad_heads[at, HD * i : HD * i + HD] = (
                grad_query[QUERY_ROWS * i : QUERY_ROWS * (i + 1)] * HD**-0.5
            )
        key_part = matmul_left_t(grad_scores, stacked)
        value_part = matmul_left_t(probs.astype(low), grads)
        for j in range(block + 1):
            at_j = slice(QUERY_ROWS * j, QUERY_ROWS * (j + 1))
            if grad_keys[j] is None:
                grad_keys[j], grad_values[j] = key_part[at_j], value_part[at_j]
            else:
                grad_keys[j] = grad_keys[j] + key_part[at_j]
                grad_values[j] = grad_values[j] + value_part[at_j]
    grad_heads[:, span : span + HD] = jnp.concatenate(grad_keys, axis=0)
    grad_values_out[...] = jnp.concatenate(grad_values, axis=0).astype(low)
    for start in range(0, span + HD, 2 * HD):
        value = grad_heads[:, start : start + 2 * HD]
        turned = value * cosine[...] - swap_halves(value) * sine[...]
        grad_turned[:, start : start + 2 * HD] = turned.astype(low)


def back_last_kernel(
    shards,
    part,
    where_ref,
    hidden_in,
    gains,
    weights,
    normed,
    grad_one,
    grad_gain_two,
    *rest,
):
    core, x, y, shard = (where_ref[i] for i in range(4))
    rows, width = hidden_in.shape
    turned, values, outs = rest[0:KV], rest[KV : 2 * KV], rest[2 * KV : 3 * KV]
    grad_tokens, keep, send, grad_low, grad_weights, sems = rest[3 * KV :]
    span = RATIO * HD
    grad_low[...] = jnp.concatenate(
        [jnp.zeros((rows, HD), low)]
        + [item[:, 0:span] for item in turned]
        + [item[:, span : span + HD] for item in turned]
        + [item[...] for item in values],
        axis=1,
    )
    normed_t = normed[...].T
    for start in range(0, 1024, 512):
        at = slice(start, start + 512)
        grad_weights[0:width, 512 + start : 1024 + start] = matmul(normed_t, grad_low[:, at]).astype(low)
    for kv in range(KV):
        grad_weights[span * kv : span * kv + span, 0:width] = outs[kv][...]
    grad_normed = matmul_right_t(grad_low[...], weights[0:width, 512:1536])
    hidden = hidden_in[...]
    grad_from, gain_row = norm_back(hidden, norm_recip(hidden), gains[0:1], grad_normed)
    grad_tokens[...] = (grad_one[...] + grad_from).astype(low).T
    row = lax.broadcasted_iota(jnp.int32, (16, width), 0)
    both = jnp.where(
        row == 0,
        jnp.broadcast_to(gain_row, (16, width)),
        jnp.where(row == 1, jnp.broadcast_to(grad_gain_two[0:1], (16, width)), 0.0),
    )
    grad_weights[width : width + 16, :] = jnp.zeros((16, grad_weights.shape[1]), low)
    grad_weights[width : width + 16, 0:width] = both.astype(low)
    copies = Copies(sems)
    for rel_core, target in enumerate((keep, send)):
        for rel_x in range(2):
            for rel_y in range(2):
                at_y = relative(y, rel_y)
                block = 2 * relative(core, rel_core) + relative(x, rel_x)
                columns = rows_at(384 * block, 384, 128)
                for step in range(shards):
                    at = shard_at(shard, step, shards)
                    piece = target.at[rel_x, rel_y, step]
                    copies.start(
                        grad_weights.at[rows_at(part * at + 80 * at_y, 64), columns],
                        piece.at[pl.ds(0, 64)],
                    )
                    last = jnp.where(at_y == 0, part * at + 64, width)
                    copies.start(grad_weights.at[rows_at(last, 16), columns], piece.at[pl.ds(64, 16)])
    copies.wait()


def finish_kernel(
    where_ref,
    pair_pieces,
    pair_other,
    rest_pieces,
    rest_other,
    out_query,
    out_key,
    out_value,
    out_out,
    out_gains,
    out_gate,
    out_up,
    out_down,
    attn,
    pair,
    down,
    sems,
):
    core, x, y = (where_ref[i] for i in range(3))
    part, width = out_out.shape
    copies = Copies(sems)
    for rel_core, (p_from, r_from) in enumerate(((pair_pieces, rest_pieces), (pair_other, rest_other))):
        for rel_x in range(2):
            for rel_y in range(2):
                at_y = relative(y, rel_y)
                block = 2 * relative(core, rel_core) + relative(x, rel_x)
                columns = rows_at(384 * block, 384, 128)
                piece = r_from.at[rel_y, rel_x]
                copies.start(p_from.at[rel_x, rel_y], pair.at[at_y, :, columns])
                copies.start(piece.at[pl.ds(0, 80)], attn.at[rows_at(80 * at_y, 80), columns])
                copies.start(piece.at[pl.ds(80, down.shape[1])], down.at[2 * block + at_y])
    copies.wait()
    kv_width = out_key.shape[1]
    out_out[...] = attn[0:part, 0:width].astype(f32)
    rest = attn[0:part, 512:].astype(f32)
    at = width - 512
    out_query[...] = rest[:, at : at + width]
    out_key[...] = rest[:, at + width : at + width + kv_width]
    out_value[...] = rest[:, at + width + kv_width :]
    out_gains[...] = attn[part : part + 16, 0:width].astype(f32)[:8]
    out_gate[...] = pair[0].astype(f32)
    out_up[...] = pair[1].astype(f32)
    half = down.shape[1] // 2
    whole = [
        jnp.concatenate([down[i, :half], down[i, half:, : width - 384]], axis=1)
        for i in range(down.shape[0])
    ]
    out_down[...] = jnp.concatenate(whole, axis=0).T.astype(f32)


VM = pl.BlockSpec(memory_space=pltpu.VMEM)
SM = pl.BlockSpec(memory_space=pltpu.SMEM)
HB = pl.BlockSpec(memory_space=pl.ANY)


def shape(sizes, kind):
    return jax.ShapeDtypeStruct(tuple(sizes), kind)


def call(kernel, name, operands, in_specs, out_shape, out_specs, scratch, micros, room):
    moved = sum(item.size * item.dtype.itemsize for item in out_shape)
    return pl.pallas_call(
        kernel,
        name=name,
        in_specs=in_specs,
        out_shape=out_shape,
        out_specs=out_specs,
        scratch_shapes=scratch,
        cost_estimate=pl.CostEstimate(
            flops=int(micros * 1e7), bytes_accessed=moved, transcendentals=0
        ),
        compiler_params=pltpu.CompilerParams(vmem_limit_bytes=room << 20),
    )(*operands)


def local(
    replicas,
    shards,
    tokens,
    lengths,
    gain_attn,
    w_query,
    w_key,
    w_value,
    w_out,
    gain_mlp,
    w_gate,
    w_up,
    w_down,
    cotangent,
):
    rows, width = tokens.shape
    part = w_gate.shape[0]
    hidden_width = w_gate.shape[1]
    down_part = w_down.shape[0]
    eighth = down_part // 8
    packed = 2 * width + 2 * w_key.shape[1]
    rep_index = lax.axis_index("rep")
    shard = lax.axis_index("shard")
    core, x, y = ((rep_index >> bit) & 1 for bit in range(3))
    where = jnp.stack([core, x, y, shard]).astype(jnp.int32)

    own, mine, own_down = call(
        pack_kernel,
        "pack",
        (
            where,
            w_out,
            w_query,
            w_key,
            w_value,
            gain_attn[None],
            gain_mlp[None],
            w_gate,
            w_up,
            w_down.T,
        ),
        [SM] + [VM] * 9,
        (
            shape((part + 16, packed), low),
            shape((part + 80 + 2 * eighth, 384), low),
            shape((down_part, width), low),
        ),
        [VM] * 3,
        [],
        2,
        16,
    )
    got = [shift_from(mine, step, shards) for step in range(1, shards)]
    table_cos, table_sin = rotation_tables(rows + 8, HD)
    cosine, sine, bias, hidden_in, scaled, grad_low = call(
        prepare_kernel,
        "prepare",
        (lengths, tokens.T, cotangent.T, table_cos, table_sin),
        [SM] + [VM] * 4,
        (
            shape((rows, 2 * HD), f32),
            shape((rows, 2 * HD), f32),
            shape((rows, rows), f32),
            shape((rows, width), f32),
            shape((rows, width), f32),
            shape((rows, width), low),
        ),
        [VM] * 6,
        [],
        5,
        24,
    )
    got[0] = after(got[0], scaled)
    attn_got = jnp.stack([item[part : part + 80] for item in got])
    pair_got = jnp.stack([item[:part] for item in got])
    down_got = unfold(jnp.stack([item[part + 80 :] for item in got]), width)
    pair_got = gather_bit(pair_got, 2, replicas)
    down_got = gather_bit(down_got, 1, replicas)
    attn_got = gather_bit(gather_bit(attn_got, 1, replicas), 2, replicas)
    attn_got = after(attn_got, pair_got, down_got)
    attn_other = flip(attn_got, 0, replicas)
    pair_got = gather_bit(after(pair_got, attn_other), 1, replicas)
    down_got = gather_bit(after(down_got, attn_other), 2, replicas)

    weights, gains, normed, query, keys, values = call(
        functools.partial(project_kernel, shards, part),
        "project",
        (where, scaled, cosine, sine, own, attn_got, attn_other),
        [SM, VM, VM, VM, HB, HB, HB],
        (
            shape((width + 16 * shards, packed), low),
            shape((8, width), f32),
            shape((rows, width), low),
            shape((HEADS, rows, HD), low),
            shape((KV, rows, HD), low),
            shape((KV, rows, HD), low),
        ),
        [VM] * 6,
        [pltpu.SemaphoreType.DMA((2 + 16 * (shards - 1),))],
        5,
        24,
    )
    mixed, log_total = [], []
    for kv in range(KV):
        outs = [shape((rows, RATIO * HD), low), shape((RATIO, rows, 1), f32)]
        operands = (bias, query, keys, values)
        if kv < KV - 1:
            one, two = call(
                functools.partial(attend_kernel, kv),
                f"attend_{kv}",
                operands,
                [VM] * 4,
                outs,
                [VM] * 2,
                [],
                3,
                24,
            )
        else:
            operands += (after(hidden_in, down_got), gains, weights, *mixed)
            one, two, hidden_one, normed_two = call(
                functools.partial(attend_last_kernel, kv),
                f"attend_{kv}",
                operands,
                [VM] * len(operands),
                outs + [shape((rows, width), f32), shape((rows, width), low)],
                [VM] * 4,
                [],
                4,
                24,
            )
        mixed.append(one)
        log_total.append(two)
    pair_other = flip(after(pair_got, normed_two), 0, replicas)
    down_other = flip(after(down_got, normed_two), 0, replicas)
    pair_shape = shape((2, 2, shards, part, 384), low)
    down_shape = shape((2, 2, shards, eighth, width), low)
    result, grad_one, grad_gain_two, pair_keep, pair_send, down_keep, down_send = call(
        functools.partial(feed_kernel, shards, part),
        "feed",
        (
            where,
            hidden_one,
            normed_two,
            gains,
            lengths,
            grad_low,
            w_gate,
            w_up,
            own_down,
            pair_got,
            pair_other,
            down_got,
            down_other,
        ),
        [SM] + [VM] * 3 + [SM, VM] + [HB] * 7,
        (
            shape((width, rows), low),
            shape((rows, width), f32),
            shape((8, width), f32),
            pair_shape,
            pair_shape,
            down_shape,
            down_shape,
        ),
        [VM] * 3 + [HB] * 4,
        [
            pltpu.VMEM((2, shards * part, hidden_width), low),
            pltpu.VMEM((hidden_width, width), low),
            pltpu.VMEM((rows, hidden_width), low),
            pltpu.VMEM((rows, hidden_width), low),
            pltpu.VMEM((rows, hidden_width), low),
            pltpu.VMEM((2, shards * part, hidden_width), low),
            pltpu.VMEM((hidden_width, width), low),
            pltpu.SemaphoreType.DMA((16 * shards + 3,)),
        ],
        19,
        48,
    )
    pair_sent = flip(pair_send, 0, replicas)
    down_sent = flip(down_send, 0, replicas)
    grad_turned, grad_values, grad_out = [], [], []
    for kv in range(KV):
        if kv == 1:
            pair_left = halve(pair_keep, after(pair_sent, grad_turned[0]), 1, replicas)
            down_left = halve(down_keep, after(down_sent, grad_turned[0]), 2, replicas)
            grad_one = after(grad_one, pair_sent, down_sent)
        one, two, three = call(
            functools.partial(back_heads_kernel, kv),
            f"back_{kv}",
            (bias, cosine, sine, weights, query, keys, values, mixed[kv], log_total[kv], grad_one),
            [VM] * 10,
            (
                shape((rows, RATIO * HD + HD), low),
                shape((rows, HD), low),
                shape((RATIO * HD, width), low),
            ),
            [VM] * 3,
            [pltpu.VMEM((rows, RATIO * HD), low), pltpu.VMEM((rows, RATIO * HD + HD), f32)],
            5,
            24,
        )
        grad_turned.append(one)
        grad_values.append(two)
        grad_out.append(three)
    grad_one = after(grad_one, down_left[1])
    attn_shape = shape((2, 2, shards, 80, 384), low)
    grad_tokens, attn_keep, attn_send = call(
        functools.partial(back_last_kernel, shards, part),
        "back_last",
        (
            where,
            hidden_in,
            gains,
            weights,
            normed,
            grad_one,
            grad_gain_two,
            *grad_turned,
            *grad_values,
            *grad_out,
        ),
        [SM] + [VM] * (6 + 3 * KV),
        (shape((width, rows), low), attn_shape, attn_shape),
        [VM, HB, HB],
        [
            pltpu.VMEM((rows, 1024), low),
            pltpu.VMEM((width + 16, packed), low),
            pltpu.SemaphoreType.DMA((16 * shards,)),
        ],
        6,
        24,
    )
    attn_left = halve(attn_keep, flip(attn_send, 0, replicas), 1, replicas)
    pair_left = halve(*pair_left, 2, replicas)
    down_left = halve(down_left[0], after(down_left[1], grad_tokens), 1, replicas)
    attn_left = halve(*attn_left, 2, replicas)
    feed_left = tuple(
        jnp.concatenate([one, fold(two)], axis=1) for one, two in zip(pair_left, down_left)
    )
    feed_total = scatter_over_shards(*feed_left, shards, replicas)
    attn_total = scatter_over_shards(*attn_left, shards, replicas)
    pair_pieces = spread(feed_total[:part], (2, 1, 0), replicas)
    rest_pieces = spread(jnp.concatenate([attn_total, feed_total[part:]]), (1, 2, 0), replicas)
    g_query, g_key, g_value, g_out, g_gains, g_gate, g_up, g_down = call(
        finish_kernel,
        "finish",
        (where, *pair_pieces, *rest_pieces),
        [SM] + [HB] * 4,
        (
            shape(w_query.shape, f32),
            shape(w_key.shape, f32),
            shape(w_value.shape, f32),
            shape(w_out.shape, f32),
            shape((8, width), f32),
            shape(w_gate.shape, f32),
            shape(w_up.shape, f32),
            shape((width, down_part), f32),
        ),
        [VM] * 8,
        [
            pltpu.VMEM((160, packed), low),
            pltpu.VMEM((2, part, hidden_width), low),
            pltpu.VMEM((8, 2 * eighth, 384), low),
            pltpu.SemaphoreType.DMA((24,)),
        ],
        5,
        24,
    )
    g_gains = lax.dynamic_slice(g_gains, (0, part * shard), (2, part))
    return (
        result.T,
        grad_tokens.T,
        g_gains[0],
        g_query,
        g_key,
        g_value,
        g_out,
        g_gains[1],
        g_gate,
        g_up,
        g_down.T,
    )


def solution(mesh):
    in_specs = (
        P(("rep", "shard"), None),
        P(("rep", "shard"), None),
        P("shard"),
        P("shard", None),
        P("shard", None),
        P("shard", None),
        P("shard", None),
        P("shard"),
        P("shard", None),
        P("shard", None),
        P("shard", None),
        P(("rep", "shard"), None),
    )
    out_specs = (
        P(("rep", "shard"), None),
        P(("rep", "shard"), None),
        P("shard"),
        P("shard", None),
        P("shard", None),
        P("shard", None),
        P("shard", None),
        P("shard"),
        P("shard", None),
        P("shard", None),
        P("shard", None),
    )
    part = functools.partial(local, mesh.shape["rep"], mesh.shape["shard"])
    return jax.shard_map(part, mesh=mesh, in_specs=in_specs, out_specs=out_specs, check_vma=False)
```

```python
import functools

import jax
import jax.numpy as jnp
from jax import lax
from jax.experimental import pallas as pl
from jax.experimental.pallas import tpu as pltpu
from jax.sharding import PartitionSpec as P
import numpy as np

HEADS = 9
KV = 3
HD = 64
RATIO = HEADS // KV


norm_eps = 1e-05
rope_base = 100000.0
neg_fill = -1e30

low = jnp.bfloat16
f32 = jnp.float32
QUERY_ROWS = 128


def rotation_tables(places, head_size):
    half = head_size // 2
    freq = np.float32(rope_base) ** (-(np.arange(half, dtype=np.float32) * np.float32(2.0) / head_size))
    angle = np.arange(places, dtype=np.float32)[:, None] * freq.astype(np.float32)[None, :]
    return np.concatenate([np.cos(angle)] * 4, axis=1), np.concatenate([np.sin(angle)] * 4, axis=1)


def matmul(left, right):
    return jnp.dot(left, right, preferred_element_type=f32)


def matmul_left_t(left, right):
    return lax.dot_general(left, right, (((0,), (0,)), ((), ())), preferred_element_type=f32)


def matmul_right_t(left, right):
    return lax.dot_general(left, right, (((1,), (1,)), ((), ())), preferred_element_type=f32)


def flip(value, bit, replicas):
    return lax.ppermute(value, "rep", [(i, i ^ (1 << bit)) for i in range(replicas)])


def shift_from(value, step, shards):
    return lax.ppermute(value, "shard", [((s + step) % shards, s) for s in range(shards)])


def shift_to(value, step, shards):
    return lax.ppermute(value, "shard", [(s, (s + step) % shards) for s in range(shards)])


def add_low(left, right):
    return (left.astype(f32) + right.astype(f32)).astype(low)


def after(value, *others):
    return lax.optimization_barrier((value, *others))[0]


def gather_shards(mine, shards):
    return jnp.stack([shift_from(mine, step, shards) for step in range(1, shards)])


def gather_bit(got, bit, replicas, *later):
    other = flip(got, bit, replicas)
    return jnp.stack([after(got, *later) if later else got, other])


def halve(keep, other, bit, replicas):
    sent = flip(add_low(keep[1], other[1]), bit, replicas)
    return add_low(keep[0], other[0]), sent


def scatter_over_shards(keep, other, shards, replicas):
    parts = [add_low(keep[step], other[step]) for step in range(1, shards)]
    moved = [shift_to(part, step + 1, shards) for step, part in enumerate(parts)]
    total = keep[0].astype(f32) + other[0].astype(f32)
    for part in moved:
        total = total + part.astype(f32)
    total = total.astype(low)
    bit = 3
    while (1 << bit) < replicas:
        total = add_low(total, flip(total, bit, replicas))
        bit += 1
    return total


def spread(total, order, replicas):
    for bit in order[:-1]:
        total = jnp.stack([total, flip(total, bit, replicas)])
    return total, flip(total, order[-1], replicas)


class Copies:
    def __init__(self, sems):
        self.sems = sems
        self.made = []

    def start(self, source, target):
        copy = pltpu.make_async_copy(source, target, self.sems.at[len(self.made)])
        copy.start()
        self.made.append(copy)

    def wait(self, first=0, last=None):
        for copy in self.made[first:last]:
            copy.wait()


def rows_at(start, count, unit=16):
    return pl.ds(pl.multiple_of(start, unit), count)


def relative(bit, rel):
    return 1 - bit if rel else bit


def shard_at(shard, step, shards):
    at = shard + step
    return jnp.where(at >= shards, at - shards, at)


def swap_halves(values):
    lane = lax.broadcasted_iota(jnp.int32, values.shape, 1)
    return jnp.where(
        lane % HD < HD // 2,
        pltpu.roll(values, 2 * HD - HD // 2, 1),
        pltpu.roll(values, HD // 2, 1),
    )


def norm_recip(values):
    return lax.rsqrt(jnp.mean(values * values, axis=-1, keepdims=True) + norm_eps)


def norm_back(values, recip, gain, grad_normed):
    scaled = grad_normed * gain
    inner = jnp.mean(scaled * values, axis=-1, keepdims=True)
    grad_values = recip * scaled - values * (recip * recip * recip * inner)
    grad_gain = jnp.sum(grad_normed * values * recip, axis=0, keepdims=True)
    return (grad_values, grad_gain)


def pack_kernel(
    where_ref,
    w_out,
    w_query,
    w_key,
    w_value,
    both_gains,
    gate,
    up,
    down_t,
    own,
    attn_mine,
    pair_mine,
    down_mine,
    down,
):
    core, x, y, shard = (where_ref[i] for i in range(4))
    block = 2 * core + x
    part = gate.shape[0]
    packed = own.shape[1]
    columns = rows_at(384 * block, 384, 128)
    pair_mine[...] = jnp.where(y == 0, gate[:, columns], up[:, columns])
    own[0:part] = jnp.concatenate([w_out[...], w_query[...], w_key[...], w_value[...]], axis=1)
    row = lax.broadcasted_iota(jnp.int32, (16, part), 0)
    gains = jnp.where(
        row == 0,
        jnp.broadcast_to(both_gains[0:1].astype(f32), row.shape),
        jnp.where(row == 1, jnp.broadcast_to(both_gains[1:2].astype(f32), row.shape), 0.0),
    )
    gains = jnp.concatenate([gains, jnp.zeros((16, packed - part), f32)], axis=1)
    own[part : part + 16] = pltpu.roll(gains, part * shard, 1).astype(low)
    attn_mine[...] = own[rows_at(80 * y, 80), columns]
    down[...] = down_t[...].T
    eighth = down_mine.shape[0]
    down_mine[...] = down[rows_at(eighth * (2 * block + y), eighth), :]


def fold(value):
    rest = value[..., 384:]
    pad = [(0, 0)] * (value.ndim - 1) + [(0, 384 - rest.shape[-1])]
    return jnp.concatenate([value[..., :384], jnp.pad(rest, pad)], axis=-2)


def unfold(value, width):
    half = value.shape[-2] // 2
    return jnp.concatenate([value[..., :half, :], value[..., half:, : width - 384]], axis=-1)


def prepare_kernel(
    lengths,
    tokens_t,
    cotangent_t,
    table_cos,
    table_sin,
    cosine,
    sine,
    bias,
    hidden,
    scaled,
    grad_low,
):
    rows = hidden.shape[0]
    count = lengths.shape[1]
    ends = []
    for i in range(count):
        ends.append(lengths[0, i] + (ends[-1] if ends else 0))
    place = lax.broadcasted_iota(jnp.int32, cosine.shape, 0)
    start_cos = jnp.broadcast_to(table_cos[0:1], cosine.shape)
    start_sin = jnp.broadcast_to(table_sin[0:1], cosine.shape)
    for end in ends:
        start_cos = jnp.where(place >= end, table_cos[pl.ds(end, 1)], start_cos)
        start_sin = jnp.where(place >= end, table_sin[pl.ds(end, 1)], start_sin)
    cos, sin = table_cos[0:rows], table_sin[0:rows]
    cosine[...] = cos * start_cos + sin * start_sin
    signed = sin * start_cos - cos * start_sin
    lane = lax.broadcasted_iota(jnp.int32, cosine.shape, 1)
    sine[...] = jnp.where(lane % HD < HD // 2, -signed, signed)
    query = lax.broadcasted_iota(jnp.int32, bias.shape, 0)
    key = lax.broadcasted_iota(jnp.int32, bias.shape, 1)
    allowed = query >= key
    for end in ends:
        allowed = allowed & ((query < end) | (key >= end))
    bias[...] = jnp.where(allowed, 0.0, neg_fill)
    values = tokens_t[...].T.astype(f32)
    hidden[...] = values
    scaled[...] = values * norm_recip(values)
    wide = lax.broadcasted_iota(jnp.int32, grad_low.shape, 0)
    grad_low[...] = jnp.where(wide < ends[-1], cotangent_t[...].T, jnp.zeros((), low))


def project_kernel(
    shards,
    part,
    where_ref,
    scaled,
    cosine,
    sine,
    own,
    pieces,
    other,
    weights,
    gains,
    normed,
    query,
    keys,
    values,
    sems,
):
    core, x, y, shard = (where_ref[i] for i in range(4))
    width = scaled.shape[1]
    copies = Copies(sems)
    copies.start(own.at[pl.ds(0, part)], weights.at[rows_at(part * shard, part)])
    copies.start(own.at[pl.ds(part, 16)], weights.at[rows_at(width + 16 * shard, 16)])
    for rel_core, source in enumerate((pieces, other)):
        for rel_x in range(2):
            for rel_y in range(2):
                at_y = relative(y, rel_y)
                block = 2 * relative(core, rel_core) + relative(x, rel_x)
                columns = rows_at(384 * block, 384, 128)
                for step in range(1, shards):
                    at = shard_at(shard, step, shards)
                    piece = source.at[rel_x, rel_y, step - 1]
                    copies.start(
                        piece.at[pl.ds(0, 64)], weights.at[rows_at(part * at + 80 * at_y, 64), columns]
                    )
                    last = jnp.where(at_y == 0, part * at + 64, width + 16 * at)
                    copies.start(piece.at[pl.ds(64, 16)], weights.at[rows_at(last, 16), columns])
    copies.wait()
    total = sum(
        weights[width + 16 * s : width + 16 * s + 16, :width].astype(f32) for s in range(shards)
    )
    gains[...] = total[:8]
    n1 = (scaled[...] * total[0:1]).astype(low)
    normed[...] = n1
    for block in range(8):
        start = 512 + 128 * block
        result = matmul(n1, weights[0:width, start : start + 128])
        heads = [2 * block - 1, 2 * block]
        if heads[0] < HEADS + KV:
            turned = result * cosine[...] + swap_halves(result) * sine[...]
        for side, head in enumerate(heads):
            lanes = slice(HD * side, HD * side + HD)
            if head < 0:
                continue
            if head < HEADS:
                query[head] = (turned[:, lanes] * HD**-0.5).astype(low)
            elif head < HEADS + KV:
                keys[head - HEADS] = turned[:, lanes].astype(low)
            else:
                values[head - HEADS - KV] = result[:, lanes].astype(low)


def attend_kernel(kv, bias, query, keys, values, mixed, log_total):
    rows = bias.shape[0]
    for block in range(rows // QUERY_ROWS):
        at = slice(QUERY_ROWS * block, QUERY_ROWS * (block + 1))
        reach = QUERY_ROWS * (block + 1)
        stacked = jnp.concatenate([query[RATIO * kv + i, at] for i in range(RATIO)], axis=0)
        scores = matmul_right_t(stacked, keys[kv, :reach])
        logits = scores.reshape(RATIO, QUERY_ROWS, reach) + bias[at, :reach][None]
        top = jnp.max(logits, axis=-1, keepdims=True)
        expo = jnp.exp(logits - top)
        total = jnp.sum(expo, axis=-1, keepdims=True)
        probs = (expo * (1.0 / total)).astype(low).reshape(RATIO * QUERY_ROWS, reach)
        log_total[:, at] = top + jnp.log(total)
        result = matmul(probs, values[kv, :reach]).astype(low)
        for i in range(RATIO):
            mixed[at, HD * i : HD * i + HD] = result[QUERY_ROWS * i : QUERY_ROWS * (i + 1)]


def attend_last_kernel(
    kv,
    bias,
    query,
    keys,
    values,
    hidden_in,
    gains,
    weights,
    *rest,
):
    before, (mixed, log_total, hidden_one, normed_two) = rest[:kv], rest[kv:]
    attend_kernel(kv, bias, query, keys, values, mixed, log_total)
    width = hidden_in.shape[1]
    every = jnp.concatenate([item[...] for item in before] + [mixed[...]], axis=1)
    hidden = hidden_in[...] + matmul(every, weights[0:width, 0:width])
    hidden_one[...] = hidden
    normed_two[...] = (hidden * norm_recip(hidden) * gains[1:2]).astype(low)


def feed_kernel(
    shards,
    part,
    where_ref,
    hidden_one,
    normed_two,
    gains,
    lengths,
    cotangent,
    own_gate,
    own_up,
    own_down,
    pair_pieces,
    pair_other,
    down_pieces,
    down_other,
    result,
    grad_one,
    grad_gain,
    pair_keep,
    pair_send,
    down_keep,
    down_send,
    pair,
    down,
    hidden,
    grad_gate,
    grad_up,
    grad_pair,
    grad_down,
    sems,
):
    core, x, y, shard = (where_ref[i] for i in range(4))
    width = hidden_one.shape[1]
    down_part = own_down.shape[0]
    eighth = down_part // 8
    copies = Copies(sems)
    copies.start(own_gate, pair.at[0, rows_at(part * shard, part)])
    copies.start(own_up, pair.at[1, rows_at(part * shard, part)])
    for rel_core, source in enumerate((pair_pieces, pair_other)):
        for rel_x in range(2):
            block = 2 * relative(core, rel_core) + relative(x, rel_x)
            columns = rows_at(384 * block, 384, 128)
            for rel_y in range(2):
                at_y = relative(y, rel_y)
                for step in range(1, shards):
                    at = shard_at(shard, step, shards)
                    copies.start(
                        source.at[rel_x, rel_y, step - 1],
                        pair.at[at_y, rows_at(part * at, part), columns],
                    )
    first = len(copies.made)
    copies.start(own_down, down.at[rows_at(down_part * shard, down_part)])
    for rel_core, source in enumerate((down_pieces, down_other)):
        for rel_x in range(2):
            block = 2 * relative(core, rel_core) + relative(x, rel_x)
            for rel_y in range(2):
                place = eighth * (2 * block + relative(y, rel_y))
                for step in range(1, shards):
                    at = shard_at(shard, step, shards)
                    copies.start(
                        source.at[rel_y, rel_x, step - 1],
                        down.at[rows_at(down_part * at + place, eighth)],
                    )
    grad_low = cotangent[...]
    n2 = normed_two[...]
    copies.wait(0, first)
    hidden_width = pair.shape[2]
    for start in range(0, hidden_width, 512):
        at = slice(start, start + 512)
        gate = matmul(n2, pair[0, :, at])
        upward = matmul(n2, pair[1, :, at])
        if start == 0:
            copies.wait(first)
        grad_hidden = matmul_right_t(grad_low, down[at, :])
        sigma = jax.nn.sigmoid(gate)
        active = gate * sigma
        hidden[:, at] = (active * upward).astype(low)
        grad_up[:, at] = (grad_hidden * active).astype(low)
        grad_gate[:, at] = (grad_hidden * upward * (sigma + active * (1.0 - sigma))).astype(low)
    turned = n2.T
    sent = Copies(sems)
    for unit, grads in enumerate((grad_gate, grad_up)):
        for start in range(0, hidden_width, 512):
            at = slice(start, start + 512)
            grad_pair[unit, :, at] = matmul(turned, grads[:, at]).astype(low)
    for start in range(0, hidden_width, 512):
        at = slice(start, start + 512)
        grad_down[at, :] = matmul_left_t(hidden[:, at], grad_low).astype(low)
    for rel_core, (target, down_target) in enumerate(((pair_keep, down_keep), (pair_send, down_send))):
        at_core = relative(core, rel_core)
        for rel_x in range(2):
            at_x = relative(x, rel_x)
            block = 2 * at_core + at_x
            columns = rows_at(384 * block, 384, 128)
            for rel_y in range(2):
                at_y = relative(y, rel_y)
                for step in range(shards):
                    at = shard_at(shard, step, shards)
                    sent.start(
                        grad_pair.at[at_y, rows_at(part * at, part), columns],
                        target.at[rel_x, rel_y, step],
                    )
                    sent.start(
                        grad_down.at[rows_at(down_part * at + eighth * (2 * block + at_y), eighth)],
                        down_target.at[rel_y, rel_x, step],
                    )
    h1 = hidden_one[...]
    total = lengths[0, 0]
    for i in range(1, lengths.shape[1]):
        total = total + lengths[0, i]
    row = lax.broadcasted_iota(jnp.int32, h1.shape, 0)
    summed = h1 + matmul(hidden[...], down[...])
    result[...] = jnp.where(row < total, summed, 0.0).astype(low).T
    grad_normed = matmul_right_t(grad_gate[...], pair[0]) + matmul_right_t(grad_up[...], pair[1])
    grad_from, gain_row = norm_back(h1, norm_recip(h1), gains[1:2], grad_normed)
    grad_one[...] = grad_low.astype(f32) + grad_from
    grad_gain[...] = jnp.broadcast_to(gain_row, grad_gain.shape)
    sent.wait()


def back_heads_kernel(
    kv,
    bias,
    cosine,
    sine,
    weights,
    query,
    keys,
    values,
    mixed,
    log_total,
    grad_one,
    grad_turned,
    grad_values_out,
    grad_out,
    grad_mixed,
    grad_heads,
):
    rows, width = grad_one.shape
    span = RATIO * HD
    da = grad_one[...].astype(low)
    grad_mixed[...] = matmul_right_t(da, weights[span * kv : span * kv + span, 0:width]).astype(low)
    grad_out[...] = matmul_left_t(mixed[...], da).astype(low)
    grad_keys = [None] * (rows // QUERY_ROWS)
    grad_values = [None] * (rows // QUERY_ROWS)
    for block in range(rows // QUERY_ROWS):
        at = slice(QUERY_ROWS * block, QUERY_ROWS * (block + 1))
        reach = QUERY_ROWS * (block + 1)
        stacked = jnp.concatenate([query[RATIO * kv + i, at] for i in range(RATIO)], axis=0)
        grads = jnp.concatenate([grad_mixed[at, HD * i : HD * i + HD] for i in range(RATIO)], axis=0)
        out = jnp.concatenate([mixed[at, HD * i : HD * i + HD] for i in range(RATIO)], axis=0)
        delta = jnp.sum(grads.astype(f32) * out.astype(f32), axis=-1, keepdims=True)
        scores = matmul_right_t(stacked, keys[kv, :reach]).reshape(RATIO, QUERY_ROWS, reach)
        probs = jnp.exp(scores + bias[at, :reach][None] - log_total[:, at]).reshape(-1, reach)
        grad_probs = matmul_right_t(grads, values[kv, :reach])
        grad_scores = (probs * (grad_probs - delta)).astype(low)
        grad_query = matmul(grad_scores, keys[kv, :reach])
        for i in range(RATIO):
            grad_heads[at, HD * i : HD * i + HD] = (
                grad_query[QUERY_ROWS * i : QUERY_ROWS * (i + 1)] * HD**-0.5
            )
        key_part = matmul_left_t(grad_scores, stacked)
        value_part = matmul_left_t(probs.astype(low), grads)
        for j in range(block + 1):
            at_j = slice(QUERY_ROWS * j, QUERY_ROWS * (j + 1))
            if grad_keys[j] is None:
                grad_keys[j], grad_values[j] = key_part[at_j], value_part[at_j]
            else:
                grad_keys[j] = grad_keys[j] + key_part[at_j]
                grad_values[j] = grad_values[j] + value_part[at_j]
    grad_heads[:, span : span + HD] = jnp.concatenate(grad_keys, axis=0)
    grad_values_out[...] = jnp.concatenate(grad_values, axis=0).astype(low)
    for start in range(0, span + HD, 2 * HD):
        value = grad_heads[:, start : start + 2 * HD]
        turned = value * cosine[...] - swap_halves(value) * sine[...]
        grad_turned[:, start : start + 2 * HD] = turned.astype(low)


def back_last_kernel(
    shards,
    part,
    where_ref,
    hidden_in,
    gains,
    weights,
    normed,
    grad_one,
    grad_gain_two,
    *rest,
):
    core, x, y, shard = (where_ref[i] for i in range(4))
    rows, width = hidden_in.shape
    turned, values, outs = rest[0:KV], rest[KV : 2 * KV], rest[2 * KV : 3 * KV]
    grad_tokens, keep, send, grad_low, grad_weights, sems = rest[3 * KV :]
    span = RATIO * HD
    grad_low[...] = jnp.concatenate(
        [jnp.zeros((rows, HD), low)]
        + [item[:, 0:span] for item in turned]
        + [item[:, span : span + HD] for item in turned]
        + [item[...] for item in values],
        axis=1,
    )
    normed_t = normed[...].T
    for start in range(0, 1024, 512):
        at = slice(start, start + 512)
        grad_weights[0:width, 512 + start : 1024 + start] = matmul(normed_t, grad_low[:, at]).astype(low)
    for kv in range(KV):
        grad_weights[span * kv : span * kv + span, 0:width] = outs[kv][...]
    grad_normed = matmul_right_t(grad_low[...], weights[0:width, 512:1536])
    hidden = hidden_in[...]
    grad_from, gain_row = norm_back(hidden, norm_recip(hidden), gains[0:1], grad_normed)
    grad_tokens[...] = (grad_one[...] + grad_from).astype(low).T
    row = lax.broadcasted_iota(jnp.int32, (16, width), 0)
    both = jnp.where(
        row == 0,
        jnp.broadcast_to(gain_row, (16, width)),
        jnp.where(row == 1, jnp.broadcast_to(grad_gain_two[0:1], (16, width)), 0.0),
    )
    grad_weights[width : width + 16, :] = jnp.zeros((16, grad_weights.shape[1]), low)
    grad_weights[width : width + 16, 0:width] = both.astype(low)
    copies = Copies(sems)
    for rel_core, target in enumerate((keep, send)):
        for rel_x in range(2):
            for rel_y in range(2):
                at_y = relative(y, rel_y)
                block = 2 * relative(core, rel_core) + relative(x, rel_x)
                columns = rows_at(384 * block, 384, 128)
                for step in range(shards):
                    at = shard_at(shard, step, shards)
                    piece = target.at[rel_x, rel_y, step]
                    copies.start(
                        grad_weights.at[rows_at(part * at + 80 * at_y, 64), columns],
                        piece.at[pl.ds(0, 64)],
                    )
                    last = jnp.where(at_y == 0, part * at + 64, width)
                    copies.start(grad_weights.at[rows_at(last, 16), columns], piece.at[pl.ds(64, 16)])
    copies.wait()


def finish_kernel(
    where_ref,
    pair_pieces,
    pair_other,
    rest_pieces,
    rest_other,
    out_query,
    out_key,
    out_value,
    out_out,
    out_gains,
    out_gate,
    out_up,
    out_down,
    attn,
    pair,
    down,
    sems,
):
    core, x, y = (where_ref[i] for i in range(3))
    part, width = out_out.shape
    copies = Copies(sems)
    for rel_core, (p_from, r_from) in enumerate(((pair_pieces, rest_pieces), (pair_other, rest_other))):
        for rel_x in range(2):
            for rel_y in range(2):
                at_y = relative(y, rel_y)
                block = 2 * relative(core, rel_core) + relative(x, rel_x)
                columns = rows_at(384 * block, 384, 128)
                piece = r_from.at[rel_y, rel_x]
                copies.start(p_from.at[rel_x, rel_y], pair.at[at_y, :, columns])
                copies.start(piece.at[pl.ds(0, 80)], attn.at[rows_at(80 * at_y, 80), columns])
                copies.start(piece.at[pl.ds(80, down.shape[1])], down.at[2 * block + at_y])
    copies.wait()
    kv_width = out_key.shape[1]
    out_out[...] = attn[0:part, 0:width].astype(f32)
    rest = attn[0:part, 512:].astype(f32)
    at = width - 512
    out_query[...] = rest[:, at : at + width]
    out_key[...] = rest[:, at + width : at + width + kv_width]
    out_value[...] = rest[:, at + width + kv_width :]
    out_gains[...] = attn[part : part + 16, 0:width].astype(f32)[:8]
    out_gate[...] = pair[0].astype(f32)
    out_up[...] = pair[1].astype(f32)
    half = down.shape[1] // 2
    whole = [
        jnp.concatenate([down[i, :half], down[i, half:, : width - 384]], axis=1)
        for i in range(down.shape[0])
    ]
    out_down[...] = jnp.concatenate(whole, axis=0).T.astype(f32)


VM = pl.BlockSpec(memory_space=pltpu.VMEM)
SM = pl.BlockSpec(memory_space=pltpu.SMEM)
HB = pl.BlockSpec(memory_space=pl.ANY)


def shape(sizes, kind):
    return jax.ShapeDtypeStruct(tuple(sizes), kind)


def call(kernel, name, operands, in_specs, out_shape, out_specs, scratch, micros, room):
    moved = sum(item.size * item.dtype.itemsize for item in out_shape)
    return pl.pallas_call(
        kernel,
        name=name,
        in_specs=in_specs,
        out_shape=out_shape,
        out_specs=out_specs,
        scratch_shapes=scratch,
        cost_estimate=pl.CostEstimate(
            flops=int(micros * 1e7), bytes_accessed=moved, transcendentals=0
        ),
        compiler_params=pltpu.CompilerParams(vmem_limit_bytes=room << 20),
    )(*operands)


def local(
    replicas,
    shards,
    tokens,
    lengths,
    gain_attn,
    w_query,
    w_key,
    w_value,
    w_out,
    gain_mlp,
    w_gate,
    w_up,
    w_down,
    cotangent,
):
    rows, width = tokens.shape
    part = w_gate.shape[0]
    hidden_width = w_gate.shape[1]
    down_part = w_down.shape[0]
    eighth = down_part // 8
    packed = 2 * width + 2 * w_key.shape[1]
    rep_index = lax.axis_index("rep")
    shard = lax.axis_index("shard")
    core, x, y = ((rep_index >> bit) & 1 for bit in range(3))
    where = jnp.stack([core, x, y, shard]).astype(jnp.int32)

    own, attn_mine, pair_mine, down_mine, own_down = call(
        pack_kernel,
        "pack",
        (
            where,
            w_out,
            w_query,
            w_key,
            w_value,
            jnp.stack([gain_attn, gain_mlp]),
            w_gate,
            w_up,
            w_down.T,
        ),
        [SM] + [VM] * 8,
        (
            shape((part + 16, packed), low),
            shape((80, 384), low),
            shape((part, 384), low),
            shape((eighth, width), low),
            shape((down_part, width), low),
        ),
        [VM] * 5,
        [],
        2,
        60,
    )
    attn_got = gather_shards(attn_mine, shards)
    table_cos, table_sin = rotation_tables(rows + 8, HD)
    cosine, sine, bias, hidden_in, scaled, grad_low = call(
        prepare_kernel,
        "prepare",
        (lengths, tokens.T, cotangent.T, table_cos, table_sin),
        [SM] + [VM] * 4,
        (
            shape((rows, 2 * HD), f32),
            shape((rows, 2 * HD), f32),
            shape((rows, rows), f32),
            shape((rows, width), f32),
            shape((rows, width), f32),
            shape((rows, width), low),
        ),
        [VM] * 6,
        [],
        5,
        60,
    )
    pair_got = gather_shards(after(pair_mine, scaled), shards)
    down_got = gather_shards(after(down_mine, attn_got), shards)
    attn_got = gather_bit(after(attn_got, scaled), 2, replicas)
    attn_got = gather_bit(after(attn_got, pair_got), 1, replicas)
    attn_other = flip(attn_got, 0, replicas)
    pair_got = gather_bit(pair_got, 2, replicas)
    scaled = after(scaled, down_got)
    weights, gains, normed, query, keys, values = call(
        functools.partial(project_kernel, shards, part),
        "project",
        (where, scaled, cosine, sine, own, attn_got, attn_other),
        [SM, VM, VM, VM, HB, HB, HB],
        (
            shape((width + 16 * shards, packed), low),
            shape((8, width), f32),
            shape((rows, width), low),
            shape((HEADS, rows, HD), low),
            shape((KV, rows, HD), low),
            shape((KV, rows, HD), low),
        ),
        [VM] * 6,
        [pltpu.SemaphoreType.DMA((2 + 16 * (shards - 1),))],
        5,
        24,
    )
    keys = after(keys, pair_got)
    down_got = gather_bit(down_got, 1, replicas, normed)
    mixed, log_total = [], []
    for kv in range(KV):
        outs = [shape((rows, RATIO * HD), low), shape((RATIO, rows, 1), f32)]
        operands = (bias, query, keys, values)
        if kv < KV - 1:
            one, two = call(
                functools.partial(attend_kernel, kv),
                f"attend_{kv}",
                operands,
                [VM] * 4,
                outs,
                [VM] * 2,
                [],
                3,
                24,
            )
        else:
            down_got = gather_bit(down_got, 2, replicas, *mixed)
            operands += (after(hidden_in, down_got), gains, weights, *mixed)
            one, two, hidden_one, normed_two = call(
                functools.partial(attend_last_kernel, kv),
                f"attend_{kv}",
                operands,
                [VM] * len(operands),
                outs + [shape((rows, width), f32), shape((rows, width), low)],
                [VM] * 4,
                [],
                4,
                24,
            )
        mixed.append(one)
        log_total.append(two)
    pair_got = gather_bit(pair_got, 1, replicas, normed_two)
    pair_other = flip(pair_got, 0, replicas)
    down_other = flip(down_got, 0, replicas)
    pair_shape = shape((2, 2, shards, part, 384), low)
    down_shape = shape((2, 2, shards, eighth, width), low)
    result, grad_one, grad_gain_two, pair_keep, pair_send, down_keep, down_send = call(
        functools.partial(feed_kernel, shards, part),
        "feed",
        (
            where,
            hidden_one,
            normed_two,
            gains,
            lengths,
            grad_low,
            w_gate,
            w_up,
            own_down,
            pair_got,
            pair_other,
            down_got,
            down_other,
        ),
        [SM] + [VM] * 3 + [SM, VM] + [HB] * 7,
        (
            shape((width, rows), low),
            shape((rows, width), f32),
            shape((8, width), f32),
            pair_shape,
            pair_shape,
            down_shape,
            down_shape,
        ),
        [VM] * 3 + [HB] * 4,
        [
            pltpu.VMEM((2, shards * part, hidden_width), low),
            pltpu.VMEM((hidden_width, width), low),
            pltpu.VMEM((rows, hidden_width), low),
            pltpu.VMEM((rows, hidden_width), low),
            pltpu.VMEM((rows, hidden_width), low),
            pltpu.VMEM((2, shards * part, hidden_width), low),
            pltpu.VMEM((hidden_width, width), low),
            pltpu.SemaphoreType.DMA((16 * shards + 3,)),
        ],
        19,
        60,
    )
    pair_sent = flip(pair_send, 0, replicas)
    down_sent = flip(down_send, 0, replicas)
    grad_turned, grad_values, grad_out = [], [], []
    for kv in range(KV):
        if kv == 1:
            pair_left = halve(pair_keep, after(pair_sent, grad_turned[0]), 1, replicas)
            down_left = halve(down_keep, after(down_sent, grad_turned[0]), 2, replicas)
            grad_one = after(grad_one, pair_sent, down_sent)
        one, two, three = call(
            functools.partial(back_heads_kernel, kv),
            f"back_{kv}",
            (bias, cosine, sine, weights, query, keys, values, mixed[kv], log_total[kv], grad_one),
            [VM] * 10,
            (
                shape((rows, RATIO * HD + HD), low),
                shape((rows, HD), low),
                shape((RATIO * HD, width), low),
            ),
            [VM] * 3,
            [pltpu.VMEM((rows, RATIO * HD), low), pltpu.VMEM((rows, RATIO * HD + HD), f32)],
            5,
            24,
        )
        grad_turned.append(one)
        grad_values.append(two)
        grad_out.append(three)
    attn_shape = shape((2, 2, shards, 80, 384), low)
    grad_tokens, attn_keep, attn_send = call(
        functools.partial(back_last_kernel, shards, part),
        "back_last",
        (
            where,
            hidden_in,
            gains,
            weights,
            normed,
            grad_one,
            grad_gain_two,
            *grad_turned,
            *grad_values,
            *grad_out,
        ),
        [SM] + [VM] * (6 + 3 * KV),
        (shape((width, rows), low), attn_shape, attn_shape),
        [VM, HB, HB],
        [
            pltpu.VMEM((rows, 1024), low),
            pltpu.VMEM((width + 16, packed), low),
            pltpu.SemaphoreType.DMA((16 * shards,)),
        ],
        6,
        24,
    )
    attn_left = halve(attn_keep, flip(after(attn_send, down_left[1]), 0, replicas), 1, replicas)
    pair_left = halve(*pair_left, 2, replicas)
    down_left = halve(down_left[0], after(down_left[1], grad_tokens), 1, replicas)
    attn_left = halve(*attn_left, 2, replicas)
    feed_left = tuple(
        jnp.concatenate([one, fold(two)], axis=1) for one, two in zip(pair_left, down_left)
    )
    feed_total = scatter_over_shards(*feed_left, shards, replicas)
    attn_total = scatter_over_shards(*attn_left, shards, replicas)
    pair_pieces = spread(feed_total[:part], (2, 1, 0), replicas)
    rest_pieces = spread(jnp.concatenate([attn_total, feed_total[part:]]), (1, 2, 0), replicas)
    g_query, g_key, g_value, g_out, g_gains, g_gate, g_up, g_down = call(
        finish_kernel,
        "finish",
        (where, *pair_pieces, *rest_pieces),
        [SM] + [HB] * 4,
        (
            shape(w_query.shape, f32),
            shape(w_key.shape, f32),
            shape(w_value.shape, f32),
            shape(w_out.shape, f32),
            shape((8, width), f32),
            shape(w_gate.shape, f32),
            shape(w_up.shape, f32),
            shape((width, down_part), f32),
        ),
        [VM] * 8,
        [
            pltpu.VMEM((160, packed), low),
            pltpu.VMEM((2, part, hidden_width), low),
            pltpu.VMEM((8, 2 * eighth, 384), low),
            pltpu.SemaphoreType.DMA((24,)),
        ],
        5,
        60,
    )
    g_gains = lax.dynamic_slice(g_gains, (0, part * shard), (2, part))
    return (
        result.T,
        grad_tokens.T,
        g_gains[0],
        g_query,
        g_key,
        g_value,
        g_out,
        g_gains[1],
        g_gate,
        g_up,
        g_down.T,
    )


def solution(mesh):
    in_specs = (
        P(("rep", "shard"), None),
        P(("rep", "shard"), None),
        P("shard"),
        P("shard", None),
        P("shard", None),
        P("shard", None),
        P("shard", None),
        P("shard"),
        P("shard", None),
        P("shard", None),
        P("shard", None),
        P(("rep", "shard"), None),
    )
    out_specs = (
        P(("rep", "shard"), None),
        P(("rep", "shard"), None),
        P("shard"),
        P("shard", None),
        P("shard", None),
        P("shard", None),
        P("shard", None),
        P("shard"),
        P("shard", None),
        P("shard", None),
        P("shard", None),
    )
    part = functools.partial(local, mesh.shape["rep"], mesh.shape["shard"])
    return jax.shard_map(part, mesh=mesh, in_specs=in_specs, out_specs=out_specs, check_vma=False)
```

```python
import functools

import jax
import jax.numpy as jnp
from jax import lax
from jax.experimental import pallas as pl
from jax.experimental.pallas import tpu as pltpu
from jax.sharding import PartitionSpec as P
import numpy as np

HEADS = 9
KV = 3
HD = 64
RATIO = HEADS // KV


norm_eps = 1e-05
rope_base = 100000.0
neg_fill = -1e30

low = jnp.bfloat16
f32 = jnp.float32
QUERY_ROWS = 128


def rotation_tables(places, head_size):
    half = head_size // 2
    freq = np.float32(rope_base) ** (-(np.arange(half, dtype=np.float32) * np.float32(2.0) / head_size))
    angle = np.arange(places, dtype=np.float32)[:, None] * freq.astype(np.float32)[None, :]
    return np.concatenate([np.cos(angle)] * 4, axis=1), np.concatenate([np.sin(angle)] * 4, axis=1)


def matmul(left, right):
    return jnp.dot(left, right, preferred_element_type=f32)


def matmul_left_t(left, right):
    return lax.dot_general(left, right, (((0,), (0,)), ((), ())), preferred_element_type=f32)


def matmul_right_t(left, right):
    return lax.dot_general(left, right, (((1,), (1,)), ((), ())), preferred_element_type=f32)


def flip(value, bit, replicas):
    return lax.ppermute(value, "rep", [(i, i ^ (1 << bit)) for i in range(replicas)])


def shift_from(value, step, shards):
    return lax.ppermute(value, "shard", [((s + step) % shards, s) for s in range(shards)])


def shift_to(value, step, shards):
    return lax.ppermute(value, "shard", [(s, (s + step) % shards) for s in range(shards)])


def add_low(left, right):
    return (left.astype(f32) + right.astype(f32)).astype(low)


def after(value, *others):
    return lax.optimization_barrier((value, *others))[0]


def gather_shards(mine, shards):
    return jnp.stack([shift_from(mine, step, shards) for step in range(1, shards)])


def gather_bit(got, bit, replicas, *later):
    other = flip(got, bit, replicas)
    return jnp.stack([after(got, *later) if later else got, other])


def halve(keep, other, bit, replicas):
    sent = flip(add_low(keep[1], other[1]), bit, replicas)
    return add_low(keep[0], other[0]), sent


def scatter_over_shards(keep, other, shards, replicas):
    parts = [add_low(keep[step], other[step]) for step in range(1, shards)]
    moved = [shift_to(part, step + 1, shards) for step, part in enumerate(parts)]
    total = keep[0].astype(f32) + other[0].astype(f32)
    for part in moved:
        total = total + part.astype(f32)
    total = total.astype(low)
    bit = 3
    while (1 << bit) < replicas:
        total = add_low(total, flip(total, bit, replicas))
        bit += 1
    return total


def spread(total, order, replicas):
    for bit in order[:-1]:
        total = jnp.stack([total, flip(total, bit, replicas)])
    return total, flip(total, order[-1], replicas)


class Copies:
    def __init__(self, sems):
        self.sems = sems
        self.made = []

    def start(self, source, target):
        copy = pltpu.make_async_copy(source, target, self.sems.at[len(self.made)])
        copy.start()
        self.made.append(copy)

    def wait(self, first=0, last=None):
        for copy in self.made[first:last]:
            copy.wait()


def rows_at(start, count, unit=16):
    return pl.ds(pl.multiple_of(start, unit), count)


def relative(bit, rel):
    return 1 - bit if rel else bit


def shard_at(shard, step, shards):
    at = shard + step
    return jnp.where(at >= shards, at - shards, at)


def swap_halves(values):
    lane = lax.broadcasted_iota(jnp.int32, values.shape, 1)
    return jnp.where(
        lane % HD < HD // 2,
        pltpu.roll(values, 2 * HD - HD // 2, 1),
        pltpu.roll(values, HD // 2, 1),
    )


def norm_recip(values):
    return lax.rsqrt(jnp.mean(values * values, axis=-1, keepdims=True) + norm_eps)


def norm_back(values, recip, gain, grad_normed):
    scaled = grad_normed * gain
    inner = jnp.mean(scaled * values, axis=-1, keepdims=True)
    grad_values = recip * scaled - values * (recip * recip * recip * inner)
    grad_gain = jnp.sum(grad_normed * values * recip, axis=0, keepdims=True)
    return (grad_values, grad_gain)


def pack_kernel(
    where_ref,
    w_out,
    w_query,
    w_key,
    w_value,
    both_gains,
    gate,
    up,
    down_t,
    own,
    attn_mine,
    pair_mine,
    down_mine,
    down,
):
    core, x, y, shard = (where_ref[i] for i in range(4))
    block = 2 * core + x
    part = gate.shape[0]
    packed = own.shape[1]
    columns = rows_at(384 * block, 384, 128)
    pair_mine[...] = jnp.where(y == 0, gate[:, columns], up[:, columns])
    own[0:part] = jnp.concatenate([w_out[...], w_query[...], w_key[...], w_value[...]], axis=1)
    row = lax.broadcasted_iota(jnp.int32, (16, part), 0)
    gains = jnp.where(
        row == 0,
        jnp.broadcast_to(both_gains[0:1].astype(f32), row.shape),
        jnp.where(row == 1, jnp.broadcast_to(both_gains[1:2].astype(f32), row.shape), 0.0),
    )
    gains = jnp.concatenate([gains, jnp.zeros((16, packed - part), f32)], axis=1)
    own[part : part + 16] = pltpu.roll(gains, part * shard, 1).astype(low)
    attn_mine[...] = own[rows_at(80 * y, 80), columns]
    down[...] = down_t[...].T
    eighth = down_mine.shape[0]
    down_mine[...] = down[rows_at(eighth * (2 * block + y), eighth), :]


def fold(value):
    rest = value[..., 384:]
    pad = [(0, 0)] * (value.ndim - 1) + [(0, 384 - rest.shape[-1])]
    return jnp.concatenate([value[..., :384], jnp.pad(rest, pad)], axis=-2)


def prepare_kernel(
    lengths,
    tokens_t,
    cotangent_t,
    table_cos,
    table_sin,
    cosine,
    sine,
    bias,
    hidden,
    scaled,
    grad_low,
):
    rows = hidden.shape[0]
    count = lengths.shape[1]
    ends = []
    for i in range(count):
        ends.append(lengths[0, i] + (ends[-1] if ends else 0))
    place = lax.broadcasted_iota(jnp.int32, cosine.shape, 0)
    start_cos = jnp.broadcast_to(table_cos[0:1], cosine.shape)
    start_sin = jnp.broadcast_to(table_sin[0:1], cosine.shape)
    for end in ends:
        start_cos = jnp.where(place >= end, table_cos[pl.ds(end, 1)], start_cos)
        start_sin = jnp.where(place >= end, table_sin[pl.ds(end, 1)], start_sin)
    cos, sin = table_cos[0:rows], table_sin[0:rows]
    cosine[...] = cos * start_cos + sin * start_sin
    signed = sin * start_cos - cos * start_sin
    lane = lax.broadcasted_iota(jnp.int32, cosine.shape, 1)
    sine[...] = jnp.where(lane % HD < HD // 2, -signed, signed)
    query = lax.broadcasted_iota(jnp.int32, bias.shape, 0)
    key = lax.broadcasted_iota(jnp.int32, bias.shape, 1)
    allowed = query >= key
    for end in ends:
        allowed = allowed & ((query < end) | (key >= end))
    bias[...] = jnp.where(allowed, 0.0, neg_fill)
    values = tokens_t[...].T.astype(f32)
    hidden[...] = values
    scaled[...] = values * norm_recip(values)
    wide = lax.broadcasted_iota(jnp.int32, grad_low.shape, 0)
    grad_low[...] = jnp.where(wide < ends[-1], cotangent_t[...].T, jnp.zeros((), low))


def project_kernel(
    shards,
    part,
    where_ref,
    scaled,
    cosine,
    sine,
    own,
    pieces,
    other,
    weights,
    gains,
    normed,
    query,
    keys,
    values,
    sems,
):
    core, x, y, shard = (where_ref[i] for i in range(4))
    width = scaled.shape[1]
    copies = Copies(sems)
    copies.start(own.at[pl.ds(0, part)], weights.at[rows_at(part * shard, part)])
    copies.start(own.at[pl.ds(part, 16)], weights.at[rows_at(width + 16 * shard, 16)])
    for rel_core, source in enumerate((pieces, other)):
        for rel_x in range(2):
            for rel_y in range(2):
                at_y = relative(y, rel_y)
                block = 2 * relative(core, rel_core) + relative(x, rel_x)
                columns = rows_at(384 * block, 384, 128)
                for step in range(1, shards):
                    at = shard_at(shard, step, shards)
                    piece = source.at[rel_x, rel_y, step - 1]
                    copies.start(
                        piece.at[pl.ds(0, 64)], weights.at[rows_at(part * at + 80 * at_y, 64), columns]
                    )
                    last = jnp.where(at_y == 0, part * at + 64, width + 16 * at)
                    copies.start(piece.at[pl.ds(64, 16)], weights.at[rows_at(last, 16), columns])
    copies.wait()
    total = sum(
        weights[width + 16 * s : width + 16 * s + 16, :width].astype(f32) for s in range(shards)
    )
    gains[...] = total[:8]
    n1 = (scaled[...] * total[0:1]).astype(low)
    normed[...] = n1
    for block in range(8):
        start = 512 + 128 * block
        result = matmul(n1, weights[0:width, start : start + 128])
        heads = [2 * block - 1, 2 * block]
        if heads[0] < HEADS + KV:
            turned = result * cosine[...] + swap_halves(result) * sine[...]
        for side, head in enumerate(heads):
            lanes = slice(HD * side, HD * side + HD)
            if head < 0:
                continue
            if head < HEADS:
                query[head] = (turned[:, lanes] * HD**-0.5).astype(low)
            elif head < HEADS + KV:
                keys[head - HEADS] = turned[:, lanes].astype(low)
            else:
                values[head - HEADS - KV] = result[:, lanes].astype(low)


def attend_kernel(bias, query, keys, values, mixed, log_total):
    rows = bias.shape[0]
    for block in range(rows // QUERY_ROWS):
        at = slice(QUERY_ROWS * block, QUERY_ROWS * (block + 1))
        reach = QUERY_ROWS * (block + 1)
        stacked = jnp.concatenate([query[i, at] for i in range(RATIO)], axis=0)
        scores = matmul_right_t(stacked, keys[0, :reach])
        logits = scores.reshape(RATIO, QUERY_ROWS, reach) + bias[at, :reach][None]
        top = jnp.max(logits, axis=-1, keepdims=True)
        expo = jnp.exp(logits - top)
        total = jnp.sum(expo, axis=-1, keepdims=True)
        probs = (expo * (1.0 / total)).astype(low).reshape(RATIO * QUERY_ROWS, reach)
        log_total[:, at] = top + jnp.log(total)
        result = matmul(probs, values[0, :reach]).astype(low)
        for i in range(RATIO):
            mixed[at, HD * i : HD * i + HD] = result[QUERY_ROWS * i : QUERY_ROWS * (i + 1)]


def attend_last_kernel(
    kv,
    bias,
    query,
    keys,
    values,
    hidden_in,
    gains,
    weights,
    *rest,
):
    before, (mixed, log_total, hidden_one, normed_two) = rest[:kv], rest[kv:]
    attend_kernel(bias, query, keys, values, mixed, log_total)
    width = hidden_in.shape[1]
    every = jnp.concatenate([item[...] for item in before] + [mixed[...]], axis=1)
    hidden = hidden_in[...] + matmul(every, weights[0:width, 0:width])
    hidden_one[...] = hidden
    normed_two[...] = (hidden * norm_recip(hidden) * gains[1:2]).astype(low)


def feed_kernel(
    shards,
    part,
    where_ref,
    hidden_one,
    normed_two,
    gains,
    lengths,
    cotangent,
    own_gate,
    own_up,
    own_down,
    pair_pieces,
    pair_other,
    down_pieces,
    down_other,
    result,
    grad_one,
    grad_gain,
    pair_keep,
    pair_send,
    down_keep,
    down_send,
    pair,
    down,
    hidden,
    grad_gate,
    grad_up,
    grad_pair,
    grad_down,
    sems,
):
    core, x, y, shard = (where_ref[i] for i in range(4))
    width = hidden_one.shape[1]
    down_part = own_down.shape[0]
    eighth = down_part // 8
    copies = Copies(sems)
    copies.start(own_gate, pair.at[0, rows_at(part * shard, part)])
    copies.start(own_up, pair.at[1, rows_at(part * shard, part)])
    for rel_core, source in enumerate((pair_pieces, pair_other)):
        for rel_x in range(2):
            block = 2 * relative(core, rel_core) + relative(x, rel_x)
            columns = rows_at(384 * block, 384, 128)
            for rel_y in range(2):
                at_y = relative(y, rel_y)
                for step in range(1, shards):
                    at = shard_at(shard, step, shards)
                    copies.start(
                        source.at[rel_x, rel_y, step - 1],
                        pair.at[at_y, rows_at(part * at, part), columns],
                    )
    first = len(copies.made)
    copies.start(own_down, down.at[rows_at(down_part * shard, down_part)])
    for rel_core, source in enumerate((down_pieces, down_other)):
        for rel_x in range(2):
            block = 2 * relative(core, rel_core) + relative(x, rel_x)
            for rel_y in range(2):
                place = eighth * (2 * block + relative(y, rel_y))
                for step in range(1, shards):
                    at = shard_at(shard, step, shards)
                    copies.start(
                        source.at[rel_y, rel_x, step - 1],
                        down.at[rows_at(down_part * at + place, eighth)],
                    )
    grad_low = cotangent[...]
    n2 = normed_two[...]
    copies.wait(0, first)
    hidden_width = pair.shape[2]
    for start in range(0, hidden_width, 512):
        at = slice(start, start + 512)
        gate = matmul(n2, pair[0, :, at])
        upward = matmul(n2, pair[1, :, at])
        if start == 0:
            copies.wait(first)
        grad_hidden = matmul_right_t(grad_low, down[at, :])
        sigma = jax.nn.sigmoid(gate)
        active = gate * sigma
        hidden[:, at] = (active * upward).astype(low)
        grad_up[:, at] = (grad_hidden * active).astype(low)
        grad_gate[:, at] = (grad_hidden * upward * (sigma + active * (1.0 - sigma))).astype(low)
    turned = n2.T
    sent = Copies(sems)
    for unit, grads in enumerate((grad_gate, grad_up)):
        for start in range(0, hidden_width, 512):
            at = slice(start, start + 512)
            grad_pair[unit, :, at] = matmul(turned, grads[:, at]).astype(low)
    for start in range(0, hidden_width, 512):
        at = slice(start, start + 512)
        grad_down[at, :] = matmul_left_t(hidden[:, at], grad_low).astype(low)
    for rel_core, (target, down_target) in enumerate(((pair_keep, down_keep), (pair_send, down_send))):
        at_core = relative(core, rel_core)
        for rel_x in range(2):
            at_x = relative(x, rel_x)
            block = 2 * at_core + at_x
            columns = rows_at(384 * block, 384, 128)
            for rel_y in range(2):
                at_y = relative(y, rel_y)
                for step in range(shards):
                    at = shard_at(shard, step, shards)
                    sent.start(
                        grad_pair.at[at_y, rows_at(part * at, part), columns],
                        target.at[rel_x, rel_y, step],
                    )
                    sent.start(
                        grad_down.at[rows_at(down_part * at + eighth * (2 * block + at_y), eighth)],
                        down_target.at[rel_y, rel_x, step],
                    )
    h1 = hidden_one[...]
    total = lengths[0, 0]
    for i in range(1, lengths.shape[1]):
        total = total + lengths[0, i]
    row = lax.broadcasted_iota(jnp.int32, h1.shape, 0)
    summed = h1 + matmul(hidden[...], down[...])
    result[...] = jnp.where(row < total, summed, 0.0).astype(low).T
    grad_normed = matmul_right_t(grad_gate[...], pair[0]) + matmul_right_t(grad_up[...], pair[1])
    grad_from, gain_row = norm_back(h1, norm_recip(h1), gains[1:2], grad_normed)
    grad_one[...] = grad_low.astype(f32) + grad_from
    grad_gain[...] = jnp.broadcast_to(gain_row, grad_gain.shape)
    sent.wait()


def back_heads_kernel(
    bias,
    cosine,
    sine,
    weights,
    query,
    keys,
    values,
    mixed,
    log_total,
    grad_one,
    grad_turned,
    grad_values_out,
    grad_out,
    grad_mixed,
    grad_heads,
):
    rows, width = grad_one.shape
    span = RATIO * HD
    da = grad_one[...].astype(low)
    grad_mixed[...] = matmul_right_t(da, weights[:, 0:width]).astype(low)
    grad_out[...] = matmul_left_t(mixed[...], da).astype(low)
    grad_keys = [None] * (rows // QUERY_ROWS)
    grad_values = [None] * (rows // QUERY_ROWS)
    for block in range(rows // QUERY_ROWS):
        at = slice(QUERY_ROWS * block, QUERY_ROWS * (block + 1))
        reach = QUERY_ROWS * (block + 1)
        stacked = jnp.concatenate([query[i, at] for i in range(RATIO)], axis=0)
        grads = jnp.concatenate([grad_mixed[at, HD * i : HD * i + HD] for i in range(RATIO)], axis=0)
        out = jnp.concatenate([mixed[at, HD * i : HD * i + HD] for i in range(RATIO)], axis=0)
        delta = jnp.sum(grads.astype(f32) * out.astype(f32), axis=-1, keepdims=True)
        scores = matmul_right_t(stacked, keys[0, :reach]).reshape(RATIO, QUERY_ROWS, reach)
        probs = jnp.exp(scores + bias[at, :reach][None] - log_total[:, at]).reshape(-1, reach)
        grad_probs = matmul_right_t(grads, values[0, :reach])
        grad_scores = (probs * (grad_probs - delta)).astype(low)
        grad_query = matmul(grad_scores, keys[0, :reach])
        for i in range(RATIO):
            grad_heads[at, HD * i : HD * i + HD] = (
                grad_query[QUERY_ROWS * i : QUERY_ROWS * (i + 1)] * HD**-0.5
            )
        key_part = matmul_left_t(grad_scores, stacked)
        value_part = matmul_left_t(probs.astype(low), grads)
        for j in range(block + 1):
            at_j = slice(QUERY_ROWS * j, QUERY_ROWS * (j + 1))
            if grad_keys[j] is None:
                grad_keys[j], grad_values[j] = key_part[at_j], value_part[at_j]
            else:
                grad_keys[j] = grad_keys[j] + key_part[at_j]
                grad_values[j] = grad_values[j] + value_part[at_j]
    grad_heads[:, span : span + HD] = jnp.concatenate(grad_keys, axis=0)
    grad_values_out[...] = jnp.concatenate(grad_values, axis=0).astype(low)
    for start in range(0, span + HD, 2 * HD):
        value = grad_heads[:, start : start + 2 * HD]
        turned = value * cosine[...] - swap_halves(value) * sine[...]
        grad_turned[:, start : start + 2 * HD] = turned.astype(low)


def back_last_kernel(
    shards,
    part,
    where_ref,
    hidden_in,
    gains,
    weights_one,
    weights_two,
    normed,
    grad_one,
    grad_gain_two,
    *rest,
):
    core, x, y, shard = (where_ref[i] for i in range(4))
    rows, width = hidden_in.shape
    turned, values, outs = rest[0:KV], rest[KV : 2 * KV], rest[2 * KV : 3 * KV]
    grad_tokens, keep, send, grad_low, grad_weights, sems = rest[3 * KV :]
    span = RATIO * HD
    grad_low[...] = jnp.concatenate(
        [jnp.zeros((rows, HD), low)]
        + [item[:, 0:span] for item in turned]
        + [item[:, span : span + HD] for item in turned]
        + [item[...] for item in values],
        axis=1,
    )
    normed_t = normed[...].T
    for start in range(0, 1024, 512):
        at = slice(start, start + 512)
        grad_weights[0:width, 512 + start : 1024 + start] = matmul(normed_t, grad_low[:, at]).astype(low)
    for kv in range(KV):
        grad_weights[span * kv : span * kv + span, 0:width] = outs[kv][...]
    grad_normed = matmul_right_t(grad_low[:, :512], weights_one[...])
    grad_normed = grad_normed + matmul_right_t(grad_low[:, 512:], weights_two[...])
    hidden = hidden_in[...]
    grad_from, gain_row = norm_back(hidden, norm_recip(hidden), gains[0:1], grad_normed)
    grad_tokens[...] = (grad_one[...] + grad_from).astype(low).T
    row = lax.broadcasted_iota(jnp.int32, (16, width), 0)
    both = jnp.where(
        row == 0,
        jnp.broadcast_to(gain_row, (16, width)),
        jnp.where(row == 1, jnp.broadcast_to(grad_gain_two[0:1], (16, width)), 0.0),
    )
    grad_weights[width : width + 16, :] = jnp.zeros((16, grad_weights.shape[1]), low)
    grad_weights[width : width + 16, 0:width] = both.astype(low)
    copies = Copies(sems)
    for rel_core, target in enumerate((keep, send)):
        for rel_x in range(2):
            for rel_y in range(2):
                at_y = relative(y, rel_y)
                block = 2 * relative(core, rel_core) + relative(x, rel_x)
                columns = rows_at(384 * block, 384, 128)
                for step in range(shards):
                    at = shard_at(shard, step, shards)
                    piece = target.at[rel_y, rel_x, step]
                    copies.start(
                        grad_weights.at[rows_at(part * at + 80 * at_y, 64), columns],
                        piece.at[pl.ds(0, 64)],
                    )
                    last = jnp.where(at_y == 0, part * at + 64, width)
                    copies.start(grad_weights.at[rows_at(last, 16), columns], piece.at[pl.ds(64, 16)])
    copies.wait()


def finish_kernel(
    where_ref,
    pair_pieces,
    pair_other,
    rest_pieces,
    rest_other,
    out_query,
    out_key,
    out_value,
    out_out,
    out_gains,
    out_gate,
    out_up,
    out_down,
    attn,
    pair,
    down,
    sems,
):
    core, x, y = (where_ref[i] for i in range(3))
    part, width = out_out.shape
    copies = Copies(sems)
    for rel_core, (p_from, r_from) in enumerate(((pair_pieces, rest_pieces), (pair_other, rest_other))):
        for rel_x in range(2):
            for rel_y in range(2):
                at_y = relative(y, rel_y)
                block = 2 * relative(core, rel_core) + relative(x, rel_x)
                columns = rows_at(384 * block, 384, 128)
                piece = r_from.at[rel_y, rel_x]
                copies.start(p_from.at[rel_x, rel_y], pair.at[at_y, :, columns])
                copies.start(piece.at[pl.ds(0, 80)], attn.at[rows_at(80 * at_y, 80), columns])
                copies.start(piece.at[pl.ds(80, down.shape[1])], down.at[2 * block + at_y])
    copies.wait()
    kv_width = out_key.shape[1]
    out_out[...] = attn[0:part, 0:width].astype(f32)
    rest = attn[0:part, 512:].astype(f32)
    at = width - 512
    out_query[...] = rest[:, at : at + width]
    out_key[...] = rest[:, at + width : at + width + kv_width]
    out_value[...] = rest[:, at + width + kv_width :]
    out_gains[...] = attn[part : part + 16, 0:width].astype(f32)[:8]
    out_gate[...] = pair[0].astype(f32)
    out_up[...] = pair[1].astype(f32)
    half = down.shape[1] // 2
    whole = [
        jnp.concatenate([down[i, :half], down[i, half:, : width - 384]], axis=1)
        for i in range(down.shape[0])
    ]
    out_down[...] = jnp.concatenate(whole, axis=0).T.astype(f32)


VM = pl.BlockSpec(memory_space=pltpu.VMEM)
SM = pl.BlockSpec(memory_space=pltpu.SMEM)
HB = pl.BlockSpec(memory_space=pl.ANY)


def block_of(sizes, *place):
    return pl.BlockSpec(tuple(sizes), lambda step: place)


def shape(sizes, kind):
    return jax.ShapeDtypeStruct(tuple(sizes), kind)


def call(kernel, name, operands, in_specs, out_shape, out_specs, scratch, micros, room):
    moved = sum(item.size * item.dtype.itemsize for item in out_shape)
    blocks = any(spec.block_shape is not None for spec in in_specs)
    return pl.pallas_call(
        kernel,
        grid=(1,) if blocks else (),
        name=name,
        in_specs=in_specs,
        out_shape=out_shape,
        out_specs=out_specs,
        scratch_shapes=scratch,
        cost_estimate=pl.CostEstimate(
            flops=int(micros * 1e7), bytes_accessed=moved, transcendentals=0
        ),
        compiler_params=pltpu.CompilerParams(vmem_limit_bytes=room << 20),
    )(*operands)


def local(
    replicas,
    shards,
    tokens,
    lengths,
    gain_attn,
    w_query,
    w_key,
    w_value,
    w_out,
    gain_mlp,
    w_gate,
    w_up,
    w_down,
    cotangent,
):
    rows, width = tokens.shape
    part = w_gate.shape[0]
    hidden_width = w_gate.shape[1]
    down_part = w_down.shape[0]
    eighth = down_part // 8
    packed = 2 * width + 2 * w_key.shape[1]
    rep_index = lax.axis_index("rep")
    shard = lax.axis_index("shard")
    core, x, y = ((rep_index >> bit) & 1 for bit in range(3))
    where = jnp.stack([core, x, y, shard]).astype(jnp.int32)

    own, attn_mine, pair_mine, down_mine, own_down = call(
        pack_kernel,
        "pack",
        (
            where,
            w_out,
            w_query,
            w_key,
            w_value,
            jnp.stack([gain_attn, gain_mlp]),
            w_gate,
            w_up,
            w_down.T,
        ),
        [SM] + [VM] * 8,
        (
            shape((part + 16, packed), low),
            shape((80, 384), low),
            shape((part, 384), low),
            shape((eighth, width), low),
            shape((down_part, width), low),
        ),
        [VM] * 5,
        [],
        2,
        60,
    )
    attn_got = gather_shards(attn_mine, shards)
    table_cos, table_sin = rotation_tables(rows + 8, HD)
    cosine, sine, bias, hidden_in, scaled, grad_low = call(
        prepare_kernel,
        "prepare",
        (lengths, tokens.T, cotangent.T, table_cos, table_sin),
        [SM] + [VM] * 4,
        (
            shape((rows, 2 * HD), f32),
            shape((rows, 2 * HD), f32),
            shape((rows, rows), f32),
            shape((rows, width), f32),
            shape((rows, width), f32),
            shape((rows, width), low),
        ),
        [VM] * 6,
        [],
        5,
        60,
    )
    pair_got = gather_shards(after(pair_mine, scaled), shards)
    down_got = gather_shards(after(down_mine, attn_got), shards)
    attn_got = gather_bit(after(attn_got, scaled), 2, replicas)
    attn_got = gather_bit(after(attn_got, pair_got, down_got), 1, replicas)
    pair_got = gather_bit(pair_got, 2, replicas)
    attn_got = after(attn_got, pair_got)
    attn_other = flip(attn_got, 0, replicas)
    weights, gains, normed, query, keys, values = call(
        functools.partial(project_kernel, shards, part),
        "project",
        (where, scaled, cosine, sine, own, attn_got, attn_other),
        [SM, VM, VM, VM, HB, HB, HB],
        (
            shape((width + 16 * shards, packed), low),
            shape((8, width), f32),
            shape((rows, width), low),
            shape((HEADS, rows, HD), low),
            shape((KV, rows, HD), low),
            shape((KV, rows, HD), low),
        ),
        [VM] * 6,
        [pltpu.SemaphoreType.DMA((2 + 16 * (shards - 1),))],
        5,
        60,
    )
    down_got = gather_bit(down_got, 1, replicas, normed)
    mixed, log_total = [], []
    for kv in range(KV):
        outs = [shape((rows, RATIO * HD), low), shape((RATIO, rows, 1), f32)]
        operands = (bias, query, keys, values)
        head_blocks = [
            VM,
            block_of((RATIO, rows, HD), kv, 0, 0),
            block_of((1, rows, HD), kv, 0, 0),
            block_of((1, rows, HD), kv, 0, 0),
        ]
        if kv < KV - 1:
            one, two = call(
                attend_kernel,
                f"attend_{kv}",
                operands,
                head_blocks,
                outs,
                [VM] * 2,
                [],
                3,
                60,
            )
        else:
            down_got = gather_bit(down_got, 2, replicas, *mixed)
            operands += (after(hidden_in, down_got), gains, weights, *mixed)
            one, two, hidden_one, normed_two = call(
                functools.partial(attend_last_kernel, kv),
                f"attend_{kv}",
                operands,
                head_blocks + [VM, VM, block_of((width, 640), 0, 0)] + [VM] * kv,
                outs + [shape((rows, width), f32), shape((rows, width), low)],
                [VM] * 4,
                [],
                4,
                60,
            )
        mixed.append(one)
        log_total.append(two)
    pair_got = gather_bit(pair_got, 1, replicas, normed_two)
    pair_other = flip(pair_got, 0, replicas)
    down_other = flip(down_got, 0, replicas)
    pair_shape = shape((2, 2, shards, part, 384), low)
    down_shape = shape((2, 2, shards, eighth, width), low)
    result, grad_one, grad_gain_two, pair_keep, pair_send, down_keep, down_send = call(
        functools.partial(feed_kernel, shards, part),
        "feed",
        (
            where,
            hidden_one,
            normed_two,
            gains,
            lengths,
            grad_low,
            w_gate,
            w_up,
            own_down,
            pair_got,
            pair_other,
            down_got,
            down_other,
        ),
        [SM] + [VM] * 3 + [SM, VM] + [HB] * 7,
        (
            shape((width, rows), low),
            shape((rows, width), f32),
            shape((8, width), f32),
            pair_shape,
            pair_shape,
            down_shape,
            down_shape,
        ),
        [VM] * 3 + [HB] * 4,
        [
            pltpu.VMEM((2, shards * part, hidden_width), low),
            pltpu.VMEM((hidden_width, width), low),
            pltpu.VMEM((rows, hidden_width), low),
            pltpu.VMEM((rows, hidden_width), low),
            pltpu.VMEM((rows, hidden_width), low),
            pltpu.VMEM((2, shards * part, hidden_width), low),
            pltpu.VMEM((hidden_width, width), low),
            pltpu.SemaphoreType.DMA((16 * shards + 3,)),
        ],
        19,
        60,
    )
    pair_sent = flip(pair_send, 0, replicas)
    down_sent = flip(down_send, 0, replicas)
    grad_turned, grad_values, grad_out = [], [], []
    for kv in range(KV):
        if kv == 1:
            pair_left = halve(pair_keep, after(pair_sent, grad_turned[0]), 1, replicas)
            down_left = halve(down_keep, after(down_sent, grad_turned[0]), 2, replicas)
            grad_one = after(grad_one, pair_sent, down_sent)
        one, two, three = call(
            back_heads_kernel,
            f"back_{kv}",
            (bias, cosine, sine, weights, query, keys, values, mixed[kv], log_total[kv], grad_one),
            [
                VM,
                VM,
                VM,
                block_of((RATIO * HD, 640), kv, 0),
                block_of((RATIO, rows, HD), kv, 0, 0),
                block_of((1, rows, HD), kv, 0, 0),
                block_of((1, rows, HD), kv, 0, 0),
                VM,
                VM,
                VM,
            ],
            (
                shape((rows, RATIO * HD + HD), low),
                shape((rows, HD), low),
                shape((RATIO * HD, width), low),
            ),
            [VM] * 3,
            [pltpu.VMEM((rows, RATIO * HD), low), pltpu.VMEM((rows, RATIO * HD + HD), f32)],
            5,
            60,
        )
        grad_turned.append(one)
        grad_values.append(two)
        grad_out.append(three)
    attn_shape = shape((2, 2, shards, 80, 384), low)
    grad_tokens, attn_keep, attn_send = call(
        functools.partial(back_last_kernel, shards, part),
        "back_last",
        (
            where,
            hidden_in,
            gains,
            weights,
            weights,
            normed,
            grad_one,
            grad_gain_two,
            *grad_turned,
            *grad_values,
            *grad_out,
        ),
        [SM, VM, VM, block_of((width, 512), 0, 1), block_of((width, 512), 0, 2)]
        + [VM] * (3 + 3 * KV),
        (shape((width, rows), low), attn_shape, attn_shape),
        [VM, HB, HB],
        [
            pltpu.VMEM((rows, 1024), low),
            pltpu.VMEM((width + 16, packed), low),
            pltpu.SemaphoreType.DMA((16 * shards,)),
        ],
        6,
        60,
    )
    attn_left = halve(attn_keep, flip(after(attn_send, down_left[1], pair_left[1]), 0, replicas), 2, replicas)
    pair_left = halve(*pair_left, 2, replicas)
    down_left = halve(down_left[0], after(down_left[1], grad_tokens), 1, replicas)
    attn_left = halve(*attn_left, 1, replicas)
    down_total = scatter_over_shards(*down_left, shards, replicas)
    pair_total = scatter_over_shards(*pair_left, shards, replicas)
    attn_total = scatter_over_shards(*attn_left, shards, replicas)
    pair_pieces = spread(pair_total, (2, 1, 0), replicas)
    rest_pieces = spread(jnp.concatenate([attn_total, fold(down_total)]), (1, 2, 0), replicas)
    g_query, g_key, g_value, g_out, g_gains, g_gate, g_up, g_down = call(
        finish_kernel,
        "finish",
        (where, *pair_pieces, *rest_pieces),
        [SM] + [HB] * 4,
        (
            shape(w_query.shape, f32),
            shape(w_key.shape, f32),
            shape(w_value.shape, f32),
            shape(w_out.shape, f32),
            shape((8, width), f32),
            shape(w_gate.shape, f32),
            shape(w_up.shape, f32),
            shape((width, down_part), f32),
        ),
        [VM] * 8,
        [
            pltpu.VMEM((160, packed), low),
            pltpu.VMEM((2, part, hidden_width), low),
            pltpu.VMEM((8, 2 * eighth, 384), low),
            pltpu.SemaphoreType.DMA((24,)),
        ],
        5,
        60,
    )
    g_gains = lax.dynamic_slice(g_gains, (0, part * shard), (2, part))
    return (
        result.T,
        grad_tokens.T,
        g_gains[0],
        g_query,
        g_key,
        g_value,
        g_out,
        g_gains[1],
        g_gate,
        g_up,
        g_down.T,
    )


def solution(mesh):
    in_specs = (
        P(("rep", "shard"), None),
        P(("rep", "shard"), None),
        P("shard"),
        P("shard", None),
        P("shard", None),
        P("shard", None),
        P("shard", None),
        P("shard"),
        P("shard", None),
        P("shard", None),
        P("shard", None),
        P(("rep", "shard"), None),
    )
    out_specs = (
        P(("rep", "shard"), None),
        P(("rep", "shard"), None),
        P("shard"),
        P("shard", None),
        P("shard", None),
        P("shard", None),
        P("shard", None),
        P("shard"),
        P("shard", None),
        P("shard", None),
        P("shard", None),
    )
    part = functools.partial(local, mesh.shape["rep"], mesh.shape["shard"])
    return jax.shard_map(part, mesh=mesh, in_specs=in_specs, out_specs=out_specs, check_vma=False)
```

```python
import functools

import jax
import jax.numpy as jnp
from jax import lax
from jax.experimental import pallas as pl
from jax.experimental.pallas import tpu as pltpu
from jax.sharding import PartitionSpec as P
import numpy as np

HEADS = 9
KV = 3
HD = 64
RATIO = HEADS // KV


norm_eps = 1e-05
rope_base = 100000.0
neg_fill = -1e30

low = jnp.bfloat16
f32 = jnp.float32
QUERY_ROWS = 128


def rotation_tables(places, head_size):
    half = head_size // 2
    freq = np.float32(rope_base) ** (-(np.arange(half, dtype=np.float32) * np.float32(2.0) / head_size))
    angle = np.arange(places, dtype=np.float32)[:, None] * freq.astype(np.float32)[None, :]
    return np.concatenate([np.cos(angle)] * 4, axis=1), np.concatenate([np.sin(angle)] * 4, axis=1)


def matmul(left, right):
    return jnp.dot(left, right, preferred_element_type=f32)


def matmul_left_t(left, right):
    return lax.dot_general(left, right, (((0,), (0,)), ((), ())), preferred_element_type=f32)


def matmul_right_t(left, right):
    return lax.dot_general(left, right, (((1,), (1,)), ((), ())), preferred_element_type=f32)


def flip(value, bit, replicas):
    return lax.ppermute(value, "rep", [(i, i ^ (1 << bit)) for i in range(replicas)])


def shift_from(value, step, shards):
    return lax.ppermute(value, "shard", [((s + step) % shards, s) for s in range(shards)])


def shift_to(value, step, shards):
    return lax.ppermute(value, "shard", [(s, (s + step) % shards) for s in range(shards)])


def add_low(left, right):
    return (left.astype(f32) + right.astype(f32)).astype(low)


def after(value, *others):
    return lax.optimization_barrier((value, *others))[0]


def gather_shards(mine, shards):
    return jnp.stack([shift_from(mine, step, shards) for step in range(1, shards)])


def gather_bit(got, bit, replicas, *later):
    other = flip(got, bit, replicas)
    return jnp.stack([after(got, *later) if later else got, other])


def halve(keep, other, bit, replicas):
    sent = flip(add_low(keep[1], other[1]), bit, replicas)
    return add_low(keep[0], other[0]), sent


def scatter_over_shards(keep, other, shards, replicas):
    parts = [add_low(keep[step], other[step]) for step in range(1, shards)]
    moved = [shift_to(part, step + 1, shards) for step, part in enumerate(parts)]
    total = keep[0].astype(f32) + other[0].astype(f32)
    for part in moved:
        total = total + part.astype(f32)
    total = total.astype(low)
    bit = 3
    while (1 << bit) < replicas:
        total = add_low(total, flip(total, bit, replicas))
        bit += 1
    return total


def spread(total, order, replicas):
    for bit in order[:-1]:
        total = jnp.stack([total, flip(total, bit, replicas)])
    return total, flip(total, order[-1], replicas)


class Copies:
    def __init__(self, sems):
        self.sems = sems
        self.made = []

    def start(self, source, target):
        copy = pltpu.make_async_copy(source, target, self.sems.at[len(self.made)])
        copy.start()
        self.made.append(copy)

    def wait(self, first=0, last=None):
        for copy in self.made[first:last]:
            copy.wait()


def rows_at(start, count, unit=16):
    return pl.ds(pl.multiple_of(start, unit), count)


def position():
    index = lax.axis_index("rep")
    return index % 2, index // 2 % 2, index // 4 % 2, lax.axis_index("shard")


def relative(bit, rel):
    return 1 - bit if rel else bit


def shard_at(shard, step, shards):
    at = shard + step
    return jnp.where(at >= shards, at - shards, at)


def swap_halves(values):
    lane = lax.broadcasted_iota(jnp.int32, values.shape, 1)
    return jnp.where(
        lane % HD < HD // 2,
        pltpu.roll(values, 2 * HD - HD // 2, 1),
        pltpu.roll(values, HD // 2, 1),
    )


def norm_recip(values):
    return lax.rsqrt(jnp.mean(values * values, axis=-1, keepdims=True) + norm_eps)


def norm_back(values, recip, gain, grad_normed):
    scaled = grad_normed * gain
    inner = jnp.mean(scaled * values, axis=-1, keepdims=True)
    grad_values = recip * scaled - values * (recip * recip * recip * inner)
    grad_gain = jnp.sum(grad_normed * values * recip, axis=0, keepdims=True)
    return (grad_values, grad_gain)


def pack_kernel(
    w_out,
    w_query,
    w_key,
    w_value,
    both_gains,
    gate,
    up,
    down_t,
    own,
    attn_mine,
    pair_mine,
    down_mine,
    down,
):
    core, x, y, shard = position()
    block = 2 * core + x
    part = gate.shape[0]
    packed = own.shape[1]
    columns = rows_at(384 * block, 384, 128)
    pair_mine[...] = jnp.where(y == 0, gate[:, columns], up[:, columns])
    own[0:part] = jnp.concatenate([w_out[...], w_query[...], w_key[...], w_value[...]], axis=1)
    row = lax.broadcasted_iota(jnp.int32, (16, part), 0)
    gains = jnp.where(
        row == 0,
        jnp.broadcast_to(both_gains[0:1].astype(f32), row.shape),
        jnp.where(row == 1, jnp.broadcast_to(both_gains[1:2].astype(f32), row.shape), 0.0),
    )
    gains = jnp.concatenate([gains, jnp.zeros((16, packed - part), f32)], axis=1)
    own[part : part + 16] = pltpu.roll(gains, part * shard, 1).astype(low)
    attn_mine[...] = own[rows_at(80 * y, 80), columns]
    down[...] = down_t[...].T
    eighth = down_mine.shape[0]
    down_mine[...] = down[rows_at(eighth * (2 * block + y), eighth), :]


def fold(value):
    rest = value[..., 384:]
    pad = [(0, 0)] * (value.ndim - 1) + [(0, 384 - rest.shape[-1])]
    return jnp.concatenate([value[..., :384], jnp.pad(rest, pad)], axis=-2)


def prepare_kernel(
    lengths,
    tokens_t,
    cotangent_t,
    table_cos,
    table_sin,
    cosine,
    sine,
    bias,
    hidden,
    scaled,
    grad_low,
):
    rows = hidden.shape[0]
    count = lengths.shape[1]
    ends = []
    for i in range(count):
        ends.append(lengths[0, i] + (ends[-1] if ends else 0))
    place = lax.broadcasted_iota(jnp.int32, cosine.shape, 0)
    start_cos = jnp.broadcast_to(table_cos[0:1], cosine.shape)
    start_sin = jnp.broadcast_to(table_sin[0:1], cosine.shape)
    for end in ends:
        start_cos = jnp.where(place >= end, table_cos[pl.ds(end, 1)], start_cos)
        start_sin = jnp.where(place >= end, table_sin[pl.ds(end, 1)], start_sin)
    cos, sin = table_cos[0:rows], table_sin[0:rows]
    cosine[...] = cos * start_cos + sin * start_sin
    signed = sin * start_cos - cos * start_sin
    lane = lax.broadcasted_iota(jnp.int32, cosine.shape, 1)
    sine[...] = jnp.where(lane % HD < HD // 2, -signed, signed)
    query = lax.broadcasted_iota(jnp.int32, bias.shape, 0)
    key = lax.broadcasted_iota(jnp.int32, bias.shape, 1)
    allowed = query >= key
    for end in ends:
        allowed = allowed & ((query < end) | (key >= end))
    bias[...] = jnp.where(allowed, 0.0, neg_fill)
    values = tokens_t[...].T.astype(f32)
    hidden[...] = values
    scaled[...] = values * norm_recip(values)
    wide = lax.broadcasted_iota(jnp.int32, grad_low.shape, 0)
    grad_low[...] = jnp.where(wide < ends[-1], cotangent_t[...].T, jnp.zeros((), low))


def project_kernel(
    shards,
    part,
    scaled,
    cosine,
    sine,
    own,
    pieces,
    other,
    weights,
    gains,
    normed,
    query,
    keys,
    values,
    sems,
):
    core, x, y, shard = position()
    width = scaled.shape[1]
    copies = Copies(sems)
    copies.start(own.at[pl.ds(0, part)], weights.at[rows_at(part * shard, part)])
    copies.start(own.at[pl.ds(part, 16)], weights.at[rows_at(width + 16 * shard, 16)])
    for rel_core, source in enumerate((pieces, other)):
        for rel_x in range(2):
            for rel_y in range(2):
                at_y = relative(y, rel_y)
                block = 2 * relative(core, rel_core) + relative(x, rel_x)
                columns = rows_at(384 * block, 384, 128)
                for step in range(1, shards):
                    at = shard_at(shard, step, shards)
                    piece = source.at[rel_x, rel_y, step - 1]
                    copies.start(
                        piece.at[pl.ds(0, 64)], weights.at[rows_at(part * at + 80 * at_y, 64), columns]
                    )
                    last = jnp.where(at_y == 0, part * at + 64, width + 16 * at)
                    copies.start(piece.at[pl.ds(64, 16)], weights.at[rows_at(last, 16), columns])
    copies.wait()
    total = sum(
        weights[width + 16 * s : width + 16 * s + 16, :width].astype(f32) for s in range(shards)
    )
    gains[...] = total[:8]
    n1 = (scaled[...] * total[0:1]).astype(low)
    normed[...] = n1
    for block in range(8):
        start = 512 + 128 * block
        result = matmul(n1, weights[0:width, start : start + 128])
        heads = [2 * block - 1, 2 * block]
        if heads[0] < HEADS + KV:
            turned = result * cosine[...] + swap_halves(result) * sine[...]
        for side, head in enumerate(heads):
            lanes = slice(HD * side, HD * side + HD)
            if head < 0:
                continue
            if head < HEADS:
                query[head] = (turned[:, lanes] * HD**-0.5).astype(low)
            elif head < HEADS + KV:
                keys[head - HEADS] = turned[:, lanes].astype(low)
            else:
                values[head - HEADS - KV] = result[:, lanes].astype(low)


def attend_kernel(kv, bias, query, keys, values, mixed, log_total):
    rows = bias.shape[0]
    for block in range(rows // QUERY_ROWS):
        at = slice(QUERY_ROWS * block, QUERY_ROWS * (block + 1))
        reach = QUERY_ROWS * (block + 1)
        stacked = jnp.concatenate([query[RATIO * kv + i, at] for i in range(RATIO)], axis=0)
        scores = matmul_right_t(stacked, keys[kv, :reach])
        logits = scores.reshape(RATIO, QUERY_ROWS, reach) + bias[at, :reach][None]
        top = jnp.max(logits, axis=-1, keepdims=True)
        expo = jnp.exp(logits - top)
        total = jnp.sum(expo, axis=-1, keepdims=True)
        probs = (expo * (1.0 / total)).astype(low).reshape(RATIO * QUERY_ROWS, reach)
        log_total[:, at] = top + jnp.log(total)
        result = matmul(probs, values[kv, :reach]).astype(low)
        for i in range(RATIO):
            mixed[at, HD * i : HD * i + HD] = result[QUERY_ROWS * i : QUERY_ROWS * (i + 1)]


def attend_last_kernel(
    kv,
    bias,
    query,
    keys,
    values,
    hidden_in,
    gains,
    weights,
    *rest,
):
    before, (mixed, log_total, hidden_one, normed_two) = rest[:kv], rest[kv:]
    attend_kernel(kv, bias, query, keys, values, mixed, log_total)
    width = hidden_in.shape[1]
    every = jnp.concatenate([item[...] for item in before] + [mixed[...]], axis=1)
    hidden = hidden_in[...] + matmul(every, weights[0:width, 0:width])
    hidden_one[...] = hidden
    normed_two[...] = (hidden * norm_recip(hidden) * gains[1:2]).astype(low)


def feed_kernel(
    shards,
    part,
    hidden_one,
    normed_two,
    gains,
    lengths,
    cotangent,
    own_gate,
    own_up,
    own_down,
    pair_pieces,
    pair_other,
    down_pieces,
    down_other,
    result,
    grad_one,
    grad_gain,
    pair_keep,
    pair_send,
    down_keep,
    down_send,
    pair,
    down,
    hidden,
    grad_gate,
    grad_up,
    grad_pair,
    grad_down,
    sems,
):
    core, x, y, shard = position()
    width = hidden_one.shape[1]
    down_part = own_down.shape[0]
    eighth = down_part // 8
    copies = Copies(sems)
    copies.start(own_gate, pair.at[0, rows_at(part * shard, part)])
    copies.start(own_up, pair.at[1, rows_at(part * shard, part)])
    for rel_core, source in enumerate((pair_pieces, pair_other)):
        for rel_x in range(2):
            block = 2 * relative(core, rel_core) + relative(x, rel_x)
            columns = rows_at(384 * block, 384, 128)
            for rel_y in range(2):
                at_y = relative(y, rel_y)
                for step in range(1, shards):
                    at = shard_at(shard, step, shards)
                    copies.start(
                        source.at[rel_x, rel_y, step - 1],
                        pair.at[at_y, rows_at(part * at, part), columns],
                    )
    first = len(copies.made)
    copies.start(own_down, down.at[rows_at(down_part * shard, down_part)])
    for rel_core, source in enumerate((down_pieces, down_other)):
        for rel_x in range(2):
            block = 2 * relative(core, rel_core) + relative(x, rel_x)
            for rel_y in range(2):
                place = eighth * (2 * block + relative(y, rel_y))
                for step in range(1, shards):
                    at = shard_at(shard, step, shards)
                    copies.start(
                        source.at[rel_y, rel_x, step - 1],
                        down.at[rows_at(down_part * at + place, eighth)],
                    )
    grad_low = cotangent[...]
    n2 = normed_two[...]
    copies.wait(0, first)
    hidden_width = pair.shape[2]
    for start in range(0, hidden_width, 512):
        at = slice(start, start + 512)
        gate = matmul(n2, pair[0, :, at])
        upward = matmul(n2, pair[1, :, at])
        if start == 0:
            copies.wait(first)
        grad_hidden = matmul_right_t(grad_low, down[at, :])
        sigma = jax.nn.sigmoid(gate)
        active = gate * sigma
        hidden[:, at] = (active * upward).astype(low)
        grad_up[:, at] = (grad_hidden * active).astype(low)
        grad_gate[:, at] = (grad_hidden * upward * (sigma + active * (1.0 - sigma))).astype(low)
    turned = n2.T
    sent = Copies(sems)
    for unit, grads in enumerate((grad_gate, grad_up)):
        for start in range(0, hidden_width, 512):
            at = slice(start, start + 512)
            grad_pair[unit, :, at] = matmul(turned, grads[:, at]).astype(low)
    for start in range(0, hidden_width, 512):
        at = slice(start, start + 512)
        grad_down[at, :] = matmul_left_t(hidden[:, at], grad_low).astype(low)
    for rel_core, (target, down_target) in enumerate(((pair_keep, down_keep), (pair_send, down_send))):
        at_core = relative(core, rel_core)
        for rel_x in range(2):
            at_x = relative(x, rel_x)
            block = 2 * at_core + at_x
            columns = rows_at(384 * block, 384, 128)
            for rel_y in range(2):
                at_y = relative(y, rel_y)
                for step in range(shards):
                    at = shard_at(shard, step, shards)
                    sent.start(
                        grad_pair.at[at_y, rows_at(part * at, part), columns],
                        target.at[rel_x, rel_y, step],
                    )
                    sent.start(
                        grad_down.at[rows_at(down_part * at + eighth * (2 * block + at_y), eighth)],
                        down_target.at[rel_y, rel_x, step],
                    )
    h1 = hidden_one[...]
    total = lengths[0, 0]
    for i in range(1, lengths.shape[1]):
        total = total + lengths[0, i]
    row = lax.broadcasted_iota(jnp.int32, h1.shape, 0)
    summed = h1 + matmul(hidden[...], down[...])
    result[...] = jnp.where(row < total, summed, 0.0).astype(low).T
    grad_normed = matmul_right_t(grad_gate[...], pair[0]) + matmul_right_t(grad_up[...], pair[1])
    grad_from, gain_row = norm_back(h1, norm_recip(h1), gains[1:2], grad_normed)
    grad_one[...] = grad_low.astype(f32) + grad_from
    grad_gain[...] = jnp.broadcast_to(gain_row, grad_gain.shape)
    sent.wait()


def back_heads_kernel(
    kv,
    bias,
    cosine,
    sine,
    weights,
    query,
    keys,
    values,
    mixed,
    log_total,
    grad_one,
    grad_turned,
    grad_values_out,
    grad_out,
    grad_mixed,
    grad_heads,
):
    rows, width = grad_one.shape
    span = RATIO * HD
    da = grad_one[...].astype(low)
    grad_mixed[...] = matmul_right_t(da, weights[span * kv : span * kv + span, 0:width]).astype(low)
    grad_out[...] = matmul_left_t(mixed[...], da).astype(low)
    grad_keys = [None] * (rows // QUERY_ROWS)
    grad_values = [None] * (rows // QUERY_ROWS)
    for block in range(rows // QUERY_ROWS):
        at = slice(QUERY_ROWS * block, QUERY_ROWS * (block + 1))
        reach = QUERY_ROWS * (block + 1)
        stacked = jnp.concatenate([query[RATIO * kv + i, at] for i in range(RATIO)], axis=0)
        grads = jnp.concatenate([grad_mixed[at, HD * i : HD * i + HD] for i in range(RATIO)], axis=0)
        out = jnp.concatenate([mixed[at, HD * i : HD * i + HD] for i in range(RATIO)], axis=0)
        delta = jnp.sum(grads.astype(f32) * out.astype(f32), axis=-1, keepdims=True)
        scores = matmul_right_t(stacked, keys[kv, :reach]).reshape(RATIO, QUERY_ROWS, reach)
        probs = jnp.exp(scores + bias[at, :reach][None] - log_total[:, at]).reshape(-1, reach)
        grad_probs = matmul_right_t(grads, values[kv, :reach])
        grad_scores = (probs * (grad_probs - delta)).astype(low)
        grad_query = matmul(grad_scores, keys[kv, :reach])
        for i in range(RATIO):
            grad_heads[at, HD * i : HD * i + HD] = (
                grad_query[QUERY_ROWS * i : QUERY_ROWS * (i + 1)] * HD**-0.5
            )
        key_part = matmul_left_t(grad_scores, stacked)
        value_part = matmul_left_t(probs.astype(low), grads)
        for j in range(block + 1):
            at_j = slice(QUERY_ROWS * j, QUERY_ROWS * (j + 1))
            if grad_keys[j] is None:
                grad_keys[j], grad_values[j] = key_part[at_j], value_part[at_j]
            else:
                grad_keys[j] = grad_keys[j] + key_part[at_j]
                grad_values[j] = grad_values[j] + value_part[at_j]
    grad_heads[:, span : span + HD] = jnp.concatenate(grad_keys, axis=0)
    grad_values_out[...] = jnp.concatenate(grad_values, axis=0).astype(low)
    for start in range(0, span + HD, 2 * HD):
        value = grad_heads[:, start : start + 2 * HD]
        turned = value * cosine[...] - swap_halves(value) * sine[...]
        grad_turned[:, start : start + 2 * HD] = turned.astype(low)


def back_last_kernel(
    shards,
    part,
    hidden_in,
    gains,
    weights,
    normed,
    grad_one,
    grad_gain_two,
    *rest,
):
    core, x, y, shard = position()
    rows, width = hidden_in.shape
    turned, values, outs = rest[0:KV], rest[KV : 2 * KV], rest[2 * KV : 3 * KV]
    grad_tokens, keep, send, grad_low, grad_weights, sems = rest[3 * KV :]
    span = RATIO * HD
    grad_low[...] = jnp.concatenate(
        [jnp.zeros((rows, HD), low)]
        + [item[:, 0:span] for item in turned]
        + [item[:, span : span + HD] for item in turned]
        + [item[...] for item in values],
        axis=1,
    )
    normed_t = normed[...].T
    for start in range(0, 1024, 512):
        at = slice(start, start + 512)
        grad_weights[0:width, 512 + start : 1024 + start] = matmul(normed_t, grad_low[:, at]).astype(low)
    for kv in range(KV):
        grad_weights[span * kv : span * kv + span, 0:width] = outs[kv][...]
    grad_normed = matmul_right_t(grad_low[...], weights[0:width, 512:1536])
    hidden = hidden_in[...]
    grad_from, gain_row = norm_back(hidden, norm_recip(hidden), gains[0:1], grad_normed)
    grad_tokens[...] = (grad_one[...] + grad_from).astype(low).T
    row = lax.broadcasted_iota(jnp.int32, (16, width), 0)
    both = jnp.where(
        row == 0,
        jnp.broadcast_to(gain_row, (16, width)),
        jnp.where(row == 1, jnp.broadcast_to(grad_gain_two[0:1], (16, width)), 0.0),
    )
    grad_weights[width : width + 16, :] = jnp.zeros((16, grad_weights.shape[1]), low)
    grad_weights[width : width + 16, 0:width] = both.astype(low)
    copies = Copies(sems)
    for rel_core, target in enumerate((keep, send)):
        for rel_x in range(2):
            for rel_y in range(2):
                at_y = relative(y, rel_y)
                block = 2 * relative(core, rel_core) + relative(x, rel_x)
                columns = rows_at(384 * block, 384, 128)
                for step in range(shards):
                    at = shard_at(shard, step, shards)
                    piece = target.at[rel_y, rel_x, step]
                    copies.start(
                        grad_weights.at[rows_at(part * at + 80 * at_y, 64), columns],
                        piece.at[pl.ds(0, 64)],
                    )
                    last = jnp.where(at_y == 0, part * at + 64, width)
                    copies.start(grad_weights.at[rows_at(last, 16), columns], piece.at[pl.ds(64, 16)])
    copies.wait()


def finish_kernel(
    pair_pieces,
    pair_other,
    rest_pieces,
    rest_other,
    out_query,
    out_key,
    out_value,
    out_out,
    out_gain_one,
    out_gain_two,
    out_gate,
    out_up,
    out_down,
    attn,
    pair,
    down,
    sems,
):
    core, x, y, shard = position()
    part, width = out_out.shape
    copies = Copies(sems)
    for rel_core, (p_from, r_from) in enumerate(((pair_pieces, rest_pieces), (pair_other, rest_other))):
        for rel_x in range(2):
            for rel_y in range(2):
                at_y = relative(y, rel_y)
                block = 2 * relative(core, rel_core) + relative(x, rel_x)
                columns = rows_at(384 * block, 384, 128)
                piece = r_from.at[rel_y, rel_x]
                copies.start(p_from.at[rel_x, rel_y], pair.at[at_y, :, columns])
                copies.start(piece.at[pl.ds(0, 80)], attn.at[rows_at(80 * at_y, 80), columns])
                copies.start(piece.at[pl.ds(80, down.shape[1])], down.at[2 * block + at_y])
    copies.wait()
    kv_width = out_key.shape[1]
    out_out[...] = attn[0:part, 0:width].astype(f32)
    rest = attn[0:part, 512:].astype(f32)
    at = width - 512
    out_query[...] = rest[:, at : at + width]
    out_key[...] = rest[:, at + width : at + width + kv_width]
    out_value[...] = rest[:, at + width + kv_width :]
    gains = attn[part : part + 16, :].astype(f32)
    gains = pltpu.roll(gains, gains.shape[1] - part * shard, 1)
    out_gain_one[...] = gains[0:1, :part]
    out_gain_two[...] = gains[1:2, :part]
    out_gate[...] = pair[0].astype(f32)
    out_up[...] = pair[1].astype(f32)
    half = down.shape[1] // 2
    whole = [
        jnp.concatenate([down[i, :half], down[i, half:, : width - 384]], axis=1)
        for i in range(down.shape[0])
    ]
    out_down[...] = jnp.concatenate(whole, axis=0).T.astype(f32)


VM = pl.BlockSpec(memory_space=pltpu.VMEM)
SM = pl.BlockSpec(memory_space=pltpu.SMEM)
HB = pl.BlockSpec(memory_space=pltpu.HBM)


def shape(sizes, kind):
    return jax.ShapeDtypeStruct(tuple(sizes), kind)


def call(kernel, name, operands, in_specs, out_shape, out_specs, scratch, micros, room):
    moved = sum(item.size * item.dtype.itemsize for item in out_shape)
    return pl.pallas_call(
        kernel,
        name=name,
        in_specs=in_specs,
        out_shape=out_shape,
        out_specs=out_specs,
        scratch_shapes=scratch,
        cost_estimate=pl.CostEstimate(
            flops=int(micros * 1e7), bytes_accessed=moved, transcendentals=0
        ),
        compiler_params=pltpu.CompilerParams(vmem_limit_bytes=room << 20),
    )(*operands)


def local(
    replicas,
    shards,
    tokens,
    lengths,
    gain_attn,
    w_query,
    w_key,
    w_value,
    w_out,
    gain_mlp,
    w_gate,
    w_up,
    w_down,
    cotangent,
):
    rows, width = tokens.shape
    part = w_gate.shape[0]
    hidden_width = w_gate.shape[1]
    down_part = w_down.shape[0]
    eighth = down_part // 8
    packed = 2 * width + 2 * w_key.shape[1]
    own, attn_mine, pair_mine, down_mine, own_down = call(
        pack_kernel,
        "pack",
        (
            w_out,
            w_query,
            w_key,
            w_value,
            jnp.stack([gain_attn, gain_mlp]),
            w_gate,
            w_up,
            w_down.T,
        ),
        [VM] * 8,
        (
            shape((part + 16, packed), low),
            shape((80, 384), low),
            shape((part, 384), low),
            shape((eighth, width), low),
            shape((down_part, width), low),
        ),
        [VM] * 5,
        [],
        2,
        60,
    )
    attn_got = gather_shards(attn_mine, shards)
    table_cos, table_sin = rotation_tables(rows + 8, HD)
    cosine, sine, bias, hidden_in, scaled, grad_low = call(
        prepare_kernel,
        "prepare",
        (lengths, tokens.T, cotangent.T, table_cos, table_sin),
        [SM] + [VM] * 4,
        (
            shape((rows, 2 * HD), f32),
            shape((rows, 2 * HD), f32),
            shape((rows, rows), f32),
            shape((rows, width), f32),
            shape((rows, width), f32),
            shape((rows, width), low),
        ),
        [VM] * 6,
        [],
        5,
        24,
    )
    pair_got = gather_shards(after(pair_mine, scaled), shards)
    down_got = gather_shards(after(down_mine, attn_got), shards)
    attn_got = gather_bit(after(attn_got, scaled), 2, replicas)
    attn_got = gather_bit(after(attn_got, pair_got, down_got), 1, replicas)
    pair_got = gather_bit(pair_got, 2, replicas)
    attn_got = after(attn_got, pair_got)
    attn_other = flip(attn_got, 0, replicas)
    weights, gains, normed, query, keys, values = call(
        functools.partial(project_kernel, shards, part),
        "project",
        (scaled, cosine, sine, own, attn_got, attn_other),
        [VM, VM, VM, HB, HB, HB],
        (
            shape((width + 16 * shards, packed), low),
            shape((8, width), f32),
            shape((rows, width), low),
            shape((HEADS, rows, HD), low),
            shape((KV, rows, HD), low),
            shape((KV, rows, HD), low),
        ),
        [VM] * 6,
        [pltpu.SemaphoreType.DMA((2 + 16 * (shards - 1),))],
        5,
        24,
    )
    down_got = gather_bit(down_got, 1, replicas, normed)
    mixed, log_total = [], []
    for kv in range(KV):
        outs = [shape((rows, RATIO * HD), low), shape((RATIO, rows, 1), f32)]
        operands = (bias, query, keys, values)
        if kv < KV - 1:
            one, two = call(
                functools.partial(attend_kernel, kv),
                f"attend_{kv}",
                operands,
                [VM] * 4,
                outs,
                [VM] * 2,
                [],
                3,
                24,
            )
        else:
            down_got = gather_bit(down_got, 2, replicas, *mixed)
            operands += (after(hidden_in, down_got), gains, weights, *mixed)
            one, two, hidden_one, normed_two = call(
                functools.partial(attend_last_kernel, kv),
                f"attend_{kv}",
                operands,
                [VM] * len(operands),
                outs + [shape((rows, width), f32), shape((rows, width), low)],
                [VM] * 4,
                [],
                4,
                24,
            )
        mixed.append(one)
        log_total.append(two)
    pair_got = gather_bit(pair_got, 1, replicas, normed_two)
    pair_other = flip(pair_got, 0, replicas)
    down_other = flip(down_got, 0, replicas)
    pair_shape = shape((2, 2, shards, part, 384), low)
    down_shape = shape((2, 2, shards, eighth, width), low)
    result, grad_one, grad_gain_two, pair_keep, pair_send, down_keep, down_send = call(
        functools.partial(feed_kernel, shards, part),
        "feed",
        (
            hidden_one,
            normed_two,
            gains,
            lengths,
            grad_low,
            w_gate,
            w_up,
            own_down,
            pair_got,
            pair_other,
            down_got,
            down_other,
        ),
        [VM] * 3 + [SM, VM] + [HB] * 7,
        (
            shape((width, rows), low),
            shape((rows, width), f32),
            shape((8, width), f32),
            pair_shape,
            pair_shape,
            down_shape,
            down_shape,
        ),
        [VM] * 3 + [HB] * 4,
        [
            pltpu.VMEM((2, shards * part, hidden_width), low),
            pltpu.VMEM((hidden_width, width), low),
            pltpu.VMEM((rows, hidden_width), low),
            pltpu.VMEM((rows, hidden_width), low),
            pltpu.VMEM((rows, hidden_width), low),
            pltpu.VMEM((2, shards * part, hidden_width), low),
            pltpu.VMEM((hidden_width, width), low),
            pltpu.SemaphoreType.DMA((16 * shards + 3,)),
        ],
        19,
        40,
    )
    pair_sent = flip(pair_send, 0, replicas)
    down_sent = flip(down_send, 0, replicas)
    grad_turned, grad_values, grad_out = [], [], []
    for kv in range(KV):
        if kv == 1:
            pair_left = halve(pair_keep, after(pair_sent, grad_turned[0]), 1, replicas)
            down_left = halve(down_keep, after(down_sent, grad_turned[0]), 2, replicas)
            grad_one = after(grad_one, pair_sent, down_sent)
        one, two, three = call(
            functools.partial(back_heads_kernel, kv),
            f"back_{kv}",
            (bias, cosine, sine, weights, query, keys, values, mixed[kv], log_total[kv], grad_one),
            [VM] * 10,
            (
                shape((rows, RATIO * HD + HD), low),
                shape((rows, HD), low),
                shape((RATIO * HD, width), low),
            ),
            [VM] * 3,
            [pltpu.VMEM((rows, RATIO * HD), low), pltpu.VMEM((rows, RATIO * HD + HD), f32)],
            5,
            24,
        )
        grad_turned.append(one)
        grad_values.append(two)
        grad_out.append(three)
    attn_shape = shape((2, 2, shards, 80, 384), low)
    grad_tokens, attn_keep, attn_send = call(
        functools.partial(back_last_kernel, shards, part),
        "back_last",
        (
            hidden_in,
            gains,
            weights,
            normed,
            grad_one,
            grad_gain_two,
            *grad_turned,
            *grad_values,
            *grad_out,
        ),
        [VM] * (6 + 3 * KV),
        (shape((width, rows), low), attn_shape, attn_shape),
        [VM, HB, HB],
        [
            pltpu.VMEM((rows, 1024), low),
            pltpu.VMEM((width + 16, packed), low),
            pltpu.SemaphoreType.DMA((16 * shards,)),
        ],
        6,
        24,
    )
    attn_left = halve(attn_keep, flip(after(attn_send, down_left[1], pair_left[1]), 0, replicas), 2, replicas)
    pair_left = halve(*pair_left, 2, replicas)
    down_left = halve(down_left[0], after(down_left[1], grad_tokens), 1, replicas)
    attn_left = halve(*attn_left, 1, replicas)
    down_total = scatter_over_shards(*down_left, shards, replicas)
    pair_total = scatter_over_shards(*pair_left, shards, replicas)
    attn_total = scatter_over_shards(*attn_left, shards, replicas)
    pair_pieces = spread(pair_total, (2, 1, 0), replicas)
    rest_pieces = spread(jnp.concatenate([attn_total, fold(down_total)]), (1, 2, 0), replicas)
    g_query, g_key, g_value, g_out, g_gain_one, g_gain_two, g_gate, g_up, g_down = call(
        finish_kernel,
        "finish",
        (*pair_pieces, *rest_pieces),
        [HB] * 4,
        (
            shape(w_query.shape, f32),
            shape(w_key.shape, f32),
            shape(w_value.shape, f32),
            shape(w_out.shape, f32),
            shape((1, part), f32),
            shape((1, part), f32),
            shape(w_gate.shape, f32),
            shape(w_up.shape, f32),
            shape((width, down_part), f32),
        ),
        [VM] * 9,
        [
            pltpu.VMEM((160, packed), low),
            pltpu.VMEM((2, part, hidden_width), low),
            pltpu.VMEM((8, 2 * eighth, 384), low),
            pltpu.SemaphoreType.DMA((24,)),
        ],
        5,
        24,
    )
    return (
        result.T,
        grad_tokens.T,
        g_gain_one.reshape(part),
        g_query,
        g_key,
        g_value,
        g_out,
        g_gain_two.reshape(part),
        g_gate,
        g_up,
        g_down.T,
    )


def solution(mesh):
    in_specs = (
        P(("rep", "shard"), None),
        P(("rep", "shard"), None),
        P("shard"),
        P("shard", None),
        P("shard", None),
        P("shard", None),
        P("shard", None),
        P("shard"),
        P("shard", None),
        P("shard", None),
        P("shard", None),
        P(("rep", "shard"), None),
    )
    out_specs = (
        P(("rep", "shard"), None),
        P(("rep", "shard"), None),
        P("shard"),
        P("shard", None),
        P("shard", None),
        P("shard", None),
        P("shard", None),
        P("shard"),
        P("shard", None),
        P("shard", None),
        P("shard", None),
    )
    part = functools.partial(local, mesh.shape["rep"], mesh.shape["shard"])
    return jax.shard_map(part, mesh=mesh, in_specs=in_specs, out_specs=out_specs, check_vma=False)
```

```python
import functools

import jax
import jax.numpy as jnp
from jax import lax
from jax.experimental import pallas as pl
from jax.experimental.pallas import tpu as pltpu
from jax.sharding import PartitionSpec as P
import numpy as np

HEADS = 9
KV = 3
HD = 64
RATIO = HEADS // KV


norm_eps = 1e-05
rope_base = 100000.0
neg_fill = -1e30

low = jnp.bfloat16
f32 = jnp.float32
QUERY_ROWS = 128


def rotation_tables(places, head_size):
    half = head_size // 2
    freq = np.float32(rope_base) ** (-(np.arange(half, dtype=np.float32) * np.float32(2.0) / head_size))
    angle = np.arange(places, dtype=np.float32)[:, None] * freq.astype(np.float32)[None, :]
    return np.concatenate([np.cos(angle)] * 4, axis=1), np.concatenate([np.sin(angle)] * 4, axis=1)


def matmul(left, right):
    return jnp.dot(left, right, preferred_element_type=f32)


def matmul_left_t(left, right):
    return lax.dot_general(left, right, (((0,), (0,)), ((), ())), preferred_element_type=f32)


def matmul_right_t(left, right):
    return lax.dot_general(left, right, (((1,), (1,)), ((), ())), preferred_element_type=f32)


def flip(value, bit, replicas):
    return lax.ppermute(value, "rep", [(i, i ^ (1 << bit)) for i in range(replicas)])


def shift_from(value, step, shards):
    return lax.ppermute(value, "shard", [((s + step) % shards, s) for s in range(shards)])


def shift_to(value, step, shards):
    return lax.ppermute(value, "shard", [(s, (s + step) % shards) for s in range(shards)])


def add_low(left, right):
    return (left.astype(f32) + right.astype(f32)).astype(low)


def after(value, *others):
    return lax.optimization_barrier((value, *others))[0]


def gather_shards(mine, shards):
    return jnp.stack([shift_from(mine, step, shards) for step in range(1, shards)])


def gather_bit(got, bit, replicas, *later):
    other = flip(got, bit, replicas)
    return jnp.stack([after(got, *later) if later else got, other])


def halve(keep, other, bit, replicas):
    sent = flip(add_low(keep[1], other[1]), bit, replicas)
    return add_low(keep[0], other[0]), sent


def scatter_over_shards(keep, other, shards, replicas):
    parts = [add_low(keep[step], other[step]) for step in range(1, shards)]
    moved = [shift_to(part, step + 1, shards) for step, part in enumerate(parts)]
    total = keep[0].astype(f32) + other[0].astype(f32)
    for part in moved:
        total = total + part.astype(f32)
    total = total.astype(low)
    bit = 3
    while (1 << bit) < replicas:
        total = add_low(total, flip(total, bit, replicas))
        bit += 1
    return total


def spread(total, order, replicas):
    for bit in order[:-1]:
        total = jnp.stack([total, flip(total, bit, replicas)])
    return total, flip(total, order[-1], replicas)


def place(source, target):
    target[...] = source[...]


def rows_at(start, count, unit=16):
    return pl.ds(pl.multiple_of(start, unit), count)


def position():
    index = lax.axis_index("rep")
    return index % 2, index // 2 % 2, index // 4 % 2, lax.axis_index("shard")


def relative(bit, rel):
    return 1 - bit if rel else bit


def shard_at(shard, step, shards):
    at = shard + step
    return jnp.where(at >= shards, at - shards, at)


def swap_halves(values):
    lane = lax.broadcasted_iota(jnp.int32, values.shape, 1)
    return jnp.where(
        lane % HD < HD // 2,
        pltpu.roll(values, 2 * HD - HD // 2, 1),
        pltpu.roll(values, HD // 2, 1),
    )


def norm_recip(values):
    return lax.rsqrt(jnp.mean(values * values, axis=-1, keepdims=True) + norm_eps)


def norm_back(values, recip, gain, grad_normed):
    scaled = grad_normed * gain
    inner = jnp.mean(scaled * values, axis=-1, keepdims=True)
    grad_values = recip * scaled - values * (recip * recip * recip * inner)
    grad_gain = jnp.sum(grad_normed * values * recip, axis=0, keepdims=True)
    return (grad_values, grad_gain)


def pack_kernel(
    w_out,
    w_query,
    w_key,
    w_value,
    both_gains,
    gate,
    up,
    down_t,
    own,
    attn_mine,
    pair_mine,
    down_mine,
    down,
):
    core, x, y, shard = position()
    block = 2 * core + x
    part = gate.shape[0]
    packed = own.shape[1]
    columns = rows_at(384 * block, 384, 128)
    pair_mine[...] = jnp.where(y == 0, gate[:, columns], up[:, columns])
    own[0:part] = jnp.concatenate([w_out[...], w_query[...], w_key[...], w_value[...]], axis=1)
    row = lax.broadcasted_iota(jnp.int32, (16, part), 0)
    gains = jnp.where(
        row == 0,
        jnp.broadcast_to(both_gains[0:1].astype(f32), row.shape),
        jnp.where(row == 1, jnp.broadcast_to(both_gains[1:2].astype(f32), row.shape), 0.0),
    )
    gains = jnp.concatenate([gains, jnp.zeros((16, packed - part), f32)], axis=1)
    own[part : part + 16] = pltpu.roll(gains, part * shard, 1).astype(low)
    attn_mine[...] = own[rows_at(80 * y, 80), columns]
    down[...] = down_t[...].T
    eighth = down_mine.shape[0]
    down_mine[...] = down[rows_at(eighth * (2 * block + y), eighth), :]


def fold(value):
    rest = value[..., 384:]
    pad = [(0, 0)] * (value.ndim - 1) + [(0, 384 - rest.shape[-1])]
    return jnp.concatenate([value[..., :384], jnp.pad(rest, pad)], axis=-2)


def prepare_kernel(
    lengths,
    tokens_t,
    cotangent_t,
    table_cos,
    table_sin,
    cosine,
    sine,
    bias,
    hidden,
    scaled,
    grad_low,
):
    rows = hidden.shape[0]
    count = lengths.shape[1]
    ends = []
    for i in range(count):
        ends.append(lengths[0, i] + (ends[-1] if ends else 0))
    place = lax.broadcasted_iota(jnp.int32, cosine.shape, 0)
    start_cos = jnp.broadcast_to(table_cos[0:1], cosine.shape)
    start_sin = jnp.broadcast_to(table_sin[0:1], cosine.shape)
    for end in ends:
        start_cos = jnp.where(place >= end, table_cos[pl.ds(end, 1)], start_cos)
        start_sin = jnp.where(place >= end, table_sin[pl.ds(end, 1)], start_sin)
    cos, sin = table_cos[0:rows], table_sin[0:rows]
    cosine[...] = cos * start_cos + sin * start_sin
    signed = sin * start_cos - cos * start_sin
    lane = lax.broadcasted_iota(jnp.int32, cosine.shape, 1)
    sine[...] = jnp.where(lane % HD < HD // 2, -signed, signed)
    query = lax.broadcasted_iota(jnp.int32, bias.shape, 0)
    key = lax.broadcasted_iota(jnp.int32, bias.shape, 1)
    allowed = query >= key
    for end in ends:
        allowed = allowed & ((query < end) | (key >= end))
    bias[...] = jnp.where(allowed, 0.0, neg_fill)
    values = tokens_t[...].T.astype(f32)
    hidden[...] = values
    scaled[...] = values * norm_recip(values)
    wide = lax.broadcasted_iota(jnp.int32, grad_low.shape, 0)
    grad_low[...] = jnp.where(wide < ends[-1], cotangent_t[...].T, jnp.zeros((), low))


def project_kernel(
    shards,
    part,
    scaled,
    cosine,
    sine,
    own,
    pieces,
    other,
    weights,
    gains,
    normed,
    query,
    keys,
    values,
):
    core, x, y, shard = position()
    width = scaled.shape[1]
    place(own.at[pl.ds(0, part)], weights.at[rows_at(part * shard, part)])
    place(own.at[pl.ds(part, 16)], weights.at[rows_at(width + 16 * shard, 16)])
    for rel_core, source in enumerate((pieces, other)):
        for rel_x in range(2):
            for rel_y in range(2):
                at_y = relative(y, rel_y)
                block = 2 * relative(core, rel_core) + relative(x, rel_x)
                columns = rows_at(384 * block, 384, 128)
                for step in range(1, shards):
                    at = shard_at(shard, step, shards)
                    piece = source.at[rel_x, rel_y, step - 1]
                    place(
                        piece.at[pl.ds(0, 64)], weights.at[rows_at(part * at + 80 * at_y, 64), columns]
                    )
                    last = jnp.where(at_y == 0, part * at + 64, width + 16 * at)
                    place(piece.at[pl.ds(64, 16)], weights.at[rows_at(last, 16), columns])
    total = sum(
        weights[width + 16 * s : width + 16 * s + 16, :width].astype(f32) for s in range(shards)
    )
    gains[...] = total[:8]
    n1 = (scaled[...] * total[0:1]).astype(low)
    normed[...] = n1
    for block in range(8):
        start = 512 + 128 * block
        result = matmul(n1, weights[0:width, start : start + 128])
        heads = [2 * block - 1, 2 * block]
        if heads[0] < HEADS + KV:
            turned = result * cosine[...] + swap_halves(result) * sine[...]
        for side, head in enumerate(heads):
            lanes = slice(HD * side, HD * side + HD)
            if head < 0:
                continue
            if head < HEADS:
                query[head] = (turned[:, lanes] * HD**-0.5).astype(low)
            elif head < HEADS + KV:
                keys[head - HEADS] = turned[:, lanes].astype(low)
            else:
                values[head - HEADS - KV] = result[:, lanes].astype(low)


def attend_kernel(kv, bias, query, keys, values, mixed, log_total):
    rows = bias.shape[0]
    for block in range(rows // QUERY_ROWS):
        at = slice(QUERY_ROWS * block, QUERY_ROWS * (block + 1))
        reach = QUERY_ROWS * (block + 1)
        stacked = jnp.concatenate([query[RATIO * kv + i, at] for i in range(RATIO)], axis=0)
        scores = matmul_right_t(stacked, keys[kv, :reach])
        logits = scores.reshape(RATIO, QUERY_ROWS, reach) + bias[at, :reach][None]
        top = jnp.max(logits, axis=-1, keepdims=True)
        expo = jnp.exp(logits - top)
        total = jnp.sum(expo, axis=-1, keepdims=True)
        probs = (expo * (1.0 / total)).astype(low).reshape(RATIO * QUERY_ROWS, reach)
        log_total[:, at] = top + jnp.log(total)
        result = matmul(probs, values[kv, :reach]).astype(low)
        for i in range(RATIO):
            mixed[at, HD * i : HD * i + HD] = result[QUERY_ROWS * i : QUERY_ROWS * (i + 1)]


def attend_last_kernel(
    kv,
    bias,
    query,
    keys,
    values,
    hidden_in,
    gains,
    weights,
    *rest,
):
    before, (mixed, log_total, hidden_one, normed_two) = rest[:kv], rest[kv:]
    attend_kernel(kv, bias, query, keys, values, mixed, log_total)
    width = hidden_in.shape[1]
    every = jnp.concatenate([item[...] for item in before] + [mixed[...]], axis=1)
    hidden = hidden_in[...] + matmul(every, weights[0:width, 0:width])
    hidden_one[...] = hidden
    normed_two[...] = (hidden * norm_recip(hidden) * gains[1:2]).astype(low)


def feed_kernel(
    shards,
    part,
    hidden_one,
    normed_two,
    gains,
    lengths,
    cotangent,
    own_gate,
    own_up,
    own_down,
    pair_pieces,
    pair_other,
    down_pieces,
    down_other,
    result,
    grad_one,
    grad_gain,
    pair_keep,
    pair_send,
    down_keep,
    down_send,
    pair,
    down,
    hidden,
    grad_gate,
    grad_up,
    grad_pair,
    grad_down,
):
    core, x, y, shard = position()
    width = hidden_one.shape[1]
    down_part = own_down.shape[0]
    eighth = down_part // 8
    place(own_gate, pair.at[0, rows_at(part * shard, part)])
    place(own_up, pair.at[1, rows_at(part * shard, part)])
    for rel_core, source in enumerate((pair_pieces, pair_other)):
        for rel_x in range(2):
            block = 2 * relative(core, rel_core) + relative(x, rel_x)
            columns = rows_at(384 * block, 384, 128)
            for rel_y in range(2):
                at_y = relative(y, rel_y)
                for step in range(1, shards):
                    at = shard_at(shard, step, shards)
                    place(
                        source.at[rel_x, rel_y, step - 1],
                        pair.at[at_y, rows_at(part * at, part), columns],
                    )
    place(own_down, down.at[rows_at(down_part * shard, down_part)])
    for rel_core, source in enumerate((down_pieces, down_other)):
        for rel_x in range(2):
            block = 2 * relative(core, rel_core) + relative(x, rel_x)
            for rel_y in range(2):
                start = eighth * (2 * block + relative(y, rel_y))
                for step in range(1, shards):
                    at = shard_at(shard, step, shards)
                    place(
                        source.at[rel_y, rel_x, step - 1],
                        down.at[rows_at(down_part * at + start, eighth)],
                    )
    grad_low = cotangent[...]
    n2 = normed_two[...]
    hidden_width = pair.shape[2]
    for start in range(0, hidden_width, 512):
        at = slice(start, start + 512)
        gate = matmul(n2, pair[0, :, at])
        upward = matmul(n2, pair[1, :, at])
        grad_hidden = matmul_right_t(grad_low, down[at, :])
        sigma = jax.nn.sigmoid(gate)
        active = gate * sigma
        hidden[:, at] = (active * upward).astype(low)
        grad_up[:, at] = (grad_hidden * active).astype(low)
        grad_gate[:, at] = (grad_hidden * upward * (sigma + active * (1.0 - sigma))).astype(low)
    turned = n2.T
    for unit, grads in enumerate((grad_gate, grad_up)):
        for start in range(0, hidden_width, 512):
            at = slice(start, start + 512)
            grad_pair[unit, :, at] = matmul(turned, grads[:, at]).astype(low)
    for start in range(0, hidden_width, 512):
        at = slice(start, start + 512)
        grad_down[at, :] = matmul_left_t(hidden[:, at], grad_low).astype(low)
    for rel_core, (target, down_target) in enumerate(((pair_keep, down_keep), (pair_send, down_send))):
        at_core = relative(core, rel_core)
        for rel_x in range(2):
            at_x = relative(x, rel_x)
            block = 2 * at_core + at_x
            columns = rows_at(384 * block, 384, 128)
            for rel_y in range(2):
                at_y = relative(y, rel_y)
                for step in range(shards):
                    at = shard_at(shard, step, shards)
                    place(
                        grad_pair.at[at_y, rows_at(part * at, part), columns],
                        target.at[rel_x, rel_y, step],
                    )
                    place(
                        grad_down.at[rows_at(down_part * at + eighth * (2 * block + at_y), eighth)],
                        down_target.at[rel_y, rel_x, step],
                    )
    h1 = hidden_one[...]
    total = lengths[0, 0]
    for i in range(1, lengths.shape[1]):
        total = total + lengths[0, i]
    row = lax.broadcasted_iota(jnp.int32, h1.shape, 0)
    summed = h1 + matmul(hidden[...], down[...])
    result[...] = jnp.where(row < total, summed, 0.0).astype(low).T
    grad_normed = matmul_right_t(grad_gate[...], pair[0]) + matmul_right_t(grad_up[...], pair[1])
    grad_from, gain_row = norm_back(h1, norm_recip(h1), gains[1:2], grad_normed)
    grad_one[...] = grad_low.astype(f32) + grad_from
    grad_gain[...] = jnp.broadcast_to(gain_row, grad_gain.shape)


def back_heads_kernel(
    kv,
    bias,
    cosine,
    sine,
    weights,
    query,
    keys,
    values,
    mixed,
    log_total,
    grad_one,
    grad_turned,
    grad_values_out,
    grad_out,
    grad_mixed,
    grad_heads,
):
    rows, width = grad_one.shape
    span = RATIO * HD
    da = grad_one[...].astype(low)
    grad_mixed[...] = matmul_right_t(da, weights[span * kv : span * kv + span, 0:width]).astype(low)
    grad_out[...] = matmul_left_t(mixed[...], da).astype(low)
    grad_keys = [None] * (rows // QUERY_ROWS)
    grad_values = [None] * (rows // QUERY_ROWS)
    for block in range(rows // QUERY_ROWS):
        at = slice(QUERY_ROWS * block, QUERY_ROWS * (block + 1))
        reach = QUERY_ROWS * (block + 1)
        stacked = jnp.concatenate([query[RATIO * kv + i, at] for i in range(RATIO)], axis=0)
        grads = jnp.concatenate([grad_mixed[at, HD * i : HD * i + HD] for i in range(RATIO)], axis=0)
        out = jnp.concatenate([mixed[at, HD * i : HD * i + HD] for i in range(RATIO)], axis=0)
        delta = jnp.sum(grads.astype(f32) * out.astype(f32), axis=-1, keepdims=True)
        scores = matmul_right_t(stacked, keys[kv, :reach]).reshape(RATIO, QUERY_ROWS, reach)
        probs = jnp.exp(scores + bias[at, :reach][None] - log_total[:, at]).reshape(-1, reach)
        grad_probs = matmul_right_t(grads, values[kv, :reach])
        grad_scores = (probs * (grad_probs - delta)).astype(low)
        grad_query = matmul(grad_scores, keys[kv, :reach])
        for i in range(RATIO):
            grad_heads[at, HD * i : HD * i + HD] = (
                grad_query[QUERY_ROWS * i : QUERY_ROWS * (i + 1)] * HD**-0.5
            )
        key_part = matmul_left_t(grad_scores, stacked)
        value_part = matmul_left_t(probs.astype(low), grads)
        for j in range(block + 1):
            at_j = slice(QUERY_ROWS * j, QUERY_ROWS * (j + 1))
            if grad_keys[j] is None:
                grad_keys[j], grad_values[j] = key_part[at_j], value_part[at_j]
            else:
                grad_keys[j] = grad_keys[j] + key_part[at_j]
                grad_values[j] = grad_values[j] + value_part[at_j]
    grad_heads[:, span : span + HD] = jnp.concatenate(grad_keys, axis=0)
    grad_values_out[...] = jnp.concatenate(grad_values, axis=0).astype(low)
    for start in range(0, span + HD, 2 * HD):
        value = grad_heads[:, start : start + 2 * HD]
        turned = value * cosine[...] - swap_halves(value) * sine[...]
        grad_turned[:, start : start + 2 * HD] = turned.astype(low)


def back_last_kernel(
    shards,
    part,
    hidden_in,
    gains,
    weights,
    normed,
    grad_one,
    grad_gain_two,
    *rest,
):
    core, x, y, shard = position()
    rows, width = hidden_in.shape
    turned, values, outs = rest[0:KV], rest[KV : 2 * KV], rest[2 * KV : 3 * KV]
    grad_tokens, keep, send, grad_low, grad_weights = rest[3 * KV :]
    span = RATIO * HD
    grad_low[...] = jnp.concatenate(
        [jnp.zeros((rows, HD), low)]
        + [item[:, 0:span] for item in turned]
        + [item[:, span : span + HD] for item in turned]
        + [item[...] for item in values],
        axis=1,
    )
    normed_t = normed[...].T
    for start in range(0, 1024, 512):
        at = slice(start, start + 512)
        grad_weights[0:width, 512 + start : 1024 + start] = matmul(normed_t, grad_low[:, at]).astype(low)
    for kv in range(KV):
        grad_weights[span * kv : span * kv + span, 0:width] = outs[kv][...]
    grad_normed = matmul_right_t(grad_low[...], weights[0:width, 512:1536])
    hidden = hidden_in[...]
    grad_from, gain_row = norm_back(hidden, norm_recip(hidden), gains[0:1], grad_normed)
    grad_tokens[...] = (grad_one[...] + grad_from).astype(low).T
    row = lax.broadcasted_iota(jnp.int32, (16, width), 0)
    both = jnp.where(
        row == 0,
        jnp.broadcast_to(gain_row, (16, width)),
        jnp.where(row == 1, jnp.broadcast_to(grad_gain_two[0:1], (16, width)), 0.0),
    )
    grad_weights[width : width + 16, :] = jnp.zeros((16, grad_weights.shape[1]), low)
    grad_weights[width : width + 16, 0:width] = both.astype(low)
    for rel_core, target in enumerate((keep, send)):
        for rel_x in range(2):
            for rel_y in range(2):
                at_y = relative(y, rel_y)
                block = 2 * relative(core, rel_core) + relative(x, rel_x)
                columns = rows_at(384 * block, 384, 128)
                for step in range(shards):
                    at = shard_at(shard, step, shards)
                    piece = target.at[rel_y, rel_x, step]
                    place(
                        grad_weights.at[rows_at(part * at + 80 * at_y, 64), columns],
                        piece.at[pl.ds(0, 64)],
                    )
                    last = jnp.where(at_y == 0, part * at + 64, width)
                    place(grad_weights.at[rows_at(last, 16), columns], piece.at[pl.ds(64, 16)])


def finish_kernel(
    pair_pieces,
    pair_other,
    rest_pieces,
    rest_other,
    out_query,
    out_key,
    out_value,
    out_out,
    out_gain_one,
    out_gain_two,
    out_gate,
    out_up,
    out_down,
    attn,
    pair,
    down,
):
    core, x, y, shard = position()
    part, width = out_out.shape
    for rel_core, (p_from, r_from) in enumerate(((pair_pieces, rest_pieces), (pair_other, rest_other))):
        for rel_x in range(2):
            for rel_y in range(2):
                at_y = relative(y, rel_y)
                block = 2 * relative(core, rel_core) + relative(x, rel_x)
                columns = rows_at(384 * block, 384, 128)
                piece = r_from.at[rel_y, rel_x]
                place(p_from.at[rel_x, rel_y], pair.at[at_y, :, columns])
                place(piece.at[pl.ds(0, 80)], attn.at[rows_at(80 * at_y, 80), columns])
                place(piece.at[pl.ds(80, down.shape[1])], down.at[2 * block + at_y])
    kv_width = out_key.shape[1]
    out_out[...] = attn[0:part, 0:width].astype(f32)
    rest = attn[0:part, 512:].astype(f32)
    at = width - 512
    out_query[...] = rest[:, at : at + width]
    out_key[...] = rest[:, at + width : at + width + kv_width]
    out_value[...] = rest[:, at + width + kv_width :]
    gains = attn[part : part + 16, :].astype(f32)
    gains = pltpu.roll(gains, gains.shape[1] - part * shard, 1)
    out_gain_one[...] = gains[0:1, :part]
    out_gain_two[...] = gains[1:2, :part]
    out_gate[...] = pair[0].astype(f32)
    out_up[...] = pair[1].astype(f32)
    half = down.shape[1] // 2
    whole = [
        jnp.concatenate([down[i, :half], down[i, half:, : width - 384]], axis=1)
        for i in range(down.shape[0])
    ]
    out_down[...] = jnp.concatenate(whole, axis=0).T.astype(f32)


VM = pl.BlockSpec(memory_space=pltpu.VMEM)
SM = pl.BlockSpec(memory_space=pltpu.SMEM)


def shape(sizes, kind):
    return jax.ShapeDtypeStruct(tuple(sizes), kind)


def call(kernel, name, operands, in_specs, out_shape, out_specs, scratch, micros, room):
    moved = sum(item.size * item.dtype.itemsize for item in out_shape)
    return pl.pallas_call(
        kernel,
        name=name,
        in_specs=in_specs,
        out_shape=out_shape,
        out_specs=out_specs,
        scratch_shapes=scratch,
        cost_estimate=pl.CostEstimate(
            flops=int(micros * 1e7), bytes_accessed=moved, transcendentals=0
        ),
        compiler_params=pltpu.CompilerParams(vmem_limit_bytes=room << 20),
    )(*operands)


def local(
    replicas,
    shards,
    tokens,
    lengths,
    gain_attn,
    w_query,
    w_key,
    w_value,
    w_out,
    gain_mlp,
    w_gate,
    w_up,
    w_down,
    cotangent,
):
    rows, width = tokens.shape
    part = w_gate.shape[0]
    hidden_width = w_gate.shape[1]
    down_part = w_down.shape[0]
    eighth = down_part // 8
    packed = 2 * width + 2 * w_key.shape[1]
    own, attn_mine, pair_mine, down_mine, own_down = call(
        pack_kernel,
        "pack",
        (
            w_out,
            w_query,
            w_key,
            w_value,
            jnp.stack([gain_attn, gain_mlp]),
            w_gate,
            w_up,
            w_down.T,
        ),
        [VM] * 8,
        (
            shape((part + 16, packed), low),
            shape((80, 384), low),
            shape((part, 384), low),
            shape((eighth, width), low),
            shape((down_part, width), low),
        ),
        [VM] * 5,
        [],
        2,
        60,
    )
    attn_got = gather_shards(attn_mine, shards)
    table_cos, table_sin = rotation_tables(rows + 8, HD)
    cosine, sine, bias, hidden_in, scaled, grad_low = call(
        prepare_kernel,
        "prepare",
        (lengths, tokens.T, cotangent.T, table_cos, table_sin),
        [SM] + [VM] * 4,
        (
            shape((rows, 2 * HD), f32),
            shape((rows, 2 * HD), f32),
            shape((rows, rows), f32),
            shape((rows, width), f32),
            shape((rows, width), f32),
            shape((rows, width), low),
        ),
        [VM] * 6,
        [],
        5,
        24,
    )
    pair_got = gather_shards(after(pair_mine, scaled), shards)
    down_got = gather_shards(after(down_mine, attn_got), shards)
    attn_got = gather_bit(after(attn_got, scaled), 2, replicas)
    attn_got = gather_bit(after(attn_got, pair_got, down_got), 1, replicas)
    pair_got = gather_bit(pair_got, 2, replicas)
    attn_got = after(attn_got, pair_got)
    attn_other = flip(attn_got, 0, replicas)
    weights, gains, normed, query, keys, values = call(
        functools.partial(project_kernel, shards, part),
        "project",
        (scaled, cosine, sine, own, attn_got, attn_other),
        [VM, VM, VM, VM, VM, VM],
        (
            shape((width + 16 * shards, packed), low),
            shape((8, width), f32),
            shape((rows, width), low),
            shape((HEADS, rows, HD), low),
            shape((KV, rows, HD), low),
            shape((KV, rows, HD), low),
        ),
        [VM] * 6,
        [],
        5,
        24,
    )
    down_got = gather_bit(down_got, 1, replicas, normed)
    mixed, log_total = [], []
    for kv in range(KV):
        outs = [shape((rows, RATIO * HD), low), shape((RATIO, rows, 1), f32)]
        operands = (bias, query, keys, values)
        if kv < KV - 1:
            one, two = call(
                functools.partial(attend_kernel, kv),
                f"attend_{kv}",
                operands,
                [VM] * 4,
                outs,
                [VM] * 2,
                [],
                3,
                24,
            )
        else:
            down_got = gather_bit(down_got, 2, replicas, *mixed)
            operands += (after(hidden_in, down_got), gains, weights, *mixed)
            one, two, hidden_one, normed_two = call(
                functools.partial(attend_last_kernel, kv),
                f"attend_{kv}",
                operands,
                [VM] * len(operands),
                outs + [shape((rows, width), f32), shape((rows, width), low)],
                [VM] * 4,
                [],
                4,
                24,
            )
        mixed.append(one)
        log_total.append(two)
    pair_got = gather_bit(pair_got, 1, replicas, normed_two)
    pair_other = flip(pair_got, 0, replicas)
    down_other = flip(down_got, 0, replicas)
    pair_shape = shape((2, 2, shards, part, 384), low)
    down_shape = shape((2, 2, shards, eighth, width), low)
    result, grad_one, grad_gain_two, pair_keep, pair_send, down_keep, down_send = call(
        functools.partial(feed_kernel, shards, part),
        "feed",
        (
            hidden_one,
            normed_two,
            gains,
            lengths,
            grad_low,
            w_gate,
            w_up,
            own_down,
            pair_got,
            pair_other,
            down_got,
            down_other,
        ),
        [VM] * 3 + [SM, VM] + [VM] * 7,
        (
            shape((width, rows), low),
            shape((rows, width), f32),
            shape((8, width), f32),
            pair_shape,
            pair_shape,
            down_shape,
            down_shape,
        ),
        [VM] * 3 + [VM] * 4,
        [
            pltpu.VMEM((2, shards * part, hidden_width), low),
            pltpu.VMEM((hidden_width, width), low),
            pltpu.VMEM((rows, hidden_width), low),
            pltpu.VMEM((rows, hidden_width), low),
            pltpu.VMEM((rows, hidden_width), low),
            pltpu.VMEM((2, shards * part, hidden_width), low),
            pltpu.VMEM((hidden_width, width), low),
        ],
        19,
        48,
    )
    pair_sent = flip(pair_send, 0, replicas)
    down_sent = flip(down_send, 0, replicas)
    grad_turned, grad_values, grad_out = [], [], []
    for kv in range(KV):
        if kv == 1:
            pair_left = halve(pair_keep, after(pair_sent, grad_turned[0]), 1, replicas)
            down_left = halve(down_keep, after(down_sent, grad_turned[0]), 2, replicas)
            grad_one = after(grad_one, pair_sent, down_sent)
        one, two, three = call(
            functools.partial(back_heads_kernel, kv),
            f"back_{kv}",
            (bias, cosine, sine, weights, query, keys, values, mixed[kv], log_total[kv], grad_one),
            [VM] * 10,
            (
                shape((rows, RATIO * HD + HD), low),
                shape((rows, HD), low),
                shape((RATIO * HD, width), low),
            ),
            [VM] * 3,
            [pltpu.VMEM((rows, RATIO * HD), low), pltpu.VMEM((rows, RATIO * HD + HD), f32)],
            5,
            24,
        )
        grad_turned.append(one)
        grad_values.append(two)
        grad_out.append(three)
    attn_shape = shape((2, 2, shards, 80, 384), low)
    grad_tokens, attn_keep, attn_send = call(
        functools.partial(back_last_kernel, shards, part),
        "back_last",
        (
            hidden_in,
            gains,
            weights,
            normed,
            grad_one,
            grad_gain_two,
            *grad_turned,
            *grad_values,
            *grad_out,
        ),
        [VM] * (6 + 3 * KV),
        (shape((width, rows), low), attn_shape, attn_shape),
        [VM, VM, VM],
        [
            pltpu.VMEM((rows, 1024), low),
            pltpu.VMEM((width + 16, packed), low),
        ],
        6,
        24,
    )
    attn_left = halve(attn_keep, flip(after(attn_send, down_left[1], pair_left[1]), 0, replicas), 2, replicas)
    pair_left = halve(*pair_left, 2, replicas)
    down_left = halve(down_left[0], after(down_left[1], grad_tokens), 1, replicas)
    attn_left = halve(*attn_left, 1, replicas)
    down_total = scatter_over_shards(*down_left, shards, replicas)
    pair_total = scatter_over_shards(*pair_left, shards, replicas)
    attn_total = scatter_over_shards(*attn_left, shards, replicas)
    pair_pieces = spread(pair_total, (2, 1, 0), replicas)
    rest_pieces = spread(jnp.concatenate([attn_total, fold(down_total)]), (1, 2, 0), replicas)
    g_query, g_key, g_value, g_out, g_gain_one, g_gain_two, g_gate, g_up, g_down = call(
        finish_kernel,
        "finish",
        (*pair_pieces, *rest_pieces),
        [VM] * 4,
        (
            shape(w_query.shape, f32),
            shape(w_key.shape, f32),
            shape(w_value.shape, f32),
            shape(w_out.shape, f32),
            shape((1, part), f32),
            shape((1, part), f32),
            shape(w_gate.shape, f32),
            shape(w_up.shape, f32),
            shape((width, down_part), f32),
        ),
        [VM] * 9,
        [
            pltpu.VMEM((160, packed), low),
            pltpu.VMEM((2, part, hidden_width), low),
            pltpu.VMEM((8, 2 * eighth, 384), low),
        ],
        5,
        24,
    )
    return (
        result.T,
        grad_tokens.T,
        g_gain_one.reshape(part),
        g_query,
        g_key,
        g_value,
        g_out,
        g_gain_two.reshape(part),
        g_gate,
        g_up,
        g_down.T,
    )


def solution(mesh):
    in_specs = (
        P(("rep", "shard"), None),
        P(("rep", "shard"), None),
        P("shard"),
        P("shard", None),
        P("shard", None),
        P("shard", None),
        P("shard", None),
        P("shard"),
        P("shard", None),
        P("shard", None),
        P("shard", None),
        P(("rep", "shard"), None),
    )
    out_specs = (
        P(("rep", "shard"), None),
        P(("rep", "shard"), None),
        P("shard"),
        P("shard", None),
        P("shard", None),
        P("shard", None),
        P("shard", None),
        P("shard"),
        P("shard", None),
        P("shard", None),
        P("shard", None),
    )
    part = functools.partial(local, mesh.shape["rep"], mesh.shape["shard"])
    return jax.shard_map(part, mesh=mesh, in_specs=in_specs, out_specs=out_specs, check_vma=False)
```

```python
import functools

import jax
import jax.numpy as jnp
from jax import lax
from jax.experimental import pallas as pl
from jax.experimental.pallas import tpu as pltpu
from jax.sharding import PartitionSpec as P
import numpy as np

HEADS = 9
KV = 3
HD = 64
RATIO = HEADS // KV


norm_eps = 1e-05
rope_base = 100000.0
neg_fill = -1e30

low = jnp.bfloat16
f32 = jnp.float32
QUERY_ROWS = 128


def rotation_tables(places, head_size):
    half = head_size // 2
    freq = np.float32(rope_base) ** (-(np.arange(half, dtype=np.float32) * np.float32(2.0) / head_size))
    angle = np.arange(places, dtype=np.float32)[:, None] * freq.astype(np.float32)[None, :]
    return np.concatenate([np.cos(angle)] * 4, axis=1), np.concatenate([np.sin(angle)] * 4, axis=1)


def matmul(left, right):
    return jnp.dot(left, right, preferred_element_type=f32)


def matmul_left_t(left, right):
    return lax.dot_general(left, right, (((0,), (0,)), ((), ())), preferred_element_type=f32)


def matmul_right_t(left, right):
    return lax.dot_general(left, right, (((1,), (1,)), ((), ())), preferred_element_type=f32)


def flip(value, bit, replicas):
    return lax.ppermute(value, "rep", [(i, i ^ (1 << bit)) for i in range(replicas)])


def shift_from(value, step, shards):
    return lax.ppermute(value, "shard", [((s + step) % shards, s) for s in range(shards)])


def shift_to(value, step, shards):
    return lax.ppermute(value, "shard", [(s, (s + step) % shards) for s in range(shards)])


def add_low(left, right):
    return (left.astype(f32) + right.astype(f32)).astype(low)


def after(value, *others):
    return lax.optimization_barrier((value, *others))[0]


def gather_shards(mine, shards):
    return jnp.stack([shift_from(mine, step, shards) for step in range(1, shards)])


def gather_bit(got, bit, replicas, *later):
    other = flip(got, bit, replicas)
    return jnp.stack([after(got, *later) if later else got, other])


def halve(keep, other, bit, replicas):
    sent = flip(add_low(keep[1], other[1]), bit, replicas)
    return add_low(keep[0], other[0]), sent


def scatter_over_shards(keep, other, shards, replicas):
    parts = [add_low(keep[step], other[step]) for step in range(1, shards)]
    moved = [shift_to(part, step + 1, shards) for step, part in enumerate(parts)]
    total = keep[0].astype(f32) + other[0].astype(f32)
    for part in moved:
        total = total + part.astype(f32)
    total = total.astype(low)
    bit = 3
    while (1 << bit) < replicas:
        total = add_low(total, flip(total, bit, replicas))
        bit += 1
    return total


def spread(total, order, replicas):
    for bit in order[:-1]:
        total = jnp.stack([total, flip(total, bit, replicas)])
    return total, flip(total, order[-1], replicas)


def place(source, target):
    target[...] = source[...]


def rows_at(start, count, unit=16):
    return pl.ds(pl.multiple_of(start, unit), count)


def position():
    index = lax.axis_index("rep")
    return index % 2, index // 2 % 2, index // 4 % 2, lax.axis_index("shard")


def relative(bit, rel):
    return 1 - bit if rel else bit


def shard_at(shard, step, shards):
    at = shard + step
    return jnp.where(at >= shards, at - shards, at)


def swap_halves(values):
    lane = lax.broadcasted_iota(jnp.int32, values.shape, 1)
    return jnp.where(
        lane % HD < HD // 2,
        pltpu.roll(values, 2 * HD - HD // 2, 1),
        pltpu.roll(values, HD // 2, 1),
    )


def norm_recip(values):
    return lax.rsqrt(jnp.mean(values * values, axis=-1, keepdims=True) + norm_eps)


def norm_back(values, recip, gain, grad_normed):
    scaled = grad_normed * gain
    inner = jnp.mean(scaled * values, axis=-1, keepdims=True)
    grad_values = recip * scaled - values * (recip * recip * recip * inner)
    grad_gain = jnp.sum(grad_normed * values * recip, axis=0, keepdims=True)
    return (grad_values, grad_gain)


def pack_kernel(
    w_out,
    w_query,
    w_key,
    w_value,
    gain_one,
    gain_two,
    gate,
    up,
    down_t,
    own,
    attn_mine,
    pair_mine,
    down_mine,
    down,
):
    core, x, y, shard = position()
    block = 2 * core + x
    part = gate.shape[0]
    packed = own.shape[1]
    columns = rows_at(384 * block, 384, 128)
    pair_mine[...] = jnp.where(y == 0, gate[:, columns], up[:, columns])
    own[0:part] = jnp.concatenate([w_out[...], w_query[...], w_key[...], w_value[...]], axis=1)
    row = lax.broadcasted_iota(jnp.int32, (16, part), 0)
    gains = jnp.where(
        row == 0,
        jnp.broadcast_to(gain_one[...].astype(f32), row.shape),
        jnp.where(row == 1, jnp.broadcast_to(gain_two[...].astype(f32), row.shape), 0.0),
    )
    gains = jnp.concatenate([gains, jnp.zeros((16, packed - part), f32)], axis=1)
    own[part : part + 16] = pltpu.roll(gains, part * shard, 1).astype(low)
    attn_mine[...] = own[rows_at(80 * y, 80), columns]
    down[...] = down_t[...].T
    eighth = down_mine.shape[0]
    down_mine[...] = down[rows_at(eighth * (2 * block + y), eighth), :]


def fold(value):
    rest = value[..., 384:]
    pad = [(0, 0)] * (value.ndim - 1) + [(0, 384 - rest.shape[-1])]
    return jnp.concatenate([value[..., :384], jnp.pad(rest, pad)], axis=-2)


def prepare_kernel(
    lengths,
    tokens_t,
    cotangent_t,
    table_cos,
    table_sin,
    cosine,
    sine,
    bias,
    hidden,
    scaled,
    grad_low,
):
    rows = hidden.shape[0]
    count = lengths.shape[1]
    ends = []
    for i in range(count):
        ends.append(lengths[0, i] + (ends[-1] if ends else 0))
    place = lax.broadcasted_iota(jnp.int32, cosine.shape, 0)
    start_cos = jnp.broadcast_to(table_cos[0:1], cosine.shape)
    start_sin = jnp.broadcast_to(table_sin[0:1], cosine.shape)
    for end in ends:
        start_cos = jnp.where(place >= end, table_cos[pl.ds(end, 1)], start_cos)
        start_sin = jnp.where(place >= end, table_sin[pl.ds(end, 1)], start_sin)
    cos, sin = table_cos[0:rows], table_sin[0:rows]
    cosine[...] = cos * start_cos + sin * start_sin
    signed = sin * start_cos - cos * start_sin
    lane = lax.broadcasted_iota(jnp.int32, cosine.shape, 1)
    sine[...] = jnp.where(lane % HD < HD // 2, -signed, signed)
    query = lax.broadcasted_iota(jnp.int32, bias.shape, 0)
    key = lax.broadcasted_iota(jnp.int32, bias.shape, 1)
    allowed = query >= key
    for end in ends:
        allowed = allowed & ((query < end) | (key >= end))
    bias[...] = jnp.where(allowed, 0.0, neg_fill)
    values = tokens_t[...].T.astype(f32)
    hidden[...] = values
    scaled[...] = values * norm_recip(values)
    wide = lax.broadcasted_iota(jnp.int32, grad_low.shape, 0)
    grad_low[...] = jnp.where(wide < ends[-1], cotangent_t[...].T, jnp.zeros((), low))


def project_kernel(
    shards,
    part,
    scaled,
    cosine,
    sine,
    own,
    pieces,
    other,
    weights,
    gains,
    normed,
    query,
    keys,
    values,
):
    core, x, y, shard = position()
    width = scaled.shape[1]
    place(own.at[pl.ds(0, part)], weights.at[rows_at(part * shard, part)])
    place(own.at[pl.ds(part, 16)], weights.at[rows_at(width + 16 * shard, 16)])
    for rel_core, source in enumerate((pieces, other)):
        for rel_x in range(2):
            for rel_y in range(2):
                at_y = relative(y, rel_y)
                block = 2 * relative(core, rel_core) + relative(x, rel_x)
                columns = rows_at(384 * block, 384, 128)
                for step in range(1, shards):
                    at = shard_at(shard, step, shards)
                    piece = source.at[rel_x, rel_y, step - 1]
                    place(
                        piece.at[pl.ds(0, 64)], weights.at[rows_at(part * at + 80 * at_y, 64), columns]
                    )
                    last = jnp.where(at_y == 0, part * at + 64, width + 16 * at)
                    place(piece.at[pl.ds(64, 16)], weights.at[rows_at(last, 16), columns])
    total = sum(
        weights[width + 16 * s : width + 16 * s + 16, :width].astype(f32) for s in range(shards)
    )
    gains[...] = total[:8]
    n1 = (scaled[...] * total[0:1]).astype(low)
    normed[...] = n1
    for block in range(8):
        start = 512 + 128 * block
        result = matmul(n1, weights[0:width, start : start + 128])
        heads = [2 * block - 1, 2 * block]
        if heads[0] < HEADS + KV:
            turned = result * cosine[...] + swap_halves(result) * sine[...]
        for side, head in enumerate(heads):
            lanes = slice(HD * side, HD * side + HD)
            if head < 0:
                continue
            if head < HEADS:
                query[head] = (turned[:, lanes] * HD**-0.5).astype(low)
            elif head < HEADS + KV:
                keys[head - HEADS] = turned[:, lanes].astype(low)
            else:
                values[head - HEADS - KV] = result[:, lanes].astype(low)


def attend_kernel(kv, bias, query, keys, values, mixed, log_total):
    rows = bias.shape[0]
    for block in range(rows // QUERY_ROWS):
        at = slice(QUERY_ROWS * block, QUERY_ROWS * (block + 1))
        reach = QUERY_ROWS * (block + 1)
        stacked = jnp.concatenate([query[RATIO * kv + i, at] for i in range(RATIO)], axis=0)
        scores = matmul_right_t(stacked, keys[kv, :reach])
        logits = scores.reshape(RATIO, QUERY_ROWS, reach) + bias[at, :reach][None]
        top = jnp.max(logits, axis=-1, keepdims=True)
        expo = jnp.exp(logits - top)
        total = jnp.sum(expo, axis=-1, keepdims=True)
        probs = (expo * (1.0 / total)).astype(low).reshape(RATIO * QUERY_ROWS, reach)
        log_total[:, at] = top + jnp.log(total)
        result = matmul(probs, values[kv, :reach]).astype(low)
        for i in range(RATIO):
            mixed[at, HD * i : HD * i + HD] = result[QUERY_ROWS * i : QUERY_ROWS * (i + 1)]


def attend_last_kernel(
    kv,
    bias,
    query,
    keys,
    values,
    hidden_in,
    gains,
    weights,
    *rest,
):
    before, (mixed, log_total, hidden_one, normed_two) = rest[:kv], rest[kv:]
    attend_kernel(kv, bias, query, keys, values, mixed, log_total)
    width = hidden_in.shape[1]
    every = jnp.concatenate([item[...] for item in before] + [mixed[...]], axis=1)
    hidden = hidden_in[...] + matmul(every, weights[0:width, 0:width])
    hidden_one[...] = hidden
    normed_two[...] = (hidden * norm_recip(hidden) * gains[1:2]).astype(low)


def feed_kernel(
    shards,
    part,
    hidden_one,
    normed_two,
    gains,
    lengths,
    cotangent,
    own_gate,
    own_up,
    own_down,
    pair_pieces,
    pair_other,
    down_pieces,
    down_other,
    result,
    grad_one,
    grad_gain,
    pair_keep,
    pair_send,
    down_keep,
    down_send,
    pair,
    down,
    hidden,
    grad_gate,
    grad_up,
    grad_pair,
    grad_down,
):
    core, x, y, shard = position()
    width = hidden_one.shape[1]
    down_part = own_down.shape[0]
    eighth = down_part // 8
    place(own_gate, pair.at[0, rows_at(part * shard, part)])
    place(own_up, pair.at[1, rows_at(part * shard, part)])
    for rel_core, source in enumerate((pair_pieces, pair_other)):
        for rel_x in range(2):
            block = 2 * relative(core, rel_core) + relative(x, rel_x)
            columns = rows_at(384 * block, 384, 128)
            for rel_y in range(2):
                at_y = relative(y, rel_y)
                for step in range(1, shards):
                    at = shard_at(shard, step, shards)
                    place(
                        source.at[rel_x, rel_y, step - 1],
                        pair.at[at_y, rows_at(part * at, part), columns],
                    )
    place(own_down, down.at[rows_at(down_part * shard, down_part)])
    for rel_core, source in enumerate((down_pieces, down_other)):
        for rel_x in range(2):
            block = 2 * relative(core, rel_core) + relative(x, rel_x)
            for rel_y in range(2):
                start = eighth * (2 * block + relative(y, rel_y))
                for step in range(1, shards):
                    at = shard_at(shard, step, shards)
                    place(
                        source.at[rel_y, rel_x, step - 1],
                        down.at[rows_at(down_part * at + start, eighth)],
                    )
    grad_low = cotangent[...]
    n2 = normed_two[...]
    hidden_width = pair.shape[2]
    for start in range(0, hidden_width, 512):
        at = slice(start, start + 512)
        gate = matmul(n2, pair[0, :, at])
        upward = matmul(n2, pair[1, :, at])
        grad_hidden = matmul_right_t(grad_low, down[at, :])
        sigma = jax.nn.sigmoid(gate)
        active = gate * sigma
        hidden[:, at] = (active * upward).astype(low)
        grad_up[:, at] = (grad_hidden * active).astype(low)
        grad_gate[:, at] = (grad_hidden * upward * (sigma + active * (1.0 - sigma))).astype(low)
    turned = n2.T
    for unit, grads in enumerate((grad_gate, grad_up)):
        for start in range(0, hidden_width, 512):
            at = slice(start, start + 512)
            grad_pair[unit, :, at] = matmul(turned, grads[:, at]).astype(low)
    for start in range(0, hidden_width, 512):
        at = slice(start, start + 512)
        grad_down[at, :] = matmul_left_t(hidden[:, at], grad_low).astype(low)
    for rel_core, (target, down_target) in enumerate(((pair_keep, down_keep), (pair_send, down_send))):
        at_core = relative(core, rel_core)
        for rel_x in range(2):
            at_x = relative(x, rel_x)
            block = 2 * at_core + at_x
            columns = rows_at(384 * block, 384, 128)
            for rel_y in range(2):
                at_y = relative(y, rel_y)
                for step in range(shards):
                    at = shard_at(shard, step, shards)
                    place(
                        grad_pair.at[at_y, rows_at(part * at, part), columns],
                        target.at[rel_x, rel_y, step],
                    )
                    place(
                        grad_down.at[rows_at(down_part * at + eighth * (2 * block + at_y), eighth)],
                        down_target.at[rel_y, rel_x, step],
                    )
    h1 = hidden_one[...]
    total = lengths[0, 0]
    for i in range(1, lengths.shape[1]):
        total = total + lengths[0, i]
    row = lax.broadcasted_iota(jnp.int32, h1.shape, 0)
    summed = h1 + matmul(hidden[...], down[...])
    result[...] = jnp.where(row < total, summed, 0.0).astype(low).T
    grad_normed = matmul_right_t(grad_gate[...], pair[0]) + matmul_right_t(grad_up[...], pair[1])
    grad_from, gain_row = norm_back(h1, norm_recip(h1), gains[1:2], grad_normed)
    grad_one[...] = grad_low.astype(f32) + grad_from
    grad_gain[...] = jnp.broadcast_to(gain_row, grad_gain.shape)


def back_heads_kernel(
    kv,
    bias,
    cosine,
    sine,
    weights,
    query,
    keys,
    values,
    mixed,
    log_total,
    grad_one,
    grad_turned,
    grad_values_out,
    grad_out,
    grad_mixed,
    grad_heads,
):
    rows, width = grad_one.shape
    span = RATIO * HD
    da = grad_one[...].astype(low)
    grad_mixed[...] = matmul_right_t(da, weights[span * kv : span * kv + span, 0:width]).astype(low)
    grad_out[...] = matmul_left_t(mixed[...], da).astype(low)
    grad_keys = [None] * (rows // QUERY_ROWS)
    grad_values = [None] * (rows // QUERY_ROWS)
    for block in range(rows // QUERY_ROWS):
        at = slice(QUERY_ROWS * block, QUERY_ROWS * (block + 1))
        reach = QUERY_ROWS * (block + 1)
        stacked = jnp.concatenate([query[RATIO * kv + i, at] for i in range(RATIO)], axis=0)
        grads = jnp.concatenate([grad_mixed[at, HD * i : HD * i + HD] for i in range(RATIO)], axis=0)
        out = jnp.concatenate([mixed[at, HD * i : HD * i + HD] for i in range(RATIO)], axis=0)
        delta = jnp.sum(grads.astype(f32) * out.astype(f32), axis=-1, keepdims=True)
        scores = matmul_right_t(stacked, keys[kv, :reach]).reshape(RATIO, QUERY_ROWS, reach)
        probs = jnp.exp(scores + bias[at, :reach][None] - log_total[:, at]).reshape(-1, reach)
        grad_probs = matmul_right_t(grads, values[kv, :reach])
        grad_scores = (probs * (grad_probs - delta)).astype(low)
        grad_query = matmul(grad_scores, keys[kv, :reach])
        for i in range(RATIO):
            grad_heads[at, HD * i : HD * i + HD] = (
                grad_query[QUERY_ROWS * i : QUERY_ROWS * (i + 1)] * HD**-0.5
            )
        key_part = matmul_left_t(grad_scores, stacked)
        value_part = matmul_left_t(probs.astype(low), grads)
        for j in range(block + 1):
            at_j = slice(QUERY_ROWS * j, QUERY_ROWS * (j + 1))
            if grad_keys[j] is None:
                grad_keys[j], grad_values[j] = key_part[at_j], value_part[at_j]
            else:
                grad_keys[j] = grad_keys[j] + key_part[at_j]
                grad_values[j] = grad_values[j] + value_part[at_j]
    grad_heads[:, span : span + HD] = jnp.concatenate(grad_keys, axis=0)
    grad_values_out[...] = jnp.concatenate(grad_values, axis=0).astype(low)
    for start in range(0, span + HD, 2 * HD):
        value = grad_heads[:, start : start + 2 * HD]
        turned = value * cosine[...] - swap_halves(value) * sine[...]
        grad_turned[:, start : start + 2 * HD] = turned.astype(low)


def back_last_kernel(
    shards,
    part,
    hidden_in,
    gains,
    weights,
    normed,
    grad_one,
    grad_gain_two,
    *rest,
):
    core, x, y, shard = position()
    rows, width = hidden_in.shape
    turned, values, outs = rest[0:KV], rest[KV : 2 * KV], rest[2 * KV : 3 * KV]
    grad_tokens, keep, send, grad_low, grad_weights = rest[3 * KV :]
    span = RATIO * HD
    grad_low[...] = jnp.concatenate(
        [jnp.zeros((rows, HD), low)]
        + [item[:, 0:span] for item in turned]
        + [item[:, span : span + HD] for item in turned]
        + [item[...] for item in values],
        axis=1,
    )
    normed_t = normed[...].T
    for start in range(0, 1024, 512):
        at = slice(start, start + 512)
        grad_weights[0:width, 512 + start : 1024 + start] = matmul(normed_t, grad_low[:, at]).astype(low)
    for kv in range(KV):
        grad_weights[span * kv : span * kv + span, 0:width] = outs[kv][...]
    grad_normed = matmul_right_t(grad_low[...], weights[0:width, 512:1536])
    hidden = hidden_in[...]
    grad_from, gain_row = norm_back(hidden, norm_recip(hidden), gains[0:1], grad_normed)
    grad_tokens[...] = (grad_one[...] + grad_from).astype(low).T
    row = lax.broadcasted_iota(jnp.int32, (16, width), 0)
    both = jnp.where(
        row == 0,
        jnp.broadcast_to(gain_row, (16, width)),
        jnp.where(row == 1, jnp.broadcast_to(grad_gain_two[0:1], (16, width)), 0.0),
    )
    grad_weights[width : width + 16, :] = jnp.zeros((16, grad_weights.shape[1]), low)
    grad_weights[width : width + 16, 0:width] = both.astype(low)
    for rel_core, target in enumerate((keep, send)):
        for rel_x in range(2):
            for rel_y in range(2):
                at_y = relative(y, rel_y)
                block = 2 * relative(core, rel_core) + relative(x, rel_x)
                columns = rows_at(384 * block, 384, 128)
                for step in range(shards):
                    at = shard_at(shard, step, shards)
                    piece = target.at[rel_y, rel_x, step]
                    place(
                        grad_weights.at[rows_at(part * at + 80 * at_y, 64), columns],
                        piece.at[pl.ds(0, 64)],
                    )
                    last = jnp.where(at_y == 0, part * at + 64, width)
                    place(grad_weights.at[rows_at(last, 16), columns], piece.at[pl.ds(64, 16)])


def finish_kernel(
    pair_pieces,
    pair_other,
    rest_pieces,
    rest_other,
    out_query,
    out_key,
    out_value,
    out_out,
    out_gain_one,
    out_gain_two,
    out_gate,
    out_up,
    out_down,
    attn,
    pair,
    down,
):
    core, x, y, shard = position()
    part, width = out_out.shape
    for rel_core, (p_from, r_from) in enumerate(((pair_pieces, rest_pieces), (pair_other, rest_other))):
        for rel_x in range(2):
            for rel_y in range(2):
                at_y = relative(y, rel_y)
                block = 2 * relative(core, rel_core) + relative(x, rel_x)
                columns = rows_at(384 * block, 384, 128)
                piece = r_from.at[rel_y, rel_x]
                place(p_from.at[rel_x, rel_y], pair.at[at_y, :, columns])
                place(piece.at[pl.ds(0, 80)], attn.at[rows_at(80 * at_y, 80), columns])
                place(piece.at[pl.ds(80, down.shape[1])], down.at[2 * block + at_y])
    kv_width = out_key.shape[1]
    out_out[...] = attn[0:part, 0:width].astype(f32)
    rest = attn[0:part, 512:].astype(f32)
    at = width - 512
    out_query[...] = rest[:, at : at + width]
    out_key[...] = rest[:, at + width : at + width + kv_width]
    out_value[...] = rest[:, at + width + kv_width :]
    gains = attn[part : part + 16, :].astype(f32)
    gains = pltpu.roll(gains, gains.shape[1] - part * shard, 1)
    out_gain_one[...] = gains[0:1, :part]
    out_gain_two[...] = gains[1:2, :part]
    out_gate[...] = pair[0].astype(f32)
    out_up[...] = pair[1].astype(f32)
    half = down.shape[1] // 2
    whole = [
        jnp.concatenate([down[i, :half], down[i, half:, : width - 384]], axis=1)
        for i in range(down.shape[0])
    ]
    out_down[...] = jnp.concatenate(whole, axis=0).T.astype(f32)


VM = pl.BlockSpec(memory_space=pltpu.VMEM)
SM = pl.BlockSpec(memory_space=pltpu.SMEM)


def shape(sizes, kind):
    return jax.ShapeDtypeStruct(tuple(sizes), kind)


def call(kernel, name, operands, in_specs, out_shape, out_specs, scratch, micros, room):
    moved = sum(item.size * item.dtype.itemsize for item in out_shape)
    return pl.pallas_call(
        kernel,
        name=name,
        in_specs=in_specs,
        out_shape=out_shape,
        out_specs=out_specs,
        scratch_shapes=scratch,
        cost_estimate=pl.CostEstimate(
            flops=int(micros * 1e7), bytes_accessed=moved, transcendentals=0
        ),
        compiler_params=pltpu.CompilerParams(vmem_limit_bytes=room << 20),
    )(*operands)


def local(
    replicas,
    shards,
    tokens,
    lengths,
    gain_attn,
    w_query,
    w_key,
    w_value,
    w_out,
    gain_mlp,
    w_gate,
    w_up,
    w_down,
    cotangent,
):
    rows, width = tokens.shape
    part = w_gate.shape[0]
    hidden_width = w_gate.shape[1]
    down_part = w_down.shape[0]
    eighth = down_part // 8
    packed = 2 * width + 2 * w_key.shape[1]
    own, attn_mine, pair_mine, down_mine, own_down = call(
        pack_kernel,
        "pack",
        (
            w_out,
            w_query,
            w_key,
            w_value,
            gain_attn[None],
            gain_mlp[None],
            w_gate,
            w_up,
            w_down.T,
        ),
        [VM] * 9,
        (
            shape((part + 16, packed), low),
            shape((80, 384), low),
            shape((part, 384), low),
            shape((eighth, width), low),
            shape((down_part, width), low),
        ),
        [VM] * 5,
        [],
        2,
        60,
    )
    attn_got = gather_shards(attn_mine, shards)
    table_cos, table_sin = rotation_tables(rows + 8, HD)
    cosine, sine, bias, hidden_in, scaled, grad_low = call(
        prepare_kernel,
        "prepare",
        (lengths, tokens.T, cotangent.T, table_cos, table_sin),
        [SM] + [VM] * 4,
        (
            shape((rows, 2 * HD), f32),
            shape((rows, 2 * HD), f32),
            shape((rows, rows), f32),
            shape((rows, width), f32),
            shape((rows, width), f32),
            shape((rows, width), low),
        ),
        [VM] * 6,
        [],
        5,
        24,
    )
    pair_got = gather_shards(after(pair_mine, scaled), shards)
    down_got = gather_shards(after(down_mine, attn_got), shards)
    attn_got = gather_bit(after(attn_got, scaled), 2, replicas)
    attn_got = gather_bit(after(attn_got, pair_got, down_got), 1, replicas)
    pair_got = gather_bit(pair_got, 2, replicas)
    attn_got = after(attn_got, pair_got)
    attn_other = flip(attn_got, 0, replicas)
    weights, gains, normed, query, keys, values = call(
        functools.partial(project_kernel, shards, part),
        "project",
        (scaled, cosine, sine, own, attn_got, attn_other),
        [VM, VM, VM, VM, VM, VM],
        (
            shape((width + 16 * shards, packed), low),
            shape((8, width), f32),
            shape((rows, width), low),
            shape((HEADS, rows, HD), low),
            shape((KV, rows, HD), low),
            shape((KV, rows, HD), low),
        ),
        [VM] * 6,
        [],
        5,
        24,
    )
    down_got = gather_bit(down_got, 1, replicas, normed)
    mixed, log_total = [], []
    for kv in range(KV):
        outs = [shape((rows, RATIO * HD), low), shape((RATIO, rows, 1), f32)]
        operands = (bias, query, keys, values)
        if kv < KV - 1:
            one, two = call(
                functools.partial(attend_kernel, kv),
                f"attend_{kv}",
                operands,
                [VM] * 4,
                outs,
                [VM] * 2,
                [],
                3,
                24,
            )
        else:
            down_got = gather_bit(down_got, 2, replicas, *mixed)
            operands += (after(hidden_in, down_got), gains, weights, *mixed)
            one, two, hidden_one, normed_two = call(
                functools.partial(attend_last_kernel, kv),
                f"attend_{kv}",
                operands,
                [VM] * len(operands),
                outs + [shape((rows, width), f32), shape((rows, width), low)],
                [VM] * 4,
                [],
                4,
                24,
            )
        mixed.append(one)
        log_total.append(two)
    pair_got = gather_bit(pair_got, 1, replicas, normed_two)
    pair_other = flip(pair_got, 0, replicas)
    down_other = flip(down_got, 0, replicas)
    pair_shape = shape((2, 2, shards, part, 384), low)
    down_shape = shape((2, 2, shards, eighth, width), low)
    result, grad_one, grad_gain_two, pair_keep, pair_send, down_keep, down_send = call(
        functools.partial(feed_kernel, shards, part),
        "feed",
        (
            hidden_one,
            normed_two,
            gains,
            lengths,
            grad_low,
            w_gate,
            w_up,
            own_down,
            pair_got,
            pair_other,
            down_got,
            down_other,
        ),
        [VM] * 3 + [SM, VM] + [VM] * 7,
        (
            shape((width, rows), low),
            shape((rows, width), f32),
            shape((8, width), f32),
            pair_shape,
            pair_shape,
            down_shape,
            down_shape,
        ),
        [VM] * 3 + [VM] * 4,
        [
            pltpu.VMEM((2, shards * part, hidden_width), low),
            pltpu.VMEM((hidden_width, width), low),
            pltpu.VMEM((rows, hidden_width), low),
            pltpu.VMEM((rows, hidden_width), low),
            pltpu.VMEM((rows, hidden_width), low),
            pltpu.VMEM((2, shards * part, hidden_width), low),
            pltpu.VMEM((hidden_width, width), low),
        ],
        19,
        38,
    )
    pair_sent = flip(pair_send, 0, replicas)
    down_sent = flip(down_send, 0, replicas)
    grad_turned, grad_values, grad_out = [], [], []
    for kv in range(KV):
        if kv == 1:
            pair_left = halve(pair_keep, after(pair_sent, grad_turned[0]), 1, replicas)
            down_left = halve(down_keep, after(down_sent, grad_turned[0]), 2, replicas)
            grad_one = after(grad_one, pair_sent, down_sent)
        one, two, three = call(
            functools.partial(back_heads_kernel, kv),
            f"back_{kv}",
            (bias, cosine, sine, weights, query, keys, values, mixed[kv], log_total[kv], grad_one),
            [VM] * 10,
            (
                shape((rows, RATIO * HD + HD), low),
                shape((rows, HD), low),
                shape((RATIO * HD, width), low),
            ),
            [VM] * 3,
            [pltpu.VMEM((rows, RATIO * HD), low), pltpu.VMEM((rows, RATIO * HD + HD), f32)],
            5,
            24,
        )
        grad_turned.append(one)
        grad_values.append(two)
        grad_out.append(three)
    attn_shape = shape((2, 2, shards, 80, 384), low)
    grad_tokens, attn_keep, attn_send = call(
        functools.partial(back_last_kernel, shards, part),
        "back_last",
        (
            hidden_in,
            gains,
            weights,
            normed,
            grad_one,
            grad_gain_two,
            *grad_turned,
            *grad_values,
            *grad_out,
        ),
        [VM] * (6 + 3 * KV),
        (shape((width, rows), low), attn_shape, attn_shape),
        [VM, VM, VM],
        [
            pltpu.VMEM((rows, 1024), low),
            pltpu.VMEM((width + 16, packed), low),
        ],
        6,
        24,
    )
    attn_left = halve(attn_keep, flip(after(attn_send, down_left[1], pair_left[1]), 0, replicas), 2, replicas)
    pair_left = halve(*pair_left, 2, replicas)
    down_left = halve(down_left[0], after(down_left[1], grad_tokens), 1, replicas)
    attn_left = halve(attn_left[0], after(attn_left[1], pair_left[1]), 1, replicas)
    down_total = scatter_over_shards(*down_left, shards, replicas)
    pair_total = scatter_over_shards(*pair_left, shards, replicas)
    attn_total = scatter_over_shards(*attn_left, shards, replicas)
    pair_pieces = spread(pair_total, (2, 1, 0), replicas)
    rest_pieces = spread(jnp.concatenate([attn_total, fold(down_total)]), (1, 2, 0), replicas)
    g_query, g_key, g_value, g_out, g_gain_one, g_gain_two, g_gate, g_up, g_down = call(
        finish_kernel,
        "finish",
        (*pair_pieces, *rest_pieces),
        [VM] * 4,
        (
            shape(w_query.shape, f32),
            shape(w_key.shape, f32),
            shape(w_value.shape, f32),
            shape(w_out.shape, f32),
            shape((1, part), f32),
            shape((1, part), f32),
            shape(w_gate.shape, f32),
            shape(w_up.shape, f32),
            shape((width, down_part), f32),
        ),
        [VM] * 9,
        [
            pltpu.VMEM((160, packed), low),
            pltpu.VMEM((2, part, hidden_width), low),
            pltpu.VMEM((8, 2 * eighth, 384), low),
        ],
        5,
        24,
    )
    return (
        result.T,
        grad_tokens.T,
        g_gain_one.reshape(part),
        g_query,
        g_key,
        g_value,
        g_out,
        g_gain_two.reshape(part),
        g_gate,
        g_up,
        g_down.T,
    )


def solution(mesh):
    in_specs = (
        P(("rep", "shard"), None),
        P(("rep", "shard"), None),
        P("shard"),
        P("shard", None),
        P("shard", None),
        P("shard", None),
        P("shard", None),
        P("shard"),
        P("shard", None),
        P("shard", None),
        P("shard", None),
        P(("rep", "shard"), None),
    )
    out_specs = (
        P(("rep", "shard"), None),
        P(("rep", "shard"), None),
        P("shard"),
        P("shard", None),
        P("shard", None),
        P("shard", None),
        P("shard", None),
        P("shard"),
        P("shard", None),
        P("shard", None),
        P("shard", None),
    )
    part = functools.partial(local, mesh.shape["rep"], mesh.shape["shard"])
    return jax.shard_map(part, mesh=mesh, in_specs=in_specs, out_specs=out_specs, check_vma=False)
```

```python
import functools

import jax
import jax.numpy as jnp
from jax import lax
from jax.experimental import pallas as pl
from jax.experimental.pallas import tpu as pltpu
from jax.sharding import PartitionSpec as P
import numpy as np

HEADS = 9
KV = 3
HD = 64
RATIO = HEADS // KV


norm_eps = 1e-05
rope_base = 100000.0
neg_fill = -1e30

low = jnp.bfloat16
f32 = jnp.float32
QUERY_ROWS = 128


def rotation_tables(places, head_size):
    half = head_size // 2
    freq = np.float32(rope_base) ** (-(np.arange(half, dtype=np.float32) * np.float32(2.0) / head_size))
    angle = np.arange(places, dtype=np.float32)[:, None] * freq.astype(np.float32)[None, :]
    return np.concatenate([np.cos(angle)] * 4, axis=1), np.concatenate([np.sin(angle)] * 4, axis=1)


def matmul(left, right):
    return jnp.dot(left, right, preferred_element_type=f32)


def matmul_left_t(left, right):
    return lax.dot_general(left, right, (((0,), (0,)), ((), ())), preferred_element_type=f32)


def matmul_right_t(left, right):
    return lax.dot_general(left, right, (((1,), (1,)), ((), ())), preferred_element_type=f32)


def flip(value, bit, replicas):
    return lax.ppermute(value, "rep", [(i, i ^ (1 << bit)) for i in range(replicas)])


def shift_from(value, step, shards):
    return lax.ppermute(value, "shard", [((s + step) % shards, s) for s in range(shards)])


def shift_to(value, step, shards):
    return lax.ppermute(value, "shard", [(s, (s + step) % shards) for s in range(shards)])


def add_low(left, right):
    return (left.astype(f32) + right.astype(f32)).astype(low)


def after(value, *others):
    return lax.optimization_barrier((value, *others))[0]


def gather_shards(mine, shards):
    return jnp.stack([shift_from(mine, step, shards) for step in range(1, shards)])


def gather_bit(got, bit, replicas, *later):
    other = flip(got, bit, replicas)
    return jnp.stack([after(got, *later) if later else got, other])


def halve(keep, other, bit, replicas):
    sent = flip(add_low(keep[1], other[1]), bit, replicas)
    return add_low(keep[0], other[0]), sent


def scatter_over_shards(keep, other, shards, replicas):
    parts = [add_low(keep[step], other[step]) for step in range(1, shards)]
    moved = [shift_to(part, step + 1, shards) for step, part in enumerate(parts)]
    total = keep[0].astype(f32) + other[0].astype(f32)
    for part in moved:
        total = total + part.astype(f32)
    total = total.astype(low)
    bit = 3
    while (1 << bit) < replicas:
        total = add_low(total, flip(total, bit, replicas))
        bit += 1
    return total


def spread(total, order, replicas):
    for bit in order[:-1]:
        total = jnp.stack([total, flip(total, bit, replicas)])
    return total, flip(total, order[-1], replicas)


def place(source, target):
    target[...] = source[...]


def rows_at(start, count, unit=16):
    return pl.ds(pl.multiple_of(start, unit), count)


def position():
    index = lax.axis_index("rep")
    return index % 2, index // 2 % 2, index // 4 % 2, lax.axis_index("shard")


def relative(bit, rel):
    return 1 - bit if rel else bit


def shard_at(shard, step, shards):
    at = shard + step
    return jnp.where(at >= shards, at - shards, at)


def swap_halves(values):
    lane = lax.broadcasted_iota(jnp.int32, values.shape, 1)
    return jnp.where(
        lane % HD < HD // 2,
        pltpu.roll(values, 2 * HD - HD // 2, 1),
        pltpu.roll(values, HD // 2, 1),
    )


def norm_recip(values):
    return lax.rsqrt(jnp.mean(values * values, axis=-1, keepdims=True) + norm_eps)


def norm_back(values, recip, gain, grad_normed):
    scaled = grad_normed * gain
    inner = jnp.mean(scaled * values, axis=-1, keepdims=True)
    grad_values = recip * scaled - values * (recip * recip * recip * inner)
    grad_gain = jnp.sum(grad_normed * values * recip, axis=0, keepdims=True)
    return (grad_values, grad_gain)


def pack_kernel(
    w_out,
    w_query,
    w_key,
    w_value,
    both_gains,
    gate,
    up,
    down_t,
    own,
    attn_mine,
    pair_mine,
    down_mine,
    down,
):
    core, x, y, shard = position()
    block = 2 * core + x
    part = gate.shape[0]
    packed = own.shape[1]
    columns = rows_at(384 * block, 384, 128)
    pair_mine[...] = jnp.where(y == 0, gate[:, columns], up[:, columns])
    own[0:part] = jnp.concatenate([w_out[...], w_query[...], w_key[...], w_value[...]], axis=1)
    row = lax.broadcasted_iota(jnp.int32, (16, part), 0)
    gains = jnp.where(
        row == 0,
        jnp.broadcast_to(both_gains[0:1].astype(f32), row.shape),
        jnp.where(row == 1, jnp.broadcast_to(both_gains[1:2].astype(f32), row.shape), 0.0),
    )
    gains = jnp.concatenate([gains, jnp.zeros((16, packed - part), f32)], axis=1)
    own[part : part + 16] = pltpu.roll(gains, part * shard, 1).astype(low)
    attn_mine[...] = own[rows_at(80 * y, 80), columns]
    down[...] = down_t[...].T
    eighth = down_mine.shape[0]
    down_mine[...] = down[rows_at(eighth * (2 * block + y), eighth), :]


def fold(value):
    rest = value[..., 384:]
    pad = [(0, 0)] * (value.ndim - 1) + [(0, 384 - rest.shape[-1])]
    return jnp.concatenate([value[..., :384], jnp.pad(rest, pad)], axis=-2)


def prepare_kernel(
    lengths,
    tokens_t,
    cotangent_t,
    table_cos,
    table_sin,
    cosine,
    sine,
    bias,
    hidden,
    scaled,
    grad_low,
):
    rows = hidden.shape[0]
    count = lengths.shape[1]
    ends = []
    for i in range(count):
        ends.append(lengths[0, i] + (ends[-1] if ends else 0))
    place = lax.broadcasted_iota(jnp.int32, cosine.shape, 0)
    start_cos = jnp.broadcast_to(table_cos[0:1], cosine.shape)
    start_sin = jnp.broadcast_to(table_sin[0:1], cosine.shape)
    for end in ends:
        start_cos = jnp.where(place >= end, table_cos[pl.ds(end, 1)], start_cos)
        start_sin = jnp.where(place >= end, table_sin[pl.ds(end, 1)], start_sin)
    cos, sin = table_cos[0:rows], table_sin[0:rows]
    cosine[...] = cos * start_cos + sin * start_sin
    signed = sin * start_cos - cos * start_sin
    lane = lax.broadcasted_iota(jnp.int32, cosine.shape, 1)
    sine[...] = jnp.where(lane % HD < HD // 2, -signed, signed)
    query = lax.broadcasted_iota(jnp.int32, bias.shape, 0)
    key = lax.broadcasted_iota(jnp.int32, bias.shape, 1)
    allowed = query >= key
    for end in ends:
        allowed = allowed & ((query < end) | (key >= end))
    bias[...] = jnp.where(allowed, 0.0, neg_fill)
    values = tokens_t[...].T.astype(f32)
    hidden[...] = values
    scaled[...] = values * norm_recip(values)
    wide = lax.broadcasted_iota(jnp.int32, grad_low.shape, 0)
    grad_low[...] = jnp.where(wide < ends[-1], cotangent_t[...].T, jnp.zeros((), low))


def project_kernel(
    shards,
    part,
    scaled,
    cosine,
    sine,
    own,
    pieces,
    other,
    weights,
    gains,
    normed,
    query,
    keys,
    values,
):
    core, x, y, shard = position()
    width = scaled.shape[1]
    place(own.at[pl.ds(0, part)], weights.at[rows_at(part * shard, part)])
    place(own.at[pl.ds(part, 16)], weights.at[rows_at(width + 16 * shard, 16)])
    for rel_core, source in enumerate((pieces, other)):
        for rel_x in range(2):
            for rel_y in range(2):
                at_y = relative(y, rel_y)
                block = 2 * relative(core, rel_core) + relative(x, rel_x)
                columns = rows_at(384 * block, 384, 128)
                for step in range(1, shards):
                    at = shard_at(shard, step, shards)
                    piece = source.at[rel_x, rel_y, step - 1]
                    place(
                        piece.at[pl.ds(0, 64)], weights.at[rows_at(part * at + 80 * at_y, 64), columns]
                    )
                    last = jnp.where(at_y == 0, part * at + 64, width + 16 * at)
                    place(piece.at[pl.ds(64, 16)], weights.at[rows_at(last, 16), columns])
    total = sum(
        weights[width + 16 * s : width + 16 * s + 16, :width].astype(f32) for s in range(shards)
    )
    gains[...] = total[:8]
    n1 = (scaled[...] * total[0:1]).astype(low)
    normed[...] = n1
    for block in range(8):
        start = 512 + 128 * block
        result = matmul(n1, weights[0:width, start : start + 128])
        heads = [2 * block - 1, 2 * block]
        if heads[0] < HEADS + KV:
            turned = result * cosine[...] + swap_halves(result) * sine[...]
        for side, head in enumerate(heads):
            lanes = slice(HD * side, HD * side + HD)
            if head < 0:
                continue
            if head < HEADS:
                query[head] = (turned[:, lanes] * HD**-0.5).astype(low)
            elif head < HEADS + KV:
                keys[head - HEADS] = turned[:, lanes].astype(low)
            else:
                values[head - HEADS - KV] = result[:, lanes].astype(low)


def attend_kernel(kv, bias, query, keys, values, mixed, log_total):
    rows = bias.shape[0]
    for block in range(rows // QUERY_ROWS):
        at = slice(QUERY_ROWS * block, QUERY_ROWS * (block + 1))
        reach = QUERY_ROWS * (block + 1)
        stacked = jnp.concatenate([query[RATIO * kv + i, at] for i in range(RATIO)], axis=0)
        scores = matmul_right_t(stacked, keys[kv, :reach])
        logits = scores.reshape(RATIO, QUERY_ROWS, reach) + bias[at, :reach][None]
        top = jnp.max(logits, axis=-1, keepdims=True)
        expo = jnp.exp(logits - top)
        total = jnp.sum(expo, axis=-1, keepdims=True)
        probs = (expo * (1.0 / total)).astype(low).reshape(RATIO * QUERY_ROWS, reach)
        log_total[:, at] = top + jnp.log(total)
        result = matmul(probs, values[kv, :reach]).astype(low)
        for i in range(RATIO):
            mixed[at, HD * i : HD * i + HD] = result[QUERY_ROWS * i : QUERY_ROWS * (i + 1)]


def attend_last_kernel(
    kv,
    bias,
    query,
    keys,
    values,
    hidden_in,
    gains,
    weights,
    *rest,
):
    before, (mixed, log_total, hidden_one, normed_two) = rest[:kv], rest[kv:]
    attend_kernel(kv, bias, query, keys, values, mixed, log_total)
    width = hidden_in.shape[1]
    every = jnp.concatenate([item[...] for item in before] + [mixed[...]], axis=1)
    hidden = hidden_in[...] + matmul(every, weights[0:width, 0:width])
    hidden_one[...] = hidden
    normed_two[...] = (hidden * norm_recip(hidden) * gains[1:2]).astype(low)


def feed_kernel(
    shards,
    part,
    hidden_one,
    normed_two,
    gains,
    lengths,
    cotangent,
    own_gate,
    own_up,
    own_down,
    pair_pieces,
    pair_other,
    down_pieces,
    down_other,
    result,
    grad_one,
    grad_gain,
    pair_keep,
    pair_send,
    down_keep,
    down_send,
    pair,
    down,
    hidden,
    grad_gate,
    grad_up,
    grad_pair,
    grad_down,
):
    core, x, y, shard = position()
    width = hidden_one.shape[1]
    down_part = own_down.shape[0]
    eighth = down_part // 8
    place(own_gate, pair.at[0, rows_at(part * shard, part)])
    place(own_up, pair.at[1, rows_at(part * shard, part)])
    for rel_core, source in enumerate((pair_pieces, pair_other)):
        for rel_x in range(2):
            block = 2 * relative(core, rel_core) + relative(x, rel_x)
            columns = rows_at(384 * block, 384, 128)
            for rel_y in range(2):
                at_y = relative(y, rel_y)
                for step in range(1, shards):
                    at = shard_at(shard, step, shards)
                    place(
                        source.at[rel_x, rel_y, step - 1],
                        pair.at[at_y, rows_at(part * at, part), columns],
                    )
    place(own_down, down.at[rows_at(down_part * shard, down_part)])
    for rel_core, source in enumerate((down_pieces, down_other)):
        for rel_x in range(2):
            block = 2 * relative(core, rel_core) + relative(x, rel_x)
            for rel_y in range(2):
                start = eighth * (2 * block + relative(y, rel_y))
                for step in range(1, shards):
                    at = shard_at(shard, step, shards)
                    place(
                        source.at[rel_y, rel_x, step - 1],
                        down.at[rows_at(down_part * at + start, eighth)],
                    )
    grad_low = cotangent[...]
    n2 = normed_two[...]
    hidden_width = pair.shape[2]
    for start in range(0, hidden_width, 512):
        at = slice(start, start + 512)
        gate = matmul(n2, pair[0, :, at])
        upward = matmul(n2, pair[1, :, at])
        grad_hidden = matmul_right_t(grad_low, down[at, :])
        sigma = jax.nn.sigmoid(gate)
        active = gate * sigma
        hidden[:, at] = (active * upward).astype(low)
        grad_up[:, at] = (grad_hidden * active).astype(low)
        grad_gate[:, at] = (grad_hidden * upward * (sigma + active * (1.0 - sigma))).astype(low)
    turned = n2.T
    for unit, grads in enumerate((grad_gate, grad_up)):
        for start in range(0, hidden_width, 512):
            at = slice(start, start + 512)
            grad_pair[unit, :, at] = matmul(turned, grads[:, at]).astype(low)
    for start in range(0, hidden_width, 512):
        at = slice(start, start + 512)
        grad_down[at, :] = matmul_left_t(hidden[:, at], grad_low).astype(low)
    for rel_core, (target, down_target) in enumerate(((pair_keep, down_keep), (pair_send, down_send))):
        at_core = relative(core, rel_core)
        for rel_x in range(2):
            at_x = relative(x, rel_x)
            block = 2 * at_core + at_x
            columns = rows_at(384 * block, 384, 128)
            for rel_y in range(2):
                at_y = relative(y, rel_y)
                for step in range(shards):
                    at = shard_at(shard, step, shards)
                    place(
                        grad_pair.at[at_y, rows_at(part * at, part), columns],
                        target.at[rel_x, rel_y, step],
                    )
                    place(
                        grad_down.at[rows_at(down_part * at + eighth * (2 * block + at_y), eighth)],
                        down_target.at[rel_y, rel_x, step],
                    )
    h1 = hidden_one[...]
    total = lengths[0, 0]
    for i in range(1, lengths.shape[1]):
        total = total + lengths[0, i]
    row = lax.broadcasted_iota(jnp.int32, h1.shape, 0)
    summed = h1 + matmul(hidden[...], down[...])
    result[...] = jnp.where(row < total, summed, 0.0).astype(low).T
    grad_normed = matmul_right_t(grad_gate[...], pair[0]) + matmul_right_t(grad_up[...], pair[1])
    grad_from, gain_row = norm_back(h1, norm_recip(h1), gains[1:2], grad_normed)
    grad_one[...] = grad_low.astype(f32) + grad_from
    grad_gain[...] = jnp.broadcast_to(gain_row, grad_gain.shape)


def back_heads_kernel(
    kv,
    bias,
    cosine,
    sine,
    weights,
    query,
    keys,
    values,
    mixed,
    log_total,
    grad_one,
    grad_turned,
    grad_values_out,
    grad_out,
    grad_mixed,
    grad_heads,
):
    rows, width = grad_one.shape
    span = RATIO * HD
    da = grad_one[...].astype(low)
    grad_mixed[...] = matmul_right_t(da, weights[span * kv : span * kv + span, 0:width]).astype(low)
    grad_out[...] = matmul_left_t(mixed[...], da).astype(low)
    grad_keys = [None] * (rows // QUERY_ROWS)
    grad_values = [None] * (rows // QUERY_ROWS)
    for block in range(rows // QUERY_ROWS):
        at = slice(QUERY_ROWS * block, QUERY_ROWS * (block + 1))
        reach = QUERY_ROWS * (block + 1)
        stacked = jnp.concatenate([query[RATIO * kv + i, at] for i in range(RATIO)], axis=0)
        grads = jnp.concatenate([grad_mixed[at, HD * i : HD * i + HD] for i in range(RATIO)], axis=0)
        out = jnp.concatenate([mixed[at, HD * i : HD * i + HD] for i in range(RATIO)], axis=0)
        delta = jnp.sum(grads.astype(f32) * out.astype(f32), axis=-1, keepdims=True)
        scores = matmul_right_t(stacked, keys[kv, :reach]).reshape(RATIO, QUERY_ROWS, reach)
        probs = jnp.exp(scores + bias[at, :reach][None] - log_total[:, at]).reshape(-1, reach)
        grad_probs = matmul_right_t(grads, values[kv, :reach])
        grad_scores = (probs * (grad_probs - delta)).astype(low)
        grad_query = matmul(grad_scores, keys[kv, :reach])
        for i in range(RATIO):
            grad_heads[at, HD * i : HD * i + HD] = (
                grad_query[QUERY_ROWS * i : QUERY_ROWS * (i + 1)] * HD**-0.5
            )
        key_part = matmul_left_t(grad_scores, stacked)
        value_part = matmul_left_t(probs.astype(low), grads)
        for j in range(block + 1):
            at_j = slice(QUERY_ROWS * j, QUERY_ROWS * (j + 1))
            if grad_keys[j] is None:
                grad_keys[j], grad_values[j] = key_part[at_j], value_part[at_j]
            else:
                grad_keys[j] = grad_keys[j] + key_part[at_j]
                grad_values[j] = grad_values[j] + value_part[at_j]
    grad_heads[:, span : span + HD] = jnp.concatenate(grad_keys, axis=0)
    grad_values_out[...] = jnp.concatenate(grad_values, axis=0).astype(low)
    for start in range(0, span + HD, 2 * HD):
        value = grad_heads[:, start : start + 2 * HD]
        turned = value * cosine[...] - swap_halves(value) * sine[...]
        grad_turned[:, start : start + 2 * HD] = turned.astype(low)


def back_last_kernel(
    shards,
    part,
    hidden_in,
    gains,
    weights,
    normed,
    grad_one,
    grad_gain_two,
    *rest,
):
    core, x, y, shard = position()
    rows, width = hidden_in.shape
    turned, values, outs = rest[0:KV], rest[KV : 2 * KV], rest[2 * KV : 3 * KV]
    grad_tokens, keep, send, grad_low, grad_weights = rest[3 * KV :]
    span = RATIO * HD
    grad_low[...] = jnp.concatenate(
        [jnp.zeros((rows, HD), low)]
        + [item[:, 0:span] for item in turned]
        + [item[:, span : span + HD] for item in turned]
        + [item[...] for item in values],
        axis=1,
    )
    normed_t = normed[...].T
    for start in range(0, 1024, 512):
        at = slice(start, start + 512)
        grad_weights[0:width, 512 + start : 1024 + start] = matmul(normed_t, grad_low[:, at]).astype(low)
    for kv in range(KV):
        grad_weights[span * kv : span * kv + span, 0:width] = outs[kv][...]
    grad_normed = matmul_right_t(grad_low[...], weights[0:width, 512:1536])
    hidden = hidden_in[...]
    grad_from, gain_row = norm_back(hidden, norm_recip(hidden), gains[0:1], grad_normed)
    grad_tokens[...] = (grad_one[...] + grad_from).astype(low).T
    row = lax.broadcasted_iota(jnp.int32, (16, width), 0)
    both = jnp.where(
        row == 0,
        jnp.broadcast_to(gain_row, (16, width)),
        jnp.where(row == 1, jnp.broadcast_to(grad_gain_two[0:1], (16, width)), 0.0),
    )
    grad_weights[width : width + 16, :] = jnp.zeros((16, grad_weights.shape[1]), low)
    grad_weights[width : width + 16, 0:width] = both.astype(low)
    for rel_core, target in enumerate((keep, send)):
        for rel_x in range(2):
            for rel_y in range(2):
                at_y = relative(y, rel_y)
                block = 2 * relative(core, rel_core) + relative(x, rel_x)
                columns = rows_at(384 * block, 384, 128)
                for step in range(shards):
                    at = shard_at(shard, step, shards)
                    piece = target.at[rel_y, rel_x, step]
                    place(
                        grad_weights.at[rows_at(part * at + 80 * at_y, 64), columns],
                        piece.at[pl.ds(0, 64)],
                    )
                    last = jnp.where(at_y == 0, part * at + 64, width)
                    place(grad_weights.at[rows_at(last, 16), columns], piece.at[pl.ds(64, 16)])


def finish_kernel(
    pair_pieces,
    pair_other,
    rest_pieces,
    rest_other,
    out_query,
    out_key,
    out_value,
    out_out,
    out_gain_one,
    out_gain_two,
    out_gate,
    out_up,
    out_down,
    attn,
    pair,
    down,
):
    core, x, y, shard = position()
    part, width = out_out.shape
    for rel_core, (p_from, r_from) in enumerate(((pair_pieces, rest_pieces), (pair_other, rest_other))):
        for rel_x in range(2):
            for rel_y in range(2):
                at_y = relative(y, rel_y)
                block = 2 * relative(core, rel_core) + relative(x, rel_x)
                columns = rows_at(384 * block, 384, 128)
                piece = r_from.at[rel_y, rel_x]
                place(p_from.at[rel_x, rel_y], pair.at[at_y, :, columns])
                place(piece.at[pl.ds(0, 80)], attn.at[rows_at(80 * at_y, 80), columns])
                place(piece.at[pl.ds(80, down.shape[1])], down.at[2 * block + at_y])
    kv_width = out_key.shape[1]
    out_out[...] = attn[0:part, 0:width].astype(f32)
    rest = attn[0:part, 512:].astype(f32)
    at = width - 512
    out_query[...] = rest[:, at : at + width]
    out_key[...] = rest[:, at + width : at + width + kv_width]
    out_value[...] = rest[:, at + width + kv_width :]
    gains = attn[part : part + 16, :].astype(f32)
    gains = pltpu.roll(gains, gains.shape[1] - part * shard, 1)
    out_gain_one[...] = gains[0:1, :part]
    out_gain_two[...] = gains[1:2, :part]
    out_gate[...] = pair[0].astype(f32)
    out_up[...] = pair[1].astype(f32)
    half = down.shape[1] // 2
    whole = [
        jnp.concatenate([down[i, :half], down[i, half:, : width - 384]], axis=1)
        for i in range(down.shape[0])
    ]
    out_down[...] = jnp.concatenate(whole, axis=0).T.astype(f32)


VM = pl.BlockSpec(memory_space=pltpu.VMEM)
SM = pl.BlockSpec(memory_space=pltpu.SMEM)


def shape(sizes, kind):
    return jax.ShapeDtypeStruct(tuple(sizes), kind)


def call(kernel, name, operands, in_specs, out_shape, out_specs, scratch, micros, room):
    moved = sum(item.size * item.dtype.itemsize for item in out_shape)
    return pl.pallas_call(
        kernel,
        name=name,
        in_specs=in_specs,
        out_shape=out_shape,
        out_specs=out_specs,
        scratch_shapes=scratch,
        cost_estimate=pl.CostEstimate(
            flops=int(micros * 1e7), bytes_accessed=moved, transcendentals=0
        ),
        compiler_params=pltpu.CompilerParams(vmem_limit_bytes=room << 20),
    )(*operands)


def local(
    replicas,
    shards,
    tokens,
    lengths,
    gain_attn,
    w_query,
    w_key,
    w_value,
    w_out,
    gain_mlp,
    w_gate,
    w_up,
    w_down,
    cotangent,
):
    rows, width = tokens.shape
    part = w_gate.shape[0]
    hidden_width = w_gate.shape[1]
    down_part = w_down.shape[0]
    eighth = down_part // 8
    packed = 2 * width + 2 * w_key.shape[1]
    own, attn_mine, pair_mine, down_mine, own_down = call(
        pack_kernel,
        "pack",
        (
            w_out,
            w_query,
            w_key,
            w_value,
            jnp.stack([gain_attn, gain_mlp]),
            w_gate,
            w_up,
            w_down.T,
        ),
        [VM] * 8,
        (
            shape((part + 16, packed), low),
            shape((80, 384), low),
            shape((part, 384), low),
            shape((eighth, width), low),
            shape((down_part, width), low),
        ),
        [VM] * 5,
        [],
        2,
        60,
    )
    attn_got = gather_shards(attn_mine, shards)
    table_cos, table_sin = rotation_tables(rows + 8, HD)
    cosine, sine, bias, hidden_in, scaled, grad_low = call(
        prepare_kernel,
        "prepare",
        (lengths, tokens.T, cotangent.T, table_cos, table_sin),
        [SM] + [VM] * 4,
        (
            shape((rows, 2 * HD), f32),
            shape((rows, 2 * HD), f32),
            shape((rows, rows), f32),
            shape((rows, width), f32),
            shape((rows, width), f32),
            shape((rows, width), low),
        ),
        [VM] * 6,
        [],
        5,
        24,
    )
    pair_got = gather_shards(after(pair_mine, scaled), shards)
    down_got = gather_shards(after(down_mine, attn_got), shards)
    attn_got = gather_bit(after(attn_got, scaled), 2, replicas)
    attn_got = gather_bit(after(attn_got, pair_got, down_got), 1, replicas)
    pair_got = gather_bit(pair_got, 2, replicas)
    attn_got = after(attn_got, pair_got)
    attn_other = flip(attn_got, 0, replicas)
    weights, gains, normed, query, keys, values = call(
        functools.partial(project_kernel, shards, part),
        "project",
        (scaled, cosine, sine, own, attn_got, attn_other),
        [VM, VM, VM, VM, VM, VM],
        (
            shape((width + 16 * shards, packed), low),
            shape((8, width), f32),
            shape((rows, width), low),
            shape((HEADS, rows, HD), low),
            shape((KV, rows, HD), low),
            shape((KV, rows, HD), low),
        ),
        [VM] * 6,
        [],
        5,
        24,
    )
    down_got = gather_bit(down_got, 1, replicas, normed)
    mixed, log_total = [], []
    for kv in range(KV):
        outs = [shape((rows, RATIO * HD), low), shape((RATIO, rows, 1), f32)]
        operands = (bias, query, keys, values)
        if kv < KV - 1:
            one, two = call(
                functools.partial(attend_kernel, kv),
                f"attend_{kv}",
                operands,
                [VM] * 4,
                outs,
                [VM] * 2,
                [],
                3,
                24,
            )
        else:
            down_got = gather_bit(down_got, 2, replicas, *mixed)
            operands += (after(hidden_in, down_got), gains, weights, *mixed)
            one, two, hidden_one, normed_two = call(
                functools.partial(attend_last_kernel, kv),
                f"attend_{kv}",
                operands,
                [VM] * len(operands),
                outs + [shape((rows, width), f32), shape((rows, width), low)],
                [VM] * 4,
                [],
                4,
                24,
            )
        mixed.append(one)
        log_total.append(two)
    pair_got = gather_bit(pair_got, 1, replicas, normed_two)
    pair_other = flip(pair_got, 0, replicas)
    down_other = flip(down_got, 0, replicas)
    pair_shape = shape((2, 2, shards, part, 384), low)
    down_shape = shape((2, 2, shards, eighth, width), low)
    result, grad_one, grad_gain_two, pair_keep, pair_send, down_keep, down_send = call(
        functools.partial(feed_kernel, shards, part),
        "feed",
        (
            hidden_one,
            normed_two,
            gains,
            lengths,
            grad_low,
            w_gate,
            w_up,
            own_down,
            pair_got,
            pair_other,
            down_got,
            down_other,
        ),
        [VM] * 3 + [SM, VM] + [VM] * 7,
        (
            shape((width, rows), low),
            shape((rows, width), f32),
            shape((8, width), f32),
            pair_shape,
            pair_shape,
            down_shape,
            down_shape,
        ),
        [VM] * 3 + [VM] * 4,
        [
            pltpu.VMEM((2, shards * part, hidden_width), low),
            pltpu.VMEM((hidden_width, width), low),
            pltpu.VMEM((rows, hidden_width), low),
            pltpu.VMEM((rows, hidden_width), low),
            pltpu.VMEM((rows, hidden_width), low),
            pltpu.VMEM((2, shards * part, hidden_width), low),
            pltpu.VMEM((hidden_width, width), low),
        ],
        19,
        38,
    )
    pair_sent = flip(pair_send, 0, replicas)
    down_sent = flip(down_send, 0, replicas)
    grad_turned, grad_values, grad_out = [], [], []
    for kv in range(KV):
        if kv == 1:
            pair_left = halve(pair_keep, after(pair_sent, grad_turned[0]), 1, replicas)
            down_left = halve(down_keep, after(down_sent, grad_turned[0]), 2, replicas)
            grad_one = after(grad_one, pair_sent, down_sent)
        one, two, three = call(
            functools.partial(back_heads_kernel, kv),
            f"back_{kv}",
            (bias, cosine, sine, weights, query, keys, values, mixed[kv], log_total[kv], grad_one),
            [VM] * 10,
            (
                shape((rows, RATIO * HD + HD), low),
                shape((rows, HD), low),
                shape((RATIO * HD, width), low),
            ),
            [VM] * 3,
            [pltpu.VMEM((rows, RATIO * HD), low), pltpu.VMEM((rows, RATIO * HD + HD), f32)],
            5,
            24,
        )
        grad_turned.append(one)
        grad_values.append(two)
        grad_out.append(three)
    attn_shape = shape((2, 2, shards, 80, 384), low)
    grad_tokens, attn_keep, attn_send = call(
        functools.partial(back_last_kernel, shards, part),
        "back_last",
        (
            hidden_in,
            gains,
            weights,
            normed,
            grad_one,
            grad_gain_two,
            *grad_turned,
            *grad_values,
            *grad_out,
        ),
        [VM] * (6 + 3 * KV),
        (shape((width, rows), low), attn_shape, attn_shape),
        [VM, VM, VM],
        [
            pltpu.VMEM((rows, 1024), low),
            pltpu.VMEM((width + 16, packed), low),
        ],
        6,
        24,
    )
    attn_sent = flip(after(attn_send, down_left[1], pair_left[1]), 0, replicas)
    pair_left = halve(*pair_left, 2, replicas)
    attn_left = halve(attn_keep, after(attn_sent, pair_left[1]), 2, replicas)
    pair_total = scatter_over_shards(*pair_left, shards, replicas)
    down_left = halve(down_left[0], after(down_left[1], grad_tokens), 1, replicas)
    attn_left = halve(attn_left[0], after(attn_left[1], pair_total), 1, replicas)
    pair_half = gather_bit(pair_total, 2, replicas)
    attn_left = (attn_left[0], after(attn_left[1], pair_half))
    down_total = scatter_over_shards(*down_left, shards, replicas)
    attn_total = scatter_over_shards(*attn_left, shards, replicas)
    pair_half = gather_bit(pair_half, 1, replicas)
    pair_pieces = spread(pair_half, (0,), replicas)
    attn_total = after(attn_total, pair_half)
    rest_pieces = spread(jnp.concatenate([attn_total, fold(down_total)]), (1, 2, 0), replicas)
    g_query, g_key, g_value, g_out, g_gain_one, g_gain_two, g_gate, g_up, g_down = call(
        finish_kernel,
        "finish",
        (*pair_pieces, *rest_pieces),
        [VM] * 4,
        (
            shape(w_query.shape, f32),
            shape(w_key.shape, f32),
            shape(w_value.shape, f32),
            shape(w_out.shape, f32),
            shape((1, part), f32),
            shape((1, part), f32),
            shape(w_gate.shape, f32),
            shape(w_up.shape, f32),
            shape((width, down_part), f32),
        ),
        [VM] * 9,
        [
            pltpu.VMEM((160, packed), low),
            pltpu.VMEM((2, part, hidden_width), low),
            pltpu.VMEM((8, 2 * eighth, 384), low),
        ],
        5,
        24,
    )
    return (
        result.T,
        grad_tokens.T,
        g_gain_one.reshape(part),
        g_query,
        g_key,
        g_value,
        g_out,
        g_gain_two.reshape(part),
        g_gate,
        g_up,
        g_down.T,
    )


def solution(mesh):
    in_specs = (
        P(("rep", "shard"), None),
        P(("rep", "shard"), None),
        P("shard"),
        P("shard", None),
        P("shard", None),
        P("shard", None),
        P("shard", None),
        P("shard"),
        P("shard", None),
        P("shard", None),
        P("shard", None),
        P(("rep", "shard"), None),
    )
    out_specs = (
        P(("rep", "shard"), None),
        P(("rep", "shard"), None),
        P("shard"),
        P("shard", None),
        P("shard", None),
        P("shard", None),
        P("shard", None),
        P("shard"),
        P("shard", None),
        P("shard", None),
        P("shard", None),
    )
    part = functools.partial(local, mesh.shape["rep"], mesh.shape["shard"])
    return jax.shard_map(part, mesh=mesh, in_specs=in_specs, out_specs=out_specs, check_vma=False)
```

```python
import functools

import jax
import jax.numpy as jnp
from jax import lax
from jax.experimental import pallas as pl
from jax.experimental.pallas import tpu as pltpu
from jax.sharding import PartitionSpec as P
import numpy as np

HEADS = 9
KV = 3
HD = 64
RATIO = HEADS // KV


norm_eps = 1e-05
rope_base = 100000.0
neg_fill = -1e30

low = jnp.bfloat16
f32 = jnp.float32
QUERY_ROWS = 128


def rotation_tables(places, head_size):
    half = head_size // 2
    freq = np.float32(rope_base) ** (-(np.arange(half, dtype=np.float32) * np.float32(2.0) / head_size))
    angle = np.arange(places, dtype=np.float32)[:, None] * freq.astype(np.float32)[None, :]
    return np.concatenate([np.cos(angle)] * 4, axis=1), np.concatenate([np.sin(angle)] * 4, axis=1)


def matmul(left, right):
    return jnp.dot(left, right, preferred_element_type=f32)


def matmul_left_t(left, right):
    return lax.dot_general(left, right, (((0,), (0,)), ((), ())), preferred_element_type=f32)


def matmul_right_t(left, right):
    return lax.dot_general(left, right, (((1,), (1,)), ((), ())), preferred_element_type=f32)


def flip(value, bit, replicas):
    return lax.ppermute(value, "rep", [(i, i ^ (1 << bit)) for i in range(replicas)])


def shift_from(value, step, shards):
    return lax.ppermute(value, "shard", [((s + step) % shards, s) for s in range(shards)])


def shift_to(value, step, shards):
    return lax.ppermute(value, "shard", [(s, (s + step) % shards) for s in range(shards)])


def add_low(left, right):
    return (left.astype(f32) + right.astype(f32)).astype(low)


def after(value, *others):
    return lax.optimization_barrier((value, *others))[0]


def gather_shards(mine, shards):
    return jnp.stack([shift_from(mine, step, shards) for step in range(1, shards)])


def gather_bit(got, bit, replicas, *later):
    other = flip(got, bit, replicas)
    return jnp.stack([after(got, *later) if later else got, other])


def halve(keep, other, bit, replicas):
    sent = flip(add_low(keep[1], other[1]), bit, replicas)
    return add_low(keep[0], other[0]), sent


def scatter_over_shards(keep, other, shards, replicas):
    parts = [add_low(keep[step], other[step]) for step in range(1, shards)]
    moved = [shift_to(part, step + 1, shards) for step, part in enumerate(parts)]
    total = keep[0].astype(f32) + other[0].astype(f32)
    for part in moved:
        total = total + part.astype(f32)
    total = total.astype(low)
    bit = 3
    while (1 << bit) < replicas:
        total = add_low(total, flip(total, bit, replicas))
        bit += 1
    return total


def spread(total, order, replicas):
    for bit in order[:-1]:
        total = jnp.stack([total, flip(total, bit, replicas)])
    return total, flip(total, order[-1], replicas)


def place(source, target):
    target[...] = source[...]


def rows_at(start, count, unit=16):
    return pl.ds(pl.multiple_of(start, unit), count)


def position():
    index = lax.axis_index("rep")
    return index % 2, index // 2 % 2, index // 4 % 2, lax.axis_index("shard")


def relative(bit, rel):
    return 1 - bit if rel else bit


def shard_at(shard, step, shards):
    at = shard + step
    return jnp.where(at >= shards, at - shards, at)


def swap_halves(values):
    lane = lax.broadcasted_iota(jnp.int32, values.shape, 1)
    return jnp.where(
        lane % HD < HD // 2,
        pltpu.roll(values, 2 * HD - HD // 2, 1),
        pltpu.roll(values, HD // 2, 1),
    )


def norm_recip(values):
    return lax.rsqrt(jnp.mean(values * values, axis=-1, keepdims=True) + norm_eps)


def norm_back(values, recip, gain, grad_normed):
    scaled = grad_normed * gain
    inner = jnp.mean(scaled * values, axis=-1, keepdims=True)
    grad_values = recip * scaled - values * (recip * recip * recip * inner)
    grad_gain = jnp.sum(grad_normed * values * recip, axis=0, keepdims=True)
    return (grad_values, grad_gain)


def pack_kernel(
    w_out,
    w_query,
    w_key,
    w_value,
    both_gains,
    gate,
    up,
    down_t,
    own,
    attn_mine,
    pair_mine,
    down_mine,
    down,
):
    core, x, y, shard = position()
    block = 2 * core + x
    part = gate.shape[0]
    packed = own.shape[1]
    columns = rows_at(384 * block, 384, 128)
    pair_mine[...] = jnp.where(y == 0, gate[:, columns], up[:, columns])
    own[0:part] = jnp.concatenate([w_out[...], w_query[...], w_key[...], w_value[...]], axis=1)
    row = lax.broadcasted_iota(jnp.int32, (16, part), 0)
    gains = jnp.where(
        row == 0,
        jnp.broadcast_to(both_gains[0:1].astype(f32), row.shape),
        jnp.where(row == 1, jnp.broadcast_to(both_gains[1:2].astype(f32), row.shape), 0.0),
    )
    gains = jnp.concatenate([gains, jnp.zeros((16, packed - part), f32)], axis=1)
    own[part : part + 16] = pltpu.roll(gains, part * shard, 1).astype(low)
    attn_mine[...] = own[rows_at(80 * y, 80), columns]
    down[...] = down_t[...].T
    eighth = down_mine.shape[0]
    down_mine[...] = down[rows_at(eighth * (2 * block + y), eighth), :]


def fold(value):
    rest = value[..., 384:]
    pad = [(0, 0)] * (value.ndim - 1) + [(0, 384 - rest.shape[-1])]
    return jnp.concatenate([value[..., :384], jnp.pad(rest, pad)], axis=-2)


def prepare_kernel(
    lengths,
    tokens_t,
    cotangent_t,
    table_cos,
    table_sin,
    cosine,
    sine,
    bias,
    hidden,
    scaled,
    grad_low,
):
    rows = hidden.shape[0]
    count = lengths.shape[1]
    ends = []
    for i in range(count):
        ends.append(lengths[0, i] + (ends[-1] if ends else 0))
    place = lax.broadcasted_iota(jnp.int32, cosine.shape, 0)
    start_cos = jnp.broadcast_to(table_cos[0:1], cosine.shape)
    start_sin = jnp.broadcast_to(table_sin[0:1], cosine.shape)
    for end in ends:
        start_cos = jnp.where(place >= end, table_cos[pl.ds(end, 1)], start_cos)
        start_sin = jnp.where(place >= end, table_sin[pl.ds(end, 1)], start_sin)
    cos, sin = table_cos[0:rows], table_sin[0:rows]
    cosine[...] = cos * start_cos + sin * start_sin
    signed = sin * start_cos - cos * start_sin
    lane = lax.broadcasted_iota(jnp.int32, cosine.shape, 1)
    sine[...] = jnp.where(lane % HD < HD // 2, -signed, signed)
    query = lax.broadcasted_iota(jnp.int32, bias.shape, 0)
    key = lax.broadcasted_iota(jnp.int32, bias.shape, 1)
    allowed = query >= key
    for end in ends:
        allowed = allowed & ((query < end) | (key >= end))
    bias[...] = jnp.where(allowed, 0.0, neg_fill)
    values = tokens_t[...].T.astype(f32)
    hidden[...] = values
    scaled[...] = values * norm_recip(values)
    wide = lax.broadcasted_iota(jnp.int32, grad_low.shape, 0)
    grad_low[...] = jnp.where(wide < ends[-1], cotangent_t[...].T, jnp.zeros((), low))


def project_kernel(
    shards,
    part,
    scaled,
    cosine,
    sine,
    own,
    pieces,
    other,
    weights,
    gains,
    normed,
    query,
    keys,
    values,
):
    core, x, y, shard = position()
    width = scaled.shape[1]
    place(own.at[pl.ds(0, part)], weights.at[rows_at(part * shard, part)])
    place(own.at[pl.ds(part, 16)], weights.at[rows_at(width + 16 * shard, 16)])
    for rel_core, source in enumerate((pieces, other)):
        for rel_x in range(2):
            for rel_y in range(2):
                at_y = relative(y, rel_y)
                block = 2 * relative(core, rel_core) + relative(x, rel_x)
                columns = rows_at(384 * block, 384, 128)
                for step in range(1, shards):
                    at = shard_at(shard, step, shards)
                    piece = source.at[rel_x, rel_y, step - 1]
                    place(
                        piece.at[pl.ds(0, 64)], weights.at[rows_at(part * at + 80 * at_y, 64), columns]
                    )
                    last = jnp.where(at_y == 0, part * at + 64, width + 16 * at)
                    place(piece.at[pl.ds(64, 16)], weights.at[rows_at(last, 16), columns])
    total = sum(
        weights[width + 16 * s : width + 16 * s + 16, :width].astype(f32) for s in range(shards)
    )
    gains[...] = total[:8]
    n1 = (scaled[...] * total[0:1]).astype(low)
    normed[...] = n1
    for block in range(8):
        start = 512 + 128 * block
        result = matmul(n1, weights[0:width, start : start + 128])
        heads = [2 * block - 1, 2 * block]
        if heads[0] < HEADS + KV:
            turned = result * cosine[...] + swap_halves(result) * sine[...]
        for side, head in enumerate(heads):
            lanes = slice(HD * side, HD * side + HD)
            if head < 0:
                continue
            if head < HEADS:
                query[head] = (turned[:, lanes] * HD**-0.5).astype(low)
            elif head < HEADS + KV:
                keys[head - HEADS] = turned[:, lanes].astype(low)
            else:
                values[head - HEADS - KV] = result[:, lanes].astype(low)


def attend_kernel(kv, bias, query, keys, values, mixed, log_total):
    rows = bias.shape[0]
    for block in range(rows // QUERY_ROWS):
        at = slice(QUERY_ROWS * block, QUERY_ROWS * (block + 1))
        reach = QUERY_ROWS * (block + 1)
        stacked = jnp.concatenate([query[RATIO * kv + i, at] for i in range(RATIO)], axis=0)
        scores = matmul_right_t(stacked, keys[kv, :reach])
        logits = scores.reshape(RATIO, QUERY_ROWS, reach) + bias[at, :reach][None]
        top = jnp.max(logits, axis=-1, keepdims=True)
        expo = jnp.exp(logits - top)
        total = jnp.sum(expo, axis=-1, keepdims=True)
        probs = (expo * (1.0 / total)).astype(low).reshape(RATIO * QUERY_ROWS, reach)
        log_total[:, at] = top + jnp.log(total)
        result = matmul(probs, values[kv, :reach]).astype(low)
        for i in range(RATIO):
            mixed[at, HD * i : HD * i + HD] = result[QUERY_ROWS * i : QUERY_ROWS * (i + 1)]


def attend_last_kernel(
    kv,
    bias,
    query,
    keys,
    values,
    hidden_in,
    gains,
    weights,
    *rest,
):
    before, (mixed, log_total, hidden_one, normed_two) = rest[:kv], rest[kv:]
    attend_kernel(kv, bias, query, keys, values, mixed, log_total)
    width = hidden_in.shape[1]
    every = jnp.concatenate([item[...] for item in before] + [mixed[...]], axis=1)
    hidden = hidden_in[...] + matmul(every, weights[0:width, 0:width])
    hidden_one[...] = hidden
    normed_two[...] = (hidden * norm_recip(hidden) * gains[1:2]).astype(low)


def feed_kernel(
    shards,
    part,
    hidden_one,
    normed_two,
    gains,
    lengths,
    cotangent,
    own_gate,
    own_up,
    own_down,
    pair_pieces,
    pair_other,
    down_pieces,
    down_other,
    result,
    grad_one,
    grad_gain,
    pair_keep,
    pair_send,
    down_keep,
    down_send,
    pair,
    down,
    hidden,
    grad_gate,
    grad_up,
    grad_pair,
    grad_down,
):
    core, x, y, shard = position()
    width = hidden_one.shape[1]
    down_part = own_down.shape[0]
    eighth = down_part // 8
    place(own_gate, pair.at[0, rows_at(part * shard, part)])
    place(own_up, pair.at[1, rows_at(part * shard, part)])
    for rel_core, source in enumerate((pair_pieces, pair_other)):
        for rel_x in range(2):
            block = 2 * relative(core, rel_core) + relative(x, rel_x)
            columns = rows_at(384 * block, 384, 128)
            for rel_y in range(2):
                at_y = relative(y, rel_y)
                for step in range(1, shards):
                    at = shard_at(shard, step, shards)
                    place(
                        source.at[rel_x, rel_y, step - 1],
                        pair.at[at_y, rows_at(part * at, part), columns],
                    )
    place(own_down, down.at[rows_at(down_part * shard, down_part)])
    for rel_core, source in enumerate((down_pieces, down_other)):
        for rel_x in range(2):
            block = 2 * relative(core, rel_core) + relative(x, rel_x)
            for rel_y in range(2):
                start = eighth * (2 * block + relative(y, rel_y))
                for step in range(1, shards):
                    at = shard_at(shard, step, shards)
                    place(
                        source.at[rel_y, rel_x, step - 1],
                        down.at[rows_at(down_part * at + start, eighth)],
                    )
    grad_low = cotangent[...]
    n2 = normed_two[...]
    hidden_width = pair.shape[2]
    for start in range(0, hidden_width, 512):
        at = slice(start, start + 512)
        gate = matmul(n2, pair[0, :, at])
        upward = matmul(n2, pair[1, :, at])
        grad_hidden = matmul_right_t(grad_low, down[at, :])
        sigma = jax.nn.sigmoid(gate)
        active = gate * sigma
        hidden[:, at] = (active * upward).astype(low)
        grad_up[:, at] = (grad_hidden * active).astype(low)
        grad_gate[:, at] = (grad_hidden * upward * (sigma + active * (1.0 - sigma))).astype(low)
    turned = n2.T
    for unit, grads in enumerate((grad_gate, grad_up)):
        for start in range(0, hidden_width, 512):
            at = slice(start, start + 512)
            grad_pair[unit, :, at] = matmul(turned, grads[:, at]).astype(low)
    for start in range(0, hidden_width, 512):
        at = slice(start, start + 512)
        grad_down[at, :] = matmul_left_t(hidden[:, at], grad_low).astype(low)
    for rel_core, (target, down_target) in enumerate(((pair_keep, down_keep), (pair_send, down_send))):
        at_core = relative(core, rel_core)
        for rel_x in range(2):
            at_x = relative(x, rel_x)
            block = 2 * at_core + at_x
            columns = rows_at(384 * block, 384, 128)
            for rel_y in range(2):
                at_y = relative(y, rel_y)
                for step in range(shards):
                    at = shard_at(shard, step, shards)
                    place(
                        grad_pair.at[at_y, rows_at(part * at, part), columns],
                        target.at[rel_x, rel_y, step],
                    )
                    place(
                        grad_down.at[rows_at(down_part * at + eighth * (2 * block + at_y), eighth)],
                        down_target.at[rel_y, rel_x, step],
                    )
    h1 = hidden_one[...]
    total = lengths[0, 0]
    for i in range(1, lengths.shape[1]):
        total = total + lengths[0, i]
    row = lax.broadcasted_iota(jnp.int32, h1.shape, 0)
    summed = h1 + matmul(hidden[...], down[...])
    result[...] = jnp.where(row < total, summed, 0.0).astype(low).T
    grad_normed = matmul_right_t(grad_gate[...], pair[0]) + matmul_right_t(grad_up[...], pair[1])
    grad_from, gain_row = norm_back(h1, norm_recip(h1), gains[1:2], grad_normed)
    grad_one[...] = grad_low.astype(f32) + grad_from
    grad_gain[...] = jnp.broadcast_to(gain_row, grad_gain.shape)


def back_heads_kernel(
    kv,
    bias,
    cosine,
    sine,
    weights,
    query,
    keys,
    values,
    mixed,
    log_total,
    grad_one,
    grad_turned,
    grad_values_out,
    grad_out,
    grad_mixed,
    grad_heads,
):
    rows, width = grad_one.shape
    span = RATIO * HD
    da = grad_one[...].astype(low)
    grad_mixed[...] = matmul_right_t(da, weights[span * kv : span * kv + span, 0:width]).astype(low)
    grad_out[...] = matmul_left_t(mixed[...], da).astype(low)
    grad_keys = [None] * (rows // QUERY_ROWS)
    grad_values = [None] * (rows // QUERY_ROWS)
    for block in range(rows // QUERY_ROWS):
        at = slice(QUERY_ROWS * block, QUERY_ROWS * (block + 1))
        reach = QUERY_ROWS * (block + 1)
        stacked = jnp.concatenate([query[RATIO * kv + i, at] for i in range(RATIO)], axis=0)
        grads = jnp.concatenate([grad_mixed[at, HD * i : HD * i + HD] for i in range(RATIO)], axis=0)
        out = jnp.concatenate([mixed[at, HD * i : HD * i + HD] for i in range(RATIO)], axis=0)
        delta = jnp.sum(grads.astype(f32) * out.astype(f32), axis=-1, keepdims=True)
        scores = matmul_right_t(stacked, keys[kv, :reach]).reshape(RATIO, QUERY_ROWS, reach)
        probs = jnp.exp(scores + bias[at, :reach][None] - log_total[:, at]).reshape(-1, reach)
        grad_probs = matmul_right_t(grads, values[kv, :reach])
        grad_scores = (probs * (grad_probs - delta)).astype(low)
        grad_query = matmul(grad_scores, keys[kv, :reach])
        for i in range(RATIO):
            grad_heads[at, HD * i : HD * i + HD] = (
                grad_query[QUERY_ROWS * i : QUERY_ROWS * (i + 1)] * HD**-0.5
            )
        key_part = matmul_left_t(grad_scores, stacked)
        value_part = matmul_left_t(probs.astype(low), grads)
        for j in range(block + 1):
            at_j = slice(QUERY_ROWS * j, QUERY_ROWS * (j + 1))
            if grad_keys[j] is None:
                grad_keys[j], grad_values[j] = key_part[at_j], value_part[at_j]
            else:
                grad_keys[j] = grad_keys[j] + key_part[at_j]
                grad_values[j] = grad_values[j] + value_part[at_j]
    grad_heads[:, span : span + HD] = jnp.concatenate(grad_keys, axis=0)
    grad_values_out[...] = jnp.concatenate(grad_values, axis=0).astype(low)
    for start in range(0, span + HD, 2 * HD):
        value = grad_heads[:, start : start + 2 * HD]
        turned = value * cosine[...] - swap_halves(value) * sine[...]
        grad_turned[:, start : start + 2 * HD] = turned.astype(low)


def back_last_kernel(
    shards,
    part,
    hidden_in,
    gains,
    weights,
    normed,
    grad_one,
    grad_gain_two,
    *rest,
):
    core, x, y, shard = position()
    rows, width = hidden_in.shape
    turned, values, outs = rest[0:KV], rest[KV : 2 * KV], rest[2 * KV : 3 * KV]
    grad_tokens, keep, send, grad_low, grad_weights = rest[3 * KV :]
    span = RATIO * HD
    grad_low[...] = jnp.concatenate(
        [jnp.zeros((rows, HD), low)]
        + [item[:, 0:span] for item in turned]
        + [item[:, span : span + HD] for item in turned]
        + [item[...] for item in values],
        axis=1,
    )
    normed_t = normed[...].T
    for start in range(0, 1024, 512):
        at = slice(start, start + 512)
        grad_weights[0:width, 512 + start : 1024 + start] = matmul(normed_t, grad_low[:, at]).astype(low)
    for kv in range(KV):
        grad_weights[span * kv : span * kv + span, 0:width] = outs[kv][...]
    grad_normed = matmul_right_t(grad_low[...], weights[0:width, 512:1536])
    hidden = hidden_in[...]
    grad_from, gain_row = norm_back(hidden, norm_recip(hidden), gains[0:1], grad_normed)
    grad_tokens[...] = (grad_one[...] + grad_from).astype(low).T
    row = lax.broadcasted_iota(jnp.int32, (16, width), 0)
    both = jnp.where(
        row == 0,
        jnp.broadcast_to(gain_row, (16, width)),
        jnp.where(row == 1, jnp.broadcast_to(grad_gain_two[0:1], (16, width)), 0.0),
    )
    grad_weights[width : width + 16, :] = jnp.zeros((16, grad_weights.shape[1]), low)
    grad_weights[width : width + 16, 0:width] = both.astype(low)
    for rel_core, target in enumerate((keep, send)):
        for rel_x in range(2):
            for rel_y in range(2):
                at_y = relative(y, rel_y)
                block = 2 * relative(core, rel_core) + relative(x, rel_x)
                columns = rows_at(384 * block, 384, 128)
                for step in range(shards):
                    at = shard_at(shard, step, shards)
                    piece = target.at[rel_y, rel_x, step]
                    place(
                        grad_weights.at[rows_at(part * at + 80 * at_y, 64), columns],
                        piece.at[pl.ds(0, 64)],
                    )
                    last = jnp.where(at_y == 0, part * at + 64, width)
                    place(grad_weights.at[rows_at(last, 16), columns], piece.at[pl.ds(64, 16)])


def finish_kernel(
    pair_pieces,
    pair_other,
    rest_pieces,
    rest_other,
    out_query,
    out_key,
    out_value,
    out_out,
    out_gain_one,
    out_gain_two,
    out_gate,
    out_up,
    out_down,
    attn,
    pair,
    down,
):
    core, x, y, shard = position()
    part, width = out_out.shape
    for rel_core, (p_from, r_from) in enumerate(((pair_pieces, rest_pieces), (pair_other, rest_other))):
        for rel_x in range(2):
            for rel_y in range(2):
                at_y = relative(y, rel_y)
                block = 2 * relative(core, rel_core) + relative(x, rel_x)
                columns = rows_at(384 * block, 384, 128)
                piece = r_from.at[rel_y, rel_x]
                place(p_from.at[rel_x, rel_y, pl.ds(0, part)], pair.at[at_y, :, columns])
                place(piece, attn.at[rows_at(80 * at_y, 80), columns])
                place(
                    p_from.at[rel_x, rel_y, pl.ds(part, down.shape[1])], down.at[2 * block + at_y]
                )
    kv_width = out_key.shape[1]
    out_out[...] = attn[0:part, 0:width].astype(f32)
    rest = attn[0:part, 512:].astype(f32)
    at = width - 512
    out_query[...] = rest[:, at : at + width]
    out_key[...] = rest[:, at + width : at + width + kv_width]
    out_value[...] = rest[:, at + width + kv_width :]
    gains = attn[part : part + 16, :].astype(f32)
    gains = pltpu.roll(gains, gains.shape[1] - part * shard, 1)
    out_gain_one[...] = gains[0:1, :part]
    out_gain_two[...] = gains[1:2, :part]
    out_gate[...] = pair[0].astype(f32)
    out_up[...] = pair[1].astype(f32)
    half = down.shape[1] // 2
    whole = [
        jnp.concatenate([down[i, :half], down[i, half:, : width - 384]], axis=1)
        for i in range(down.shape[0])
    ]
    out_down[...] = jnp.concatenate(whole, axis=0).T.astype(f32)


VM = pl.BlockSpec(memory_space=pltpu.VMEM)
SM = pl.BlockSpec(memory_space=pltpu.SMEM)


def shape(sizes, kind):
    return jax.ShapeDtypeStruct(tuple(sizes), kind)


def call(kernel, name, operands, in_specs, out_shape, out_specs, scratch, micros, room):
    moved = sum(item.size * item.dtype.itemsize for item in out_shape)
    return pl.pallas_call(
        kernel,
        name=name,
        in_specs=in_specs,
        out_shape=out_shape,
        out_specs=out_specs,
        scratch_shapes=scratch,
        cost_estimate=pl.CostEstimate(
            flops=int(micros * 1e7), bytes_accessed=moved, transcendentals=0
        ),
        compiler_params=pltpu.CompilerParams(vmem_limit_bytes=room << 20),
    )(*operands)


def local(
    replicas,
    shards,
    tokens,
    lengths,
    gain_attn,
    w_query,
    w_key,
    w_value,
    w_out,
    gain_mlp,
    w_gate,
    w_up,
    w_down,
    cotangent,
):
    rows, width = tokens.shape
    part = w_gate.shape[0]
    hidden_width = w_gate.shape[1]
    down_part = w_down.shape[0]
    eighth = down_part // 8
    packed = 2 * width + 2 * w_key.shape[1]
    own, attn_mine, pair_mine, down_mine, own_down = call(
        pack_kernel,
        "pack",
        (
            w_out,
            w_query,
            w_key,
            w_value,
            jnp.stack([gain_attn, gain_mlp]),
            w_gate,
            w_up,
            w_down.T,
        ),
        [VM] * 8,
        (
            shape((part + 16, packed), low),
            shape((80, 384), low),
            shape((part, 384), low),
            shape((eighth, width), low),
            shape((down_part, width), low),
        ),
        [VM] * 5,
        [],
        2,
        60,
    )
    attn_got = gather_shards(attn_mine, shards)
    table_cos, table_sin = rotation_tables(rows + 8, HD)
    cosine, sine, bias, hidden_in, scaled, grad_low = call(
        prepare_kernel,
        "prepare",
        (lengths, tokens.T, cotangent.T, table_cos, table_sin),
        [SM] + [VM] * 4,
        (
            shape((rows, 2 * HD), f32),
            shape((rows, 2 * HD), f32),
            shape((rows, rows), f32),
            shape((rows, width), f32),
            shape((rows, width), f32),
            shape((rows, width), low),
        ),
        [VM] * 6,
        [],
        5,
        24,
    )
    pair_got = gather_shards(after(pair_mine, scaled), shards)
    down_got = gather_shards(after(down_mine, attn_got), shards)
    attn_got = gather_bit(after(attn_got, scaled), 2, replicas)
    attn_got = gather_bit(after(attn_got, pair_got, down_got), 1, replicas)
    pair_got = gather_bit(pair_got, 2, replicas)
    attn_got = after(attn_got, pair_got)
    attn_other = flip(attn_got, 0, replicas)
    weights, gains, normed, query, keys, values = call(
        functools.partial(project_kernel, shards, part),
        "project",
        (scaled, cosine, sine, own, attn_got, attn_other),
        [VM, VM, VM, VM, VM, VM],
        (
            shape((width + 16 * shards, packed), low),
            shape((8, width), f32),
            shape((rows, width), low),
            shape((HEADS, rows, HD), low),
            shape((KV, rows, HD), low),
            shape((KV, rows, HD), low),
        ),
        [VM] * 6,
        [],
        5,
        24,
    )
    down_got = gather_bit(down_got, 1, replicas, normed)
    mixed, log_total = [], []
    for kv in range(KV):
        outs = [shape((rows, RATIO * HD), low), shape((RATIO, rows, 1), f32)]
        operands = (bias, query, keys, values)
        if kv < KV - 1:
            one, two = call(
                functools.partial(attend_kernel, kv),
                f"attend_{kv}",
                operands,
                [VM] * 4,
                outs,
                [VM] * 2,
                [],
                3,
                24,
            )
        else:
            down_got = gather_bit(down_got, 2, replicas, *mixed)
            operands += (after(hidden_in, down_got), gains, weights, *mixed)
            one, two, hidden_one, normed_two = call(
                functools.partial(attend_last_kernel, kv),
                f"attend_{kv}",
                operands,
                [VM] * len(operands),
                outs + [shape((rows, width), f32), shape((rows, width), low)],
                [VM] * 4,
                [],
                4,
                24,
            )
        mixed.append(one)
        log_total.append(two)
    pair_got = gather_bit(pair_got, 1, replicas, normed_two)
    pair_other = flip(pair_got, 0, replicas)
    down_other = flip(down_got, 0, replicas)
    pair_shape = shape((2, 2, shards, part, 384), low)
    down_shape = shape((2, 2, shards, eighth, width), low)
    result, grad_one, grad_gain_two, pair_keep, pair_send, down_keep, down_send = call(
        functools.partial(feed_kernel, shards, part),
        "feed",
        (
            hidden_one,
            normed_two,
            gains,
            lengths,
            grad_low,
            w_gate,
            w_up,
            own_down,
            pair_got,
            pair_other,
            down_got,
            down_other,
        ),
        [VM] * 3 + [SM, VM] + [VM] * 7,
        (
            shape((width, rows), low),
            shape((rows, width), f32),
            shape((8, width), f32),
            pair_shape,
            pair_shape,
            down_shape,
            down_shape,
        ),
        [VM] * 3 + [VM] * 4,
        [
            pltpu.VMEM((2, shards * part, hidden_width), low),
            pltpu.VMEM((hidden_width, width), low),
            pltpu.VMEM((rows, hidden_width), low),
            pltpu.VMEM((rows, hidden_width), low),
            pltpu.VMEM((rows, hidden_width), low),
            pltpu.VMEM((2, shards * part, hidden_width), low),
            pltpu.VMEM((hidden_width, width), low),
        ],
        19,
        38,
    )
    pair_sent = flip(pair_send, 0, replicas)
    down_sent = flip(down_send, 0, replicas)
    grad_turned, grad_values, grad_out = [], [], []
    for kv in range(KV):
        if kv == 1:
            pair_left = halve(pair_keep, after(pair_sent, grad_turned[0]), 1, replicas)
            down_left = halve(down_keep, after(down_sent, grad_turned[0]), 2, replicas)
            grad_one = after(grad_one, pair_sent, down_sent)
        one, two, three = call(
            functools.partial(back_heads_kernel, kv),
            f"back_{kv}",
            (bias, cosine, sine, weights, query, keys, values, mixed[kv], log_total[kv], grad_one),
            [VM] * 10,
            (
                shape((rows, RATIO * HD + HD), low),
                shape((rows, HD), low),
                shape((RATIO * HD, width), low),
            ),
            [VM] * 3,
            [pltpu.VMEM((rows, RATIO * HD), low), pltpu.VMEM((rows, RATIO * HD + HD), f32)],
            5,
            24,
        )
        grad_turned.append(one)
        grad_values.append(two)
        grad_out.append(three)
    attn_shape = shape((2, 2, shards, 80, 384), low)
    grad_tokens, attn_keep, attn_send = call(
        functools.partial(back_last_kernel, shards, part),
        "back_last",
        (
            hidden_in,
            gains,
            weights,
            normed,
            grad_one,
            grad_gain_two,
            *grad_turned,
            *grad_values,
            *grad_out,
        ),
        [VM] * (6 + 3 * KV),
        (shape((width, rows), low), attn_shape, attn_shape),
        [VM, VM, VM],
        [
            pltpu.VMEM((rows, 1024), low),
            pltpu.VMEM((width + 16, packed), low),
        ],
        6,
        24,
    )
    attn_sent = flip(after(attn_send, down_left[1], pair_left[1]), 0, replicas)
    pair_left = halve(*pair_left, 2, replicas)
    attn_left = halve(attn_keep, after(attn_sent, pair_left[1]), 2, replicas)
    pair_total = scatter_over_shards(*pair_left, shards, replicas)
    down_left = halve(down_left[0], after(down_left[1], grad_tokens), 1, replicas)
    attn_left = halve(attn_left[0], after(attn_left[1], pair_total), 1, replicas)
    down_total = scatter_over_shards(*down_left, shards, replicas)
    feed_total = jnp.concatenate([pair_total, fold(down_total)])
    pair_half = gather_bit(feed_total, 2, replicas)
    attn_left = (attn_left[0], after(attn_left[1], pair_half))
    attn_total = scatter_over_shards(*attn_left, shards, replicas)
    pair_half = gather_bit(pair_half, 1, replicas)
    pair_pieces = spread(pair_half, (0,), replicas)
    attn_total = after(attn_total, pair_half)
    rest_pieces = spread(attn_total, (1, 2, 0), replicas)
    g_query, g_key, g_value, g_out, g_gain_one, g_gain_two, g_gate, g_up, g_down = call(
        finish_kernel,
        "finish",
        (*pair_pieces, *rest_pieces),
        [VM] * 4,
        (
            shape(w_query.shape, f32),
            shape(w_key.shape, f32),
            shape(w_value.shape, f32),
            shape(w_out.shape, f32),
            shape((1, part), f32),
            shape((1, part), f32),
            shape(w_gate.shape, f32),
            shape(w_up.shape, f32),
            shape((width, down_part), f32),
        ),
        [VM] * 9,
        [
            pltpu.VMEM((160, packed), low),
            pltpu.VMEM((2, part, hidden_width), low),
            pltpu.VMEM((8, 2 * eighth, 384), low),
        ],
        5,
        24,
    )
    return (
        result.T,
        grad_tokens.T,
        g_gain_one.reshape(part),
        g_query,
        g_key,
        g_value,
        g_out,
        g_gain_two.reshape(part),
        g_gate,
        g_up,
        g_down.T,
    )


def solution(mesh):
    in_specs = (
        P(("rep", "shard"), None),
        P(("rep", "shard"), None),
        P("shard"),
        P("shard", None),
        P("shard", None),
        P("shard", None),
        P("shard", None),
        P("shard"),
        P("shard", None),
        P("shard", None),
        P("shard", None),
        P(("rep", "shard"), None),
    )
    out_specs = (
        P(("rep", "shard"), None),
        P(("rep", "shard"), None),
        P("shard"),
        P("shard", None),
        P("shard", None),
        P("shard", None),
        P("shard", None),
        P("shard"),
        P("shard", None),
        P("shard", None),
        P("shard", None),
    )
    part = functools.partial(local, mesh.shape["rep"], mesh.shape["shard"])
    return jax.shard_map(part, mesh=mesh, in_specs=in_specs, out_specs=out_specs, check_vma=False)
```
